32 devices in a mesh: dp: 8 (over z, x), pipe: 4 (over y, core).
Axes of the slice: x: 2, y: 2, z: 4, core: 2. Of those that a mesh axis runs over, the one named last changes fastest.
Arguments:
- images: bfloat16 [64, 14, 14, 320], P('dp'), may hold values from -18 to 18
- image_counts: int32 [8], P('dp'), may hold values from 4 to 8, as said below
- conv_kernel: bfloat16 [4, 3, 3, 320], P('pipe'), may hold values from -2 to 2
- bn_gain: float32 [4, 320], P('pipe'), may hold values from 0.1 to 1.9
- bn_bias: float32 [4, 320], P('pipe'), may hold values from -3 to 3
- mix_h: bfloat16 [4, 14, 14], P('pipe'), may hold values from -1.5 to 1.5
- mix_h_bias: float32 [4, 14], P('pipe'), may hold values from -3 to 3
- mix_w: bfloat16 [4, 14, 14], P('pipe'), may hold values from -1.5 to 1.5
- mix_w_bias: float32 [4, 14], P('pipe'), may hold values from -3 to 3
- unite_w: bfloat16 [4, 960, 320], P('pipe'), may hold values from -0.1875 to 0.1875
- unite_b: float32 [4, 320], P('pipe'), may hold values from -2 to 2
- ln_gain: float32 [4, 320], P('pipe'), may hold values from 0.1 to 1.9
- ln_bias: float32 [4, 320], P('pipe'), may hold values from -2 to 2
- w_in: bfloat16 [4, 320, 1280], P('pipe'), may hold values from -0.3125 to 0.3125
- b_in: float32 [4, 1280], P('pipe'), may hold values from -3 to 3
- w_out: bfloat16 [4, 1280, 320], P('pipe'), may hold values from -0.15625 to 0.15625
- b_out: float32 [4, 320], P('pipe'), may hold values from -2 to 2
- running_mean: float32 [4, 320], P('pipe'), may hold values from -4 to 4
- running_var: float32 [4, 320], P('pipe'), may hold values from 0.5 to 2
- cotangent: bfloat16 [64, 14, 14, 320], P('dp'), may hold values from -18 to 18
Outputs:
- layer_outputs: bfloat16 [4, 64, 14, 14, 320], P('pipe', 'dp')
- input_grads: bfloat16 [4, 64, 14, 14, 320], P('pipe', 'dp')
- grad_conv_kernel: float32 [4, 3, 3, 320], P('pipe')
- grad_bn_gain: float32 [4, 320], P('pipe')
- grad_bn_bias: float32 [4, 320], P('pipe')
- grad_mix_h: float32 [4, 14, 14], P('pipe')
- grad_mix_h_bias: float32 [4, 14], P('pipe')
- grad_mix_w: float32 [4, 14, 14], P('pipe')
- grad_mix_w_bias: float32 [4, 14], P('pipe')
- grad_unite_w: float32 [4, 960, 320], P('pipe')
- grad_unite_b: float32 [4, 320], P('pipe')
- grad_ln_gain: float32 [4, 320], P('pipe')
- grad_ln_bias: float32 [4, 320], P('pipe')
- grad_w_in: float32 [4, 320, 1280], P('pipe')
- grad_b_in: float32 [4, 1280], P('pipe')
- grad_w_out: float32 [4, 1280, 320], P('pipe')
- grad_b_out: float32 [4, 320], P('pipe')
- new_running_mean: float32 [4, 320], P('pipe')
- new_running_var: float32 [4, 320], P('pipe')
The draws below stay inside these ranges and needn't reach their ends.
Inputs may be any that keep to these rules, and one draw needn't show every extreme that they name: `image_counts`: some index of dp has all 8 images valid in every draw.
All inputs are finite; a program needn't handle non-finite values.
Results may differ from the reference program's by a relative error of at most 0.014.
Values may be sent and summed in bfloat16 or wider, within the bound.
No kernel may reach another device: no remote copies, remote signals or barrier semaphores. Data moves between devices by JAX's collectives and lax.ppermute only.
A program may use at most 192 MiB of HBM per device.

```python
import math
import jax
import jax.numpy as jnp
from jax import lax

CH = 320
HID = 1280
SIDE = 14
MICRO = 4
IMG_MB = 2
IMG_DEV = 8
IMGS = 64
LAYERS = 4
N_DP = 8


def rising_rows():
    group = jnp.arange(IMGS) // IMG_DEV
    return 1.0 + 2.0 * group.astype(jnp.float32) / max(N_DP - 1, 1)


def draw_images(key, part):
    key = jax.random.fold_in(key, 5)
    values = jax.random.normal(key, (IMGS, SIDE, SIDE, CH), jnp.float32)
    return (jnp.clip(values, -6.0, 6.0) * rising_rows()[:, None, None, None]).astype(jnp.bfloat16)


def draw_cotangent(key, part):
    key = jax.random.fold_in(key, 7)
    values = jax.random.normal(key, (IMGS, SIDE, SIDE, CH), jnp.float32)
    return (jnp.clip(values, -6.0, 6.0) * rising_rows()[:, None, None, None]).astype(jnp.bfloat16)


def draw_image_counts(key, part):
    key = jax.random.fold_in(key, 11)
    first, second = jax.random.split(key)
    counts = jax.random.randint(first, (N_DP,), IMG_DEV // 2, IMG_DEV + 1)
    chosen = jax.random.randint(second, (), 0, N_DP)
    return jnp.where(jnp.arange(N_DP) == chosen, IMG_DEV, counts).astype(jnp.int32)


def steps_of(key, extent, cuts, least, top_value):
    level, own = 1.0, jax.random.fold_in(key, 6)
    for dim, blocks in cuts:
        heights = jnp.exp(jax.random.uniform(jax.random.fold_in(own, dim), (blocks,), jnp.float32, least / len(cuts), top_value / len(cuts)))
        level = level * jnp.repeat(heights, extent[dim] // blocks).reshape([-1 if axis == dim else 1 for axis in range(len(extent))])
    return level


def bell_draw(key, extent, width, limit, pieces=(), kind=jnp.bfloat16):
    array = jax.random.normal(key, extent, jnp.float32) * width
    if len(pieces) > 0:
        array = steps_of(key, extent, pieces, -0.22, 0.18) * array
    return jnp.clip(array, min=-limit, max=limit).astype(kind)


def setup_inputs(seed: int = 0) -> dict:
    keys = jax.random.split(jax.random.key(seed), 21)
    images = draw_images(jax.random.fold_in(keys[20], 71), 0)
    image_counts = draw_image_counts(jax.random.fold_in(keys[20], 71), 0)
    conv_kernel = bell_draw(keys[2], (LAYERS, 3, 3, CH), 9 ** -0.5, 2.0, ((0, 4),))
    bn_gain = jnp.clip(1.0 + 0.18 * jax.random.normal(keys[3], (LAYERS, CH), jnp.float32), 0.1, 1.9)
    bn_bias = bell_draw(keys[4], (LAYERS, CH), 0.5, 3.0, ((0, 4),), jnp.float32)
    mix_h = bell_draw(keys[5], (LAYERS, SIDE, SIDE), SIDE ** -0.5, 1.5, ((0, 4),))
    mix_h_bias = bell_draw(keys[6], (LAYERS, SIDE), 0.5, 3.0, ((0, 4),), jnp.float32)
    mix_w = bell_draw(keys[7], (LAYERS, SIDE, SIDE), SIDE ** -0.5, 1.5, ((0, 4),))
    mix_w_bias = bell_draw(keys[8], (LAYERS, SIDE), 0.5, 3.0, ((0, 4),), jnp.float32)
    unite_w = bell_draw(keys[9], (LAYERS, 3 * CH, CH), (3 * CH) ** -0.5, 0.1875, ((0, 4),))
    unite_b = bell_draw(keys[10], (LAYERS, CH), 0.3, 2.0, ((0, 4),), jnp.float32)
    ln_gain = jnp.clip(1.0 + 0.18 * jax.random.normal(keys[11], (LAYERS, CH), jnp.float32), 0.1, 1.9)
    ln_bias = bell_draw(keys[12], (LAYERS, CH), 0.3, 2.0, ((0, 4),), jnp.float32)
    w_in = bell_draw(keys[13], (LAYERS, CH, HID), CH ** -0.5, 0.3125, ((0, 4),))
    b_in = bell_draw(keys[14], (LAYERS, HID), 0.5, 3.0, ((0, 4),), jnp.float32)
    w_out = bell_draw(keys[15], (LAYERS, HID, CH), HID ** -0.5, 0.15625, ((0, 4),))
    b_out = bell_draw(keys[16], (LAYERS, CH), 0.3, 2.0, ((0, 4),), jnp.float32)
    running_mean = bell_draw(keys[17], (LAYERS, CH), 1.0, 4.0, ((0, 4),), jnp.float32)
    running_var = jnp.clip(jnp.exp(math.log(2.0) - 1.3862944 * jax.random.uniform(keys[18], (LAYERS, CH), jnp.float32) ** steps_of(keys[18], (LAYERS, CH), ((0, 4),), -0.2, 0.2)), 0.5, 2.0)
    cotangent = draw_cotangent(jax.random.fold_in(keys[20], 71), 0)
    return {"images": images, "image_counts": image_counts, "conv_kernel": conv_kernel, "bn_gain": bn_gain, "bn_bias": bn_bias, "mix_h": mix_h, "mix_h_bias": mix_h_bias, "mix_w": mix_w, "mix_w_bias": mix_w_bias, "unite_w": unite_w, "unite_b": unite_b, "ln_gain": ln_gain, "ln_bias": ln_bias, "w_in": w_in, "b_in": b_in, "w_out": w_out, "b_out": b_out, "running_mean": running_mean, "running_var": running_var, "cotangent": cotangent}


@jax.custom_vjp
def low(v):
    return lax.optimization_barrier(v.astype(jnp.bfloat16)).astype(jnp.float32)

@jax.custom_vjp
def low_back(v):
    return v

def low_keep(v):
    return (low(v), None)

def low_pass(kept, grad):
    return (grad,)

def back_keep(v):
    return (v, None)

def back_low(kept, grad):
    return (low(grad),)
low.defvjp(low_keep, low_pass)
low_back.defvjp(back_keep, back_low)

def depthwise(field, kernel):
    side = field.shape[1]
    padded = jnp.pad(field, ((0, 0), (1, 1), (1, 1), (0, 0)))
    total = jnp.zeros(field.shape, field.dtype)
    for row_shift in range(3):
        for col_shift in range(3):
            total = total + kernel[row_shift, col_shift] * padded[:, row_shift:row_shift + side, col_shift:col_shift + side]
    return total

def layer_apply(field, mask, weights):
    kernel, bn_gain, bn_bias, mix_h, mix_h_bias, mix_w, mix_w_bias, unite_w, unite_b, ln_gain, ln_bias, w_in, b_in, w_out, b_out = weights
    side = field.shape[1]
    highest = lax.Precision.HIGHEST
    conv = depthwise(field, kernel)
    weight = mask[:, None, None, None]
    count = jnp.sum(mask) * (side * side)
    center = lax.optimization_barrier(jnp.sum(weight * conv, axis=(0, 1, 2))) / count
    square = lax.optimization_barrier(jnp.sum(weight * conv * conv, axis=(0, 1, 2))) / count
    variance = square - center * center
    unit_conv = (conv - center) * lax.rsqrt(variance + 1e-05)
    normed = low(unit_conv * bn_gain + bn_bias)
    rows_mixed = low(low_back(jnp.einsum('ik,bkjc->bijc', mix_h, normed, precision=highest) + mix_h_bias[None, :, None, None]))
    cols_mixed = low(low_back(jnp.einsum('jk,bikc->bijc', mix_w, normed, precision=highest) + mix_w_bias[None, None, :, None]))
    joined = jnp.concatenate([normed, rows_mixed, cols_mixed], axis=-1)
    hidden = field + low_back(jnp.einsum('bijc,cd->bijd', joined, unite_w, precision=highest) + unite_b)
    offset = hidden - lax.optimization_barrier(jnp.mean(hidden, axis=-1, keepdims=True))
    spread = lax.rsqrt(lax.optimization_barrier(jnp.mean(offset * offset, axis=-1, keepdims=True)) + 1e-06)
    lnormed = low(offset * spread * ln_gain + ln_bias)
    before = low_back(jnp.einsum('bijc,cf->bijf', lnormed, w_in, precision=highest) + b_in)
    active = low(jax.nn.gelu(before, approximate=True))
    branch = low_back(jnp.einsum('bijf,fc->bijc', active, w_out, precision=highest) + b_out)
    return (weight * (hidden + branch), (center, variance, count))

def reference(images, image_counts, conv_kernel, bn_gain, bn_bias, mix_h, mix_h_bias, mix_w, mix_w_bias, unite_w, unite_b, ln_gain, ln_bias, w_in, b_in, w_out, b_out, running_mean, running_var, cotangent):
    weights = tuple((item.astype(jnp.float32) for item in (conv_kernel, bn_gain, bn_bias, mix_h, mix_h_bias, mix_w, mix_w_bias, unite_w, unite_b, ln_gain, ln_bias, w_in, b_in, w_out, b_out)))
    side = images.shape[1]
    chans = images.shape[3]
    position = jnp.arange(IMG_DEV).astype(jnp.int32)
    masks = (position[None, :] < image_counts[:, None]).astype(jnp.float32).reshape(N_DP, MICRO, IMG_MB)
    pictures = images.astype(jnp.float32).reshape(N_DP, MICRO, IMG_MB, side, side, chans)
    upstream = cotangent.astype(jnp.float32).reshape(N_DP, MICRO, IMG_MB, side, side, chans)
    run_mean = running_mean
    run_var = running_var
    totals = None
    outputs = []
    in_grads = []
    for micro in range(MICRO):
        field_in = pictures[:, micro].reshape(N_DP * IMG_MB, side, side, chans)
        mask = masks[:, micro].reshape(N_DP * IMG_MB)
        extras = tuple((jnp.zeros_like(field_in) for depth in range(LAYERS)))

        def forward(params, added):
            field = field_in
            outs = []
            stats = []
            for depth in range(LAYERS):
                field = low_back(field + added[depth])
                result, stat = layer_apply(field, mask, tuple((item[depth] for item in params)))
                field = low(result)
                outs.append(field)
                stats.append(stat)
            return (jnp.stack(outs), stats)
        outs, pullback, stats = jax.vjp(forward, weights, extras, has_aux=True)
        start_grad = jnp.zeros_like(outs).at[LAYERS - 1].set(upstream[:, micro].reshape(N_DP * IMG_MB, side, side, chans))
        weight_grads, extra_grads = pullback(start_grad)
        totals = weight_grads if totals is None else jax.tree.map(lambda left, right: left + right, totals, weight_grads)
        outputs.append(outs.reshape(LAYERS, N_DP, IMG_MB, side, side, chans))
        in_grads.append(jnp.stack(extra_grads).reshape(LAYERS, N_DP, IMG_MB, side, side, chans))
        for depth in range(LAYERS):
            center, variance, count = stats[depth]
            run_mean = run_mean.at[depth].set(0.9 * run_mean[depth] + 0.1 * center)
            run_var = run_var.at[depth].set(0.9 * run_var[depth] + 0.1 * (variance * count / (count - 1.0)))
    layer_outputs = jnp.stack(outputs, axis=2).reshape(LAYERS, N_DP * IMG_DEV, side, side, chans).astype(jnp.bfloat16)
    input_grads = jnp.stack(in_grads, axis=2).reshape(LAYERS, N_DP * IMG_DEV, side, side, chans).astype(jnp.bfloat16)
    return (layer_outputs, input_grads, totals[0], totals[1], totals[2], totals[3], totals[4], totals[5], totals[6], totals[7], totals[8], totals[9], totals[10], totals[11], totals[12], totals[13], totals[14], run_mean, run_var)
```

```python
import functools

import jax
import jax.numpy as jnp
from jax import lax
from jax.experimental import pallas as pl
from jax.experimental.pallas import tpu as pltpu
from jax.sharding import PartitionSpec as P

F32 = jnp.float32
BF16 = jnp.bfloat16
LANES = 128
HID_STEP = 256
EXTRA = 128
ROW_BN_GAIN, ROW_BN_BIAS, ROW_UNITE_B, ROW_LN_GAIN, ROW_LN_BIAS, ROW_B_OUT = range(9, 15)
ROW_MIX_BIAS, ROW_B_IN, ROW_MIX = 15, 16, 24
SMALL_ROWS = 40
CLOSE_ROWS = 16
GRAD_ROWS = 64


def wide(value):
    return -(-value // LANES) * LANES


def tall(value):
    return -(-value // 16) * 16


def dot(left, right):
    return lax.dot_general(left, right, (((1,), (0,)), ((), ())), preferred_element_type=F32)


def dot_nt(left, right):
    return lax.dot_general(left, right, (((1,), (1,)), ((), ())), preferred_element_type=F32)


def dot_tn(left, right):
    return lax.dot_general(left, right, (((0,), (0,)), ((), ())), preferred_element_type=F32)


def dot_exact(left, right):
    return lax.dot_general(
        left,
        right,
        (((1,), (0,)), ((), ())),
        preferred_element_type=F32,
        precision=lax.Precision.HIGHEST,
    )


class Sizes:
    def __init__(self, batch, side, chans, hid, n_dp):
        self.batch, self.side, self.chans, self.hid, self.n_dp = batch, side, chans, hid, n_dp
        self.pad = tall(side)
        self.image = side * self.pad
        self.tokens = batch * self.image
        self.lanes = wide(chans)
        self.full = chans // LANES
        self.rest = chans - self.full * LANES
        self.hid_blocks = hid // LANES
        left_blocks = -(-3 * self.rest // LANES)
        self.unite_blocks = 3 * self.full + left_blocks
        self.blocks = 2 * self.hid_blocks + self.unite_blocks
        self.half_blocks = self.blocks // 2
        self.half_rows = self.half_blocks * chans + EXTRA

    def row(self, block):
        half, place = divmod(block, self.half_blocks)
        return half * self.half_rows + place * self.chans


def token_mask(sz, valid):
    row = lax.broadcasted_iota(jnp.int32, (sz.tokens, 1), 0)
    return ((row < valid * sz.image) & (row % sz.pad < sz.side)).astype(F32)


def by_image(sz, value, change):
    return jnp.concatenate(
        [change(value[n * sz.image : (n + 1) * sz.image]) for n in range(sz.batch)], axis=0
    )


def from_above(sz, value):
    zeros = jnp.zeros((sz.pad, value.shape[1]), value.dtype)
    return by_image(sz, value, lambda part: jnp.concatenate([zeros, part[: -sz.pad]], axis=0))


def from_below(sz, value):
    zeros = jnp.zeros((sz.pad, value.shape[1]), value.dtype)
    return by_image(sz, value, lambda part: jnp.concatenate([part[sz.pad :], zeros], axis=0))


def from_left(sz, value):
    return pltpu.roll(value, 1, 0)


def from_right(sz, value):
    return pltpu.roll(value, sz.tokens - 1, 0)


def depthwise(sz, field, taps):
    left, right = from_left(sz, field), from_right(sz, field)
    rows = [
        taps[3 * p] * left + taps[3 * p + 1] * field + taps[3 * p + 2] * right for p in range(3)
    ]
    return from_above(sz, rows[0]) + rows[1] + from_below(sz, rows[2])


def depthwise_back(sz, grad, taps):
    left, right = from_left(sz, grad), from_right(sz, grad)
    rows = [
        taps[3 * p] * right + taps[3 * p + 1] * grad + taps[3 * p + 2] * left for p in range(3)
    ]
    return from_below(sz, rows[0]) + rows[1] + from_above(sz, rows[2])


def taps_of(sz, small):
    return [small[k : k + 1, : sz.chans] for k in range(9)]


def row_of(sz, small, index):
    return small[index : index + 1, : sz.chans]


def fill_lanes(sz, row):
    if sz.lanes == sz.chans:
        return row
    return jnp.concatenate([row, jnp.zeros((1, sz.lanes - sz.chans), F32)], axis=1)


def lane_rows(sz, row):
    row = fill_lanes(sz, row)
    return [row[:, k * LANES : (k + 1) * LANES] for k in range(sz.lanes // LANES)]


def put_sums(sz, ref, first, second, number):
    pieces = lane_rows(sz, first) + lane_rows(sz, second)
    pieces.append(jnp.zeros((1, LANES), F32) + number)
    pieces.append(jnp.zeros((8 - len(pieces), LANES), F32))
    block = jnp.concatenate(pieces, axis=0)
    for index in range(sz.n_dp):
        ref[index] = block


def take_sums(sz, ref):
    total = ref[0]
    for index in range(1, sz.n_dp):
        total = total + ref[index]
    count = sz.lanes // LANES
    first = jnp.concatenate([total[k : k + 1] for k in range(count)], axis=1)
    second = jnp.concatenate([total[count + k : count + k + 1] for k in range(count)], axis=1)
    return first[:, : sz.chans], second[:, : sz.chans], total[2 * count : 2 * count + 1, 0:1]


def sum_rows(value):
    return jnp.sum(value, axis=0, keepdims=True)


def mean_lanes(value):
    return jnp.mean(value, axis=1, keepdims=True)


def pick_rows(sz):
    row = lax.broadcasted_iota(jnp.int32, (sz.image, sz.pad), 0)
    col = lax.broadcasted_iota(jnp.int32, (sz.image, sz.pad), 1)
    return (row // sz.pad == col), (row % sz.pad == col)


def same_masks(sz):
    row = lax.broadcasted_iota(jnp.int32, (sz.image, sz.image), 0)
    col = lax.broadcasted_iota(jnp.int32, (sz.image, sz.image), 1)
    return (row % sz.pad == col % sz.pad), (row // sz.pad == col // sz.pad)


def mixers(sz, small, turned):
    pick_i, pick_j = pick_rows(sz)
    same_j, same_i = same_masks(sz)
    product = dot_nt if turned else dot
    found = []
    for pick, same, lane in ((pick_i, same_j, 0), (pick_j, same_i, LANES)):
        mix = small[ROW_MIX : ROW_MIX + sz.pad, lane : lane + sz.pad].astype(BF16)
        pick = pick.astype(BF16)
        spread = dot_nt(product(pick, mix).astype(BF16), pick)
        found.append(jnp.where(same, spread, 0.0).astype(BF16))
    return found


def fetch(role, sources, targets, sems):
    count = len(targets)
    for place in range(len(sources) // count):

        @pl.when(role == place)
        def _(place=place):
            for k in range(count):
                pltpu.make_async_copy(
                    sources[place * count + k], targets[k], sems.at[k]
                ).start()


def fetched(sources, targets, sems, index):
    pltpu.make_async_copy(sources[index], targets[index], sems.at[index]).wait()


def start_kernel(sz, info, field_ref, small_ref, conv_ref, sums_ref):
    conv = depthwise(sz, field_ref[...].astype(F32), taps_of(sz, small_ref[0]))
    conv_ref[...] = conv
    masked = token_mask(sz, info[0]) * conv
    number = (info[0] * (sz.side * sz.side)).astype(F32)
    put_sums(sz, sums_ref, sum_rows(masked), sum_rows(masked * conv), number)


def forward_kernel(sz, depth, last, info, field_ref, conv_ref, got_ref, small_ref, *refs):
    sources, refs = refs[:12], refs[12:]
    (out_ref, active_ref, slope_ref, unit_ref, spread_ref, normed_ref, rows_ref, cols_ref, stat_ref), refs = (
        refs[:9],
        refs[9:],
    )
    if not last:
        (conv_next_ref, sums_ref), refs = refs[:2], refs[2:]
    targets, sems = refs[:3], refs[3]
    fetch(info[1] ^ depth, sources, targets, sems)
    unite_ref, in_ref, w_out_ref = targets
    small = small_ref[depth]
    total, square, count = take_sums(sz, got_ref)
    center = total / count
    variance = square / count - center * center
    inverse = lax.rsqrt(variance + 1e-05)
    stat_ref[...] = jnp.concatenate(
        [
            fill_lanes(sz, center),
            fill_lanes(sz, inverse),
            fill_lanes(sz, variance * count / (count - 1.0)),
            jnp.zeros((1, sz.lanes), F32) + count,
            jnp.zeros((4, sz.lanes), F32),
        ],
        axis=0,
    )
    scaled = (conv_ref[...] - center) * inverse
    normed = (
        scaled * row_of(sz, small, ROW_BN_GAIN) + row_of(sz, small, ROW_BN_BIAS)
    ).astype(BF16)
    normed_ref[...] = normed
    mix_h, mix_w = mixers(sz, small, False)
    pick_i, pick_j = pick_rows(sz)
    bias = small[ROW_MIX_BIAS : ROW_MIX_BIAS + 1]
    bias_h = jnp.sum(jnp.where(pick_i, bias[:, : sz.pad], 0.0), axis=1, keepdims=True)
    bias_w = jnp.sum(
        jnp.where(pick_j, bias[:, LANES : LANES + sz.pad], 0.0), axis=1, keepdims=True
    )
    rows_mixed = by_image(sz, normed, lambda part: (dot(mix_h, part) + bias_h).astype(BF16))
    cols_mixed = by_image(sz, normed, lambda part: (dot(mix_w, part) + bias_w).astype(BF16))
    rows_ref[...] = rows_mixed
    cols_ref[...] = cols_mixed
    fetched(sources, targets, sems, 0)
    hidden = field_ref[...].astype(F32) + (
        dot(normed, unite_ref[: sz.chans])
        + dot(rows_mixed, unite_ref[sz.chans : 2 * sz.chans])
        + dot(cols_mixed, unite_ref[2 * sz.chans :])
        + row_of(sz, small, ROW_UNITE_B)
    )
    offset = hidden - mean_lanes(hidden)
    spread = lax.rsqrt(mean_lanes(offset * offset) + 1e-06)
    unit = offset * spread
    unit_ref[...] = unit
    spread_ref[...] = spread
    lnormed = (
        unit * row_of(sz, small, ROW_LN_GAIN) + row_of(sz, small, ROW_LN_BIAS)
    ).astype(BF16)
    fetched(sources, targets, sems, 1)
    fetched(sources, targets, sems, 2)
    branch = jnp.zeros((sz.tokens, sz.chans), F32)
    lanes_in = [small[ROW_B_IN + k : ROW_B_IN + k + 1] for k in range(-(-sz.hid // sz.lanes))]
    b_in = jnp.concatenate(lanes_in, axis=1)
    root = 0.7978845608028654
    cubic = 0.044715
    for k in range(0, sz.hid, HID_STEP):
        before = dot(lnormed, in_ref[:, k : k + HID_STEP]) + b_in[:, k : k + HID_STEP]
        squared = before * before
        bent = jnp.tanh(before * (root + (root * cubic) * squared))
        half = 0.5 + 0.5 * bent
        active = (before * half).astype(BF16)
        slope = half + (before * (half * (1.0 - bent))) * (
            root + (3.0 * root * cubic) * squared
        )
        active_ref[:, k : k + HID_STEP] = active
        slope_ref[:, k : k + HID_STEP] = slope.astype(BF16)
        branch = branch + dot(active, w_out_ref[k : k + HID_STEP])
    mask = token_mask(sz, info[0])
    result = (mask * (hidden + (branch + row_of(sz, small, ROW_B_OUT)))).astype(BF16)
    out_ref[...] = result
    if not last:
        conv = depthwise(sz, result.astype(F32), taps_of(sz, small_ref[depth + 1]))
        conv_next_ref[...] = conv
        masked = mask * conv
        number = (info[0] * (sz.side * sz.side)).astype(F32)
        put_sums(sz, sums_ref, sum_rows(masked), sum_rows(masked * conv), number)


def finish_layer(sz, depth, info, refs, grad_ref, close_ref):
    got_ref, normed_grad_ref, hidden_grad_ref, conv_ref, stat_ref, field_ref, small_ref = refs
    small = small_ref[depth]
    taps = taps_of(sz, small)
    sum_dz, sum_dzx, _ = take_sums(sz, got_ref)
    count = stat_ref[3:4, 0:1]
    center = stat_ref[0:1, : sz.chans]
    inverse = stat_ref[1:2, : sz.chans]
    scaled = (conv_ref[...] - center) * inverse
    conv_grad = (token_mask(sz, info[0]) * (inverse * row_of(sz, small, ROW_BN_GAIN))) * (
        normed_grad_ref[...] - sum_dz / count - scaled * (sum_dzx / count)
    )
    grad = hidden_grad_ref[...] + depthwise_back(sz, conv_grad, taps)
    grad = grad.astype(BF16)
    grad_ref[...] = grad
    field = field_ref[...].astype(F32)
    across = [from_left(sz, field), field, from_right(sz, field)]
    along = [from_below(sz, conv_grad), conv_grad, from_above(sz, conv_grad)]
    rows = [sum_rows(along[p] * across[q]) for p in range(3) for q in range(3)]
    pieces = [center, stat_ref[2:3, : sz.chans], sum_dz, sum_dzx] + rows
    close_ref[...] = jnp.concatenate(
        [fill_lanes(sz, piece) for piece in pieces]
        + [jnp.zeros((CLOSE_ROWS - len(pieces), sz.lanes), F32)],
        axis=0,
    )
    return grad


def finish_kernel(sz, depth, info, *refs):
    finish_layer(sz, depth, info, refs[:7], refs[7], refs[8])


def backward_kernel(sz, depth, first, info, *refs):
    if first:
        upstream_ref, refs = refs[0], refs[1:]
    else:
        behind, refs = refs[:6], refs[6:]
    (small_ref, active_ref, slope_ref, unit_ref, spread_ref, normed_ref, rows_ref, cols_ref, conv_ref, stat_ref), refs = (
        refs[:10],
        refs[10:],
    )
    sources, refs = refs[:12], refs[12:]
    (pack_ref, normed_grad_ref, hidden_grad_ref, sums_ref), refs = refs[:4], refs[4:]
    if not first:
        (grad_ref, close_ref), refs = refs[:2], refs[2:]
    targets, sems = refs[:3], refs[3]
    fetch(info[1] ^ depth, sources, targets, sems)
    unite_ref, in_ref, w_out_ref = targets
    if first:
        upstream = upstream_ref[...]
    else:
        upstream = finish_layer(
            sz, depth + 1, info, tuple(behind) + (small_ref,), grad_ref, close_ref
        )
    small = small_ref[depth]
    chans, tokens = sz.chans, sz.tokens
    out_grad = token_mask(sz, info[0]) * upstream.astype(F32)
    branch_grad = out_grad.astype(BF16)
    unit = unit_ref[...]
    ln_gain = row_of(sz, small, ROW_LN_GAIN)
    lnormed = (unit * ln_gain + row_of(sz, small, ROW_LN_BIAS)).astype(BF16)
    fetched(sources, targets, sems, 0)
    fetched(sources, targets, sems, 1)
    fetched(sources, targets, sems, 2)
    norm_grad = jnp.zeros((tokens, chans), F32)
    in_pieces = []
    for k in range(0, sz.hid, HID_STEP):
        step = slice(k, k + HID_STEP)
        before_grad = dot_nt(branch_grad, w_out_ref[step]) * slope_ref[:, step].astype(F32)
        before_grad = before_grad.astype(BF16)
        norm_grad = norm_grad + dot_nt(before_grad, in_ref[:, step])
        grad_in = dot_tn(lnormed, before_grad).astype(BF16)
        grad_out = dot_tn(branch_grad, active_ref[:, step]).astype(BF16)
        for lane in range(0, HID_STEP, LANES):
            block = (k + lane) // LANES
            row = sz.row(block)
            pack_ref[row : row + chans] = grad_in[:, lane : lane + LANES]
            row = sz.row(sz.hid_blocks + block)
            pack_ref[row : row + chans] = grad_out[:, lane : lane + LANES]
        step_sum = sum_rows(before_grad.astype(F32))
        in_pieces += [step_sum[:, lane : lane + LANES] for lane in range(0, HID_STEP, LANES)]
    unit_grad = norm_grad * ln_gain
    hidden_grad = out_grad + spread_ref[...] * (
        unit_grad - mean_lanes(unit_grad) - unit * mean_lanes(unit_grad * unit)
    )
    hidden_grad_ref[...] = hidden_grad
    token_grad = hidden_grad.astype(BF16)
    normed, rows_mixed, cols_mixed = normed_ref[...], rows_ref[...], cols_ref[...]
    direct = dot_nt(token_grad, unite_ref[:chans])
    rows_grad = dot_nt(token_grad, unite_ref[chans : 2 * chans]).astype(BF16)
    cols_grad = dot_nt(token_grad, unite_ref[2 * chans :]).astype(BF16)
    block = 2 * sz.hid_blocks
    leftovers = []
    for joined in (normed, rows_mixed, cols_mixed):
        part = dot_tn(token_grad, joined).astype(BF16)
        for lane in range(0, sz.full * LANES, LANES):
            row = sz.row(block)
            pack_ref[row : row + chans] = part[:, lane : lane + LANES]
            block += 1
        if sz.rest:
            leftovers.append(part[:, sz.full * LANES :])
    if sz.rest:
        left = jnp.concatenate(leftovers, axis=1)
        fill = wide(left.shape[1]) - left.shape[1]
        if fill:
            left = jnp.concatenate([left, jnp.zeros((chans, fill), BF16)], axis=1)
        for lane in range(0, left.shape[1], LANES):
            row = sz.row(block)
            pack_ref[row : row + chans] = left[:, lane : lane + LANES]
            block += 1
    turned_h, turned_w = mixers(sz, small, True)
    back = jnp.concatenate(
        [
            dot(turned_h, rows_grad[n * sz.image : (n + 1) * sz.image])
            + dot(turned_w, cols_grad[n * sz.image : (n + 1) * sz.image])
            for n in range(sz.batch)
        ],
        axis=0,
    )
    normed_grad = direct + back
    normed_grad_ref[...] = normed_grad
    scaled = (conv_ref[...] - stat_ref[0:1, :chans]) * stat_ref[1:2, :chans]
    put_sums(
        sz,
        sums_ref,
        sum_rows(normed_grad),
        sum_rows(normed_grad * scaled),
        0.0,
    )
    pick_i, pick_j = pick_rows(sz)
    same_j, same_i = same_masks(sz)
    mix_pieces, bias_pieces = [], []
    for grads, pick, same in ((rows_grad, pick_i, same_j), (cols_grad, pick_j, same_i)):
        pairs = jnp.zeros((sz.image, sz.image), F32)
        sums = jnp.zeros((sz.image, 1), F32)
        for n in range(sz.batch):
            part = slice(n * sz.image, (n + 1) * sz.image)
            pairs = pairs + dot_nt(grads[part], normed[part])
            sums = sums + jnp.sum(grads[part].astype(F32), axis=1, keepdims=True)
        picked = pick.astype(F32)
        near = dot_exact(jnp.where(same, pairs, 0.0), picked)
        small_grad = lax.dot_general(
            picked,
            near,
            (((0,), (0,)), ((), ())),
            preferred_element_type=F32,
            precision=lax.Precision.HIGHEST,
        )
        gap = LANES - sz.pad
        mix_pieces.append(
            jnp.concatenate([small_grad, jnp.zeros((sz.pad, gap), F32)], axis=1)
        )
        bias_pieces.append(
            jnp.concatenate([sum_rows(picked * sums), jnp.zeros((1, gap), F32)], axis=1)
        )
    pieces = (
        lane_rows(sz, sum_rows(token_grad.astype(F32)))
        + lane_rows(sz, sum_rows(norm_grad * unit))
        + lane_rows(sz, sum_rows(norm_grad))
        + lane_rows(sz, sum_rows(branch_grad.astype(F32)))
        + in_pieces
        + bias_pieces
        + mix_pieces
    )
    used = sum(piece.shape[0] for piece in pieces)
    pieces.append(jnp.zeros((EXTRA - used, LANES), F32))
    place = sz.half_blocks * chans
    pack_ref[place : place + EXTRA] = jnp.concatenate(pieces, axis=0).astype(BF16)
    place += sz.half_rows
    pack_ref[place : place + EXTRA] = jnp.zeros((EXTRA, LANES), BF16)


def closing_kernel(sz, info, pack_ref, mine_ref, close_ref, mean_ref, var_ref, *outs):
    (
        taps_ref,
        gain_ref,
        bias_ref,
        mix_h_ref,
        mix_h_bias_ref,
        mix_w_ref,
        mix_w_bias_ref,
        unite_ref,
        unite_b_ref,
        ln_gain_ref,
        ln_bias_ref,
        in_ref,
        b_in_ref,
        w_out_ref,
        b_out_ref,
        new_mean_ref,
        new_var_ref,
    ) = outs
    chans = sz.chans
    mean, var = mean_ref[...], var_ref[...]
    dz = jnp.zeros((1, sz.lanes), F32)
    dzx = jnp.zeros((1, sz.lanes), F32)
    for m in range(close_ref.shape[0]):
        block = close_ref[m]
        mean = 0.9 * mean + 0.1 * block[0:1, :chans]
        var = 0.9 * var + 0.1 * block[1:2, :chans]
        dz = dz + block[2:3]
        dzx = dzx + block[3:4]
    new_mean_ref[...] = mean
    new_var_ref[...] = var
    bias_ref[...] = dz[:, :chans]
    gain_ref[...] = dzx[:, :chans]
    for block in range(sz.hid_blocks):
        row = sz.row(block)
        in_ref[:, block * LANES : (block + 1) * LANES] = pack_ref[row : row + chans].astype(F32)
        row = sz.row(sz.hid_blocks + block)
        w_out_ref[block * LANES : (block + 1) * LANES] = (
            pack_ref[row : row + chans].astype(F32).T
        )
    block = 2 * sz.hid_blocks
    for part in range(3):
        for k in range(sz.full):
            row = sz.row(block)
            place = part * chans + k * LANES
            unite_ref[place : place + LANES] = pack_ref[row : row + chans].astype(F32).T
            block += 1
    if sz.rest:
        turned = [
            pack_ref[sz.row(b) : sz.row(b) + chans].astype(F32).T
            for b in range(block, sz.blocks)
        ]
        turned = jnp.concatenate(turned, axis=0)
        for part in range(3):
            place = part * chans + sz.full * LANES
            unite_ref[place : place + sz.rest] = turned[part * sz.rest : (part + 1) * sz.rest]
    place = sz.half_blocks * chans
    small = pack_ref[place : place + EXTRA].astype(F32)
    count = sz.lanes // LANES

    def joined(first, number, size):
        row = jnp.concatenate([small[first + k : first + k + 1] for k in range(number)], axis=1)
        return row[:, :size]

    unite_b_ref[...] = joined(0, count, chans)
    ln_gain_ref[...] = joined(count, count, chans)
    ln_bias_ref[...] = joined(2 * count, count, chans)
    b_out_ref[...] = joined(3 * count, count, chans)
    first = 4 * count
    b_in_ref[...] = joined(first, sz.hid_blocks, sz.hid)
    first += sz.hid_blocks
    mix_h_bias_ref[...] = small[first : first + 1, : sz.side]
    mix_w_bias_ref[...] = small[first + 1 : first + 2, : sz.side]
    first += 2
    mix_h_ref[...] = small[first : first + sz.side, : sz.side]
    first += sz.pad
    mix_w_ref[...] = small[first : first + sz.side, : sz.side]
    mine = mine_ref[...].astype(F32)
    for p in range(3):
        for q in range(3):
            at = GRAD_ROWS + (3 * p + q) * count
            row = jnp.concatenate([mine[at + k : at + k + 1] for k in range(count)], axis=1)
            taps_ref[p, q : q + 1, :] = row[:, :chans]


def vmem():
    return pl.BlockSpec(memory_space=pltpu.VMEM)


def run(body, outs, flat, weights=(), scratch=(), flops=0, name=None):
    specs = [pl.BlockSpec(memory_space=pltpu.SMEM)] + [vmem() for _ in flat[1:]]
    specs += [pl.BlockSpec(memory_space=pl.ANY) for _ in weights]
    args = tuple(flat) + tuple(weights)
    moved = sum(item.size * item.dtype.itemsize for item in tuple(flat) + tuple(outs))
    return pl.pallas_call(
        body,
        out_shape=tuple(outs),
        in_specs=specs,
        out_specs=tuple(vmem() for _ in outs),
        scratch_shapes=list(scratch),
        compiler_params=pltpu.CompilerParams(vmem_limit_bytes=48 * 1024 * 1024),
        cost_estimate=pl.CostEstimate(flops=flops, bytes_accessed=moved, transcendentals=0),
        name=name,
    )(*args)


def swap(block, axis, size, bit):
    return lax.ppermute(block, axis, [(i, i ^ bit) for i in range(size)])


def halve(block, axis, size, index, bit):
    side = jnp.where((index & bit) != 0, 1, 0)
    parts = block.reshape((2, block.shape[0] // 2) + block.shape[1:])
    kept = lax.dynamic_index_in_dim(parts, side, 0, keepdims=False)
    sent = lax.dynamic_index_in_dim(parts, 1 - side, 0, keepdims=False)
    got = swap(sent, axis, size, bit)
    return (kept.astype(F32) + got.astype(F32)).astype(BF16)


def double(block, axis, size, index, bit):
    got = swap(block, axis, size, bit)
    upper = (index & bit) != 0
    return jnp.concatenate(
        [jnp.where(upper, got, block), jnp.where(upper, block, got)], axis=0
    )


def smalls_of(sz, conv_kernel, rows, b_in, mix_h_bias, mix_w_bias, mix_h, mix_w):
    lanes = sz.lanes

    def to_lanes(block):
        return jnp.pad(block, ((0, 0), (0, lanes - block.shape[1])))

    count = -(-sz.hid // lanes)
    inner = jnp.pad(b_in, (0, count * lanes - sz.hid)).reshape(count, lanes)
    gap = LANES - sz.side
    biases = jnp.concatenate([jnp.pad(mix_h_bias, (0, gap)), mix_w_bias])[None]
    mixes = jnp.concatenate([jnp.pad(mix_h, ((0, 0), (0, gap))), mix_w], axis=1).astype(F32)
    top = jnp.concatenate(
        [to_lanes(conv_kernel.reshape(9, sz.chans).astype(F32)), to_lanes(rows), to_lanes(biases), inner]
    )
    top = jnp.pad(top, ((0, ROW_MIX - top.shape[0]), (0, 0)))
    return jnp.concatenate(
        [top, jnp.pad(to_lanes(mixes), ((0, SMALL_ROWS - ROW_MIX - sz.side), (0, 0)))]
    )


def shards(
    images,
    image_counts,
    conv_kernel,
    bn_gain,
    bn_bias,
    mix_h,
    mix_h_bias,
    mix_w,
    mix_w_bias,
    unite_w,
    unite_b,
    ln_gain,
    ln_bias,
    w_in,
    b_in,
    w_out,
    b_out,
    running_mean,
    running_var,
    cotangent,
):
    n_dp, n_pipe = lax.axis_size("dp"), lax.axis_size("pipe")
    dp, pipe = lax.axis_index("dp"), lax.axis_index("pipe")
    layers = n_pipe
    batch = images.shape[0] // n_pipe
    side, chans, hid = images.shape[1], images.shape[3], w_in.shape[2]
    sz = Sizes(batch, side, chans, hid, n_dp)
    core, plane = pipe & 1, pipe >> 1
    tokens = sz.tokens

    own = (unite_w[0], w_in[0], w_out[0])
    small_own = smalls_of(
        sz,
        conv_kernel[0],
        jnp.stack([bn_gain[0], bn_bias[0], unite_b[0], ln_gain[0], ln_bias[0], b_out[0]]),
        b_in[0],
        mix_h_bias[0],
        mix_w_bias[0],
        mix_h[0],
        mix_w[0],
    )
    small = lax.all_to_all(
        jnp.broadcast_to(small_own[None], (n_pipe,) + small_own.shape), "pipe", 0, 0
    )
    beside = tuple(swap(item, "pipe", n_pipe, 1) for item in own)
    across = tuple(lax.ppermute(item, "pipe", [(0, 2), (2, 0)]) for item in own)
    across_beside = tuple(lax.ppermute(item, "pipe", [(0, 1), (2, 3)]) for item in across)
    held = lax.optimization_barrier(own + across)[: len(own)]
    across_odd = tuple(lax.ppermute(item, "pipe", [(1, 3), (3, 1)]) for item in held)
    across_odd_beside = tuple(
        lax.ppermute(item, "pipe", [(1, 0), (3, 2)]) for item in across_odd
    )
    even = own + beside + across + across_beside
    odd = own + beside + across_odd + across_odd_beside

    def weights_of(depth):
        return odd if depth & 1 else even

    scratch = [pltpu.VMEM(item.shape, item.dtype) for item in own]
    scratch.append(pltpu.SemaphoreType.DMA((len(own),)))

    def micro(array):
        block = lax.dynamic_slice_in_dim(array, pipe * batch, batch, 0)
        block = jnp.pad(block, ((0, 0), (0, 0), (0, sz.pad - side), (0, 0)))
        return block.reshape(tokens, chans)

    valid = jnp.clip(image_counts[0] - pipe * batch, 0, batch).astype(jnp.int32)
    info = jnp.stack([valid, pipe.astype(jnp.int32)])

    def shape(*dims, dtype=F32):
        return jax.ShapeDtypeStruct(dims, dtype)

    sums_shape = shape(n_dp, 8, LANES)
    plain = shape(tokens, chans)
    small_flops = 2 * tokens * (3 * chans * chans + 2 * chans * hid)

    field = micro(images)
    conv, sums = run(
        functools.partial(start_kernel, sz), (plain, sums_shape), (info, field, small), name="start"
    )
    fields, convs, saved, stats = [field], [conv], [], []
    for depth in range(layers):
        got = lax.all_to_all(sums, "dp", 0, 0)
        last = depth + 1 == layers
        outs = (
            shape(tokens, chans, dtype=BF16),
            shape(tokens, hid, dtype=BF16),
            shape(tokens, hid, dtype=BF16),
            plain,
            shape(tokens, 1),
            shape(tokens, chans, dtype=BF16),
            shape(tokens, chans, dtype=BF16),
            shape(tokens, chans, dtype=BF16),
            shape(8, sz.lanes),
        )
        if not last:
            outs += (plain, sums_shape)
        results = run(
            functools.partial(forward_kernel, sz, depth, last),
            outs,
            (info, fields[depth], convs[depth], got, small),
            weights_of(depth),
            scratch,
            small_flops,
            name=f"layer_{depth}_forward",
        )
        fields.append(results[0])
        saved.append(results[1:8])
        stats.append(results[8])
        if not last:
            convs.append(results[9])
            sums = results[10]

    def to_owner(own_parts):
        whole = jnp.zeros((n_pipe, batch, side, side, chans), BF16)
        for bit in range(n_pipe):
            part = lax.select_n(pipe ^ bit, *own_parts)
            if bit:
                part = swap(part, "pipe", n_pipe, bit)
            part = part.reshape(1, batch, side, sz.pad, chans)[:, :, :, :side]
            whole = lax.dynamic_update_slice(whole, part, (pipe ^ bit, 0, 0, 0, 0))
        return whole.reshape(1, n_pipe * batch, side, side, chans)

    layer_outputs = to_owner(fields[1:])

    pack_shape = shape(2 * sz.half_rows, LANES, dtype=BF16)
    halves = [None] * layers
    grads, closes = [None] * layers, [None] * layers
    behind = None
    for depth in reversed(range(layers)):
        outs = (pack_shape, plain, plain, sums_shape)
        if behind is None:
            front = (micro(cotangent),)
        else:
            front = behind
            outs += (shape(tokens, chans, dtype=BF16), shape(CLOSE_ROWS, sz.lanes))
        results = run(
            functools.partial(backward_kernel, sz, depth, behind is None),
            outs,
            (info,) + front + (small,) + saved[depth] + (convs[depth], stats[depth]),
            weights_of(depth),
            scratch,
            2 * small_flops,
            name=f"layer_{depth}_backward",
        )
        pack, normed_grad, hidden_grad, sums = results[:4]
        if behind is not None:
            grads[depth + 1], closes[depth + 1] = results[4:]
        half = halve(pack, "pipe", n_pipe, pipe, 1)
        if depth >> 1:
            moved = lax.ppermute(half, "pipe", [(0, 2), (1, 3)])
        else:
            moved = lax.ppermute(half, "pipe", [(2, 0), (3, 1)])
        halves[depth] = (half, moved)
        got = lax.all_to_all(sums, "dp", 0, 0)
        behind = (got, normed_grad, hidden_grad, convs[depth], stats[depth], fields[depth])
    grads[0], closes[0] = run(
        functools.partial(finish_kernel, sz, 0),
        (shape(tokens, chans, dtype=BF16), shape(CLOSE_ROWS, sz.lanes)),
        (info,) + behind + (small,),
        name="finish",
    )
    input_grads = to_owner(grads)
    closing = lax.all_to_all(jnp.stack(closes), "pipe", 0, 0)

    taps = jnp.sum(closing[:, 4:13], axis=0).reshape(9 * (sz.lanes // LANES), LANES)
    taps = jnp.pad(
        taps, ((sz.half_rows - EXTRA + GRAD_ROWS, EXTRA - GRAD_ROWS - taps.shape[0]), (0, 0))
    )

    def plane_layer(offset):
        pairs = [halves[offset], halves[offset + 2]]
        half = lax.select(plane == 0, pairs[0][0], pairs[1][0]).astype(F32)
        moved = lax.select(plane == 0, pairs[0][1], pairs[1][1]).astype(F32)
        mine = jnp.where(core == offset, taps, 0.0)
        return (half + moved + mine).astype(BF16)

    parts = [plane_layer(0), plane_layer(1)]
    bits = [1 << k for k in range(n_dp.bit_length() - 1)]
    orders = [bits, bits[1:] + bits[:1]]
    for step in range(len(bits)):
        parts = [
            halve(part, "dp", n_dp, dp, order[step]) for part, order in zip(parts, orders)
        ]
    for step in reversed(range(len(bits))):
        parts = [
            double(part, "dp", n_dp, dp, order[step]) for part, order in zip(parts, orders)
        ]
    mine = lax.select(core == 0, parts[0], parts[1])
    other = lax.select(core == 0, parts[1], parts[0])
    got = swap(other, "pipe", n_pipe, 1)
    pack = jnp.concatenate(
        [lax.select(core == 0, mine, got), lax.select(core == 0, got, mine)], axis=0
    )
    row = shape(1, chans)
    outs = (
        shape(3, 3, chans),
        row,
        row,
        shape(side, side),
        shape(1, side),
        shape(side, side),
        shape(1, side),
        shape(3 * chans, chans),
        row,
        row,
        row,
        shape(chans, hid),
        shape(1, hid),
        shape(hid, chans),
        row,
        row,
        row,
    )
    finished = run(
        functools.partial(closing_kernel, sz),
        outs,
        (info, pack, mine[-EXTRA:], closing, running_mean, running_var),
        name="closing",
    )
    shaped = [
        item if item.ndim == 2 and item.shape[0] == 1 else item[None] for item in finished
    ]
    return (layer_outputs, input_grads) + tuple(shaped)


def solution(mesh):
    four = P("pipe", None, None, None)
    three = P("pipe", None, None)
    two = P("pipe", None)
    images = P("dp", None, None, None)
    in_specs = (
        images, P("dp"), four, two, two, three, two, three, two, three, two, two, two,
        three, two, three, two, two, two, images,
    )
    stacked = P("pipe", "dp", None, None, None)
    out_specs = (
        stacked, stacked, four, two, two, three, two, three, two, three, two, two, two,
        three, two, three, two, two, two,
    )
    return jax.shard_map(
        shards, mesh=mesh, in_specs=in_specs, out_specs=out_specs, check_vma=False
    )
```

```python
import functools

import jax
import jax.numpy as jnp
from jax import lax
from jax.experimental import pallas as pl
from jax.experimental.pallas import tpu as pltpu
from jax.sharding import PartitionSpec as P

F32 = jnp.float32
BF16 = jnp.bfloat16
LANES = 128
HID_STEP = 256
VMEM_BYTES = 58 * 1024 * 1024
EXTRA = 128
ROW_BN_GAIN, ROW_BN_BIAS, ROW_UNITE_B, ROW_LN_GAIN, ROW_LN_BIAS, ROW_B_OUT = range(9, 15)
ROW_MIX_BIAS, ROW_B_IN, ROW_MIX = 15, 16, 24
SMALL_ROWS = 40
CLOSE_ROWS = 16
GRAD_ROWS = 64


def wide(value):
    return -(-value // LANES) * LANES


def tall(value):
    return -(-value // 16) * 16


def dot(left, right):
    return lax.dot_general(left, right, (((1,), (0,)), ((), ())), preferred_element_type=F32)


def dot_nt(left, right):
    return lax.dot_general(left, right, (((1,), (1,)), ((), ())), preferred_element_type=F32)


def dot_tn(left, right):
    return lax.dot_general(left, right, (((0,), (0,)), ((), ())), preferred_element_type=F32)


def dot_exact(left, right):
    return lax.dot_general(
        left,
        right,
        (((1,), (0,)), ((), ())),
        preferred_element_type=F32,
        precision=lax.Precision.HIGHEST,
    )


class Sizes:
    def __init__(self, batch, side, chans, hid, n_dp):
        self.batch, self.side, self.chans, self.hid, self.n_dp = batch, side, chans, hid, n_dp
        self.pad = tall(side)
        self.image = side * self.pad
        self.tokens = batch * self.image
        self.lanes = wide(chans)
        self.full = chans // LANES
        self.rest = chans - self.full * LANES
        self.hid_blocks = hid // LANES
        left_blocks = -(-3 * self.rest // LANES)
        self.unite_blocks = 3 * self.full + left_blocks
        self.blocks = 2 * self.hid_blocks + self.unite_blocks
        self.half_blocks = self.blocks // 2
        self.half_rows = self.half_blocks * chans + EXTRA
        self.weight_lanes = 2 * hid + 3 * self.lanes

    def place(self, block):
        half, place = divmod(block, self.half_blocks)
        return half, place * self.chans

    def unite(self, part):
        first = 2 * self.hid + part * self.lanes
        return slice(first, first + self.chans)


def token_mask(sz, valid):
    row = lax.broadcasted_iota(jnp.int32, (sz.tokens, 1), 0)
    return ((row < valid * sz.image) & (row % sz.pad < sz.side)).astype(F32)


def by_image(sz, value, change):
    return jnp.concatenate(
        [change(value[n * sz.image : (n + 1) * sz.image]) for n in range(sz.batch)], axis=0
    )


def from_above(sz, value):
    zeros = jnp.zeros((sz.pad, value.shape[1]), value.dtype)
    return by_image(sz, value, lambda part: jnp.concatenate([zeros, part[: -sz.pad]], axis=0))


def from_below(sz, value):
    zeros = jnp.zeros((sz.pad, value.shape[1]), value.dtype)
    return by_image(sz, value, lambda part: jnp.concatenate([part[sz.pad :], zeros], axis=0))


def from_left(sz, value):
    return pltpu.roll(value, 1, 0)


def from_right(sz, value):
    return pltpu.roll(value, sz.tokens - 1, 0)


def depthwise(sz, field, taps):
    left, right = from_left(sz, field), from_right(sz, field)
    rows = [
        taps[3 * p] * left + taps[3 * p + 1] * field + taps[3 * p + 2] * right for p in range(3)
    ]
    return from_above(sz, rows[0]) + rows[1] + from_below(sz, rows[2])


def depthwise_back(sz, grad, taps):
    left, right = from_left(sz, grad), from_right(sz, grad)
    rows = [
        taps[3 * p] * right + taps[3 * p + 1] * grad + taps[3 * p + 2] * left for p in range(3)
    ]
    return from_below(sz, rows[0]) + rows[1] + from_above(sz, rows[2])


def taps_of(sz, small):
    return [small[k : k + 1, : sz.chans] for k in range(9)]


def row_of(sz, small, index):
    return small[index : index + 1, : sz.chans]


def fill_lanes(sz, row):
    if sz.lanes == sz.chans:
        return row
    return jnp.concatenate([row, jnp.zeros((1, sz.lanes - sz.chans), F32)], axis=1)


def lane_rows(sz, row):
    row = fill_lanes(sz, row)
    return [row[:, k * LANES : (k + 1) * LANES] for k in range(sz.lanes // LANES)]


def put_sums(sz, ref, first, second, number):
    pieces = lane_rows(sz, first) + lane_rows(sz, second)
    pieces.append(jnp.zeros((1, LANES), F32) + number)
    pieces.append(jnp.zeros((8 - len(pieces), LANES), F32))
    block = jnp.concatenate(pieces, axis=0)
    for index in range(sz.n_dp):
        ref[index] = block


def take_sums(sz, ref):
    total = ref[0]
    for index in range(1, sz.n_dp):
        total = total + ref[index]
    count = sz.lanes // LANES
    first = jnp.concatenate([total[k : k + 1] for k in range(count)], axis=1)
    second = jnp.concatenate([total[count + k : count + k + 1] for k in range(count)], axis=1)
    return first[:, : sz.chans], second[:, : sz.chans], total[2 * count : 2 * count + 1, 0:1]


def sum_rows(value):
    return jnp.sum(value, axis=0, keepdims=True)


def mean_lanes(value):
    return jnp.mean(value, axis=1, keepdims=True)


def pick_rows(sz):
    row = lax.broadcasted_iota(jnp.int32, (sz.image, sz.pad), 0)
    col = lax.broadcasted_iota(jnp.int32, (sz.image, sz.pad), 1)
    return (row // sz.pad == col), (row % sz.pad == col)


def same_masks(sz):
    row = lax.broadcasted_iota(jnp.int32, (sz.image, sz.image), 0)
    col = lax.broadcasted_iota(jnp.int32, (sz.image, sz.image), 1)
    return (row % sz.pad == col % sz.pad), (row // sz.pad == col // sz.pad)


def mixers(sz, small, turned):
    pick_i, pick_j = pick_rows(sz)
    same_j, same_i = same_masks(sz)
    product = dot_nt if turned else dot
    found = []
    for pick, same, lane in ((pick_i, same_j, 0), (pick_j, same_i, LANES)):
        mix = small[ROW_MIX : ROW_MIX + sz.pad, lane : lane + sz.pad].astype(BF16)
        pick = pick.astype(BF16)
        spread = dot_nt(product(pick, mix).astype(BF16), pick)
        found.append(jnp.where(same, spread, 0.0).astype(BF16))
    return found


class Arrivals:
    def __init__(self, sources, buffers, sems, role_of, bit, layers):
        self.buffers, self.copies = buffers, []
        for k, (source, buffer) in enumerate(zip(sources, buffers)):
            if layers[k] is None:
                copies = [pltpu.make_async_copy(source, buffer, sems.at[k, 0])]
                copies[0].start()
            else:
                halved = isinstance(source[-1], tuple)
                rows = buffer.shape[0] // 2 if halved else buffer.shape[0]
                spots = [pl.ds(0, rows), pl.ds(rows, rows)] if halved else [pl.ds(0, rows)]
                copies = [
                    pltpu.make_async_copy(source[0].at[spot], buffer.at[spot], sems.at[k, h])
                    for h, spot in enumerate(spots)
                ]
                for place, held in enumerate(source):

                    @pl.when(role_of(layers[k]) == place)
                    def _(held=held, buffer=buffer, k=k, spots=spots, rows=rows):
                        for h, spot in enumerate(spots):
                            if isinstance(held, tuple):
                                piece = held[h]
                                at = h ^ bit
                                spot = pl.ds(pl.multiple_of(at * rows, 16), rows)
                            else:
                                piece = held.at[spot]
                            pltpu.make_async_copy(piece, buffer.at[spot], sems.at[k, h]).start()

            self.copies.append(copies)

    def __getitem__(self, k):
        if self.copies[k] is not None:
            for copy in self.copies[k]:
                copy.wait()
            self.copies[k] = None
        return self.buffers[k]

    def close(self):
        for k in range(len(self.copies)):
            self[k]


class Departures:
    def __init__(self, targets, buffers, sems, direct):
        self.buffers, self.targets = buffers, targets
        self.copies = [
            None if k < direct else pltpu.make_async_copy(buffer, target, sems.at[k])
            for k, (target, buffer) in enumerate(zip(targets, buffers))
        ]
        self.started = [False] * len(self.copies)

    def put(self, k, value):
        self.buffers[k][...] = value
        self.send(k)

    def send(self, k):
        self.copies[k].start()
        self.started[k] = True

    def close(self):
        for copy, started in zip(self.copies, self.started):
            if started:
                copy.wait()


def prepare_kernel(
    sz,
    info,
    taps_ref,
    bn_gain_ref,
    bn_bias_ref,
    mix_h_ref,
    mix_h_bias_ref,
    mix_w_ref,
    mix_w_bias_ref,
    unite_ref,
    unite_b_ref,
    ln_gain_ref,
    ln_bias_ref,
    in_ref,
    b_in_ref,
    w_out_ref,
    b_out_ref,
    weights_ref,
    half_ref,
    small_ref,
):
    chans, hid = sz.chans, sz.hid
    weights_ref[:, :hid] = in_ref[...]
    weights_ref[:, hid : 2 * hid] = w_out_ref[...]
    gap = jnp.zeros((chans, sz.lanes - chans), BF16)
    for part in range(3):
        first = 2 * hid + part * sz.lanes
        weights_ref[:, first : first + sz.lanes] = jnp.concatenate(
            [unite_ref[:, part * chans : (part + 1) * chans], gap], axis=1
        )
    rows = half_ref.shape[0]
    half_ref[...] = weights_ref[pl.ds(pl.multiple_of(info[2] * rows, 16), rows)]
    small_ref[...] = jnp.zeros(small_ref.shape, F32)
    for p in range(3):
        small_ref[3 * p : 3 * p + 3, :chans] = taps_ref[p].astype(F32)
    rows = (bn_gain_ref, bn_bias_ref, unite_b_ref, ln_gain_ref, ln_bias_ref, b_out_ref)
    for place, ref in zip(range(ROW_BN_GAIN, ROW_MIX_BIAS), rows):
        small_ref[place : place + 1, :chans] = ref[...]
    place = ROW_MIX_BIAS
    small_ref[place : place + 1, : sz.side] = mix_h_bias_ref[...]
    small_ref[place : place + 1, LANES : LANES + sz.side] = mix_w_bias_ref[...]
    for k, lane in enumerate(range(0, hid, sz.lanes)):
        wide_part = min(sz.lanes, hid - lane)
        small_ref[ROW_B_IN + k : ROW_B_IN + k + 1, :wide_part] = b_in_ref[
            :, lane : lane + wide_part
        ]
    rows = slice(ROW_MIX, ROW_MIX + sz.side)
    small_ref[rows, : sz.side] = mix_h_ref[...].astype(F32)
    small_ref[rows, LANES : LANES + sz.side] = mix_w_ref[...].astype(F32)


def start_kernel(sz, info, ins, outs):
    conv = depthwise(sz, ins[0][...].astype(F32), taps_of(sz, ins[1]))
    outs.put(0, conv)
    masked = token_mask(sz, info[0]) * conv
    number = (info[0] * (sz.side * sz.side)).astype(F32)
    put_sums(sz, outs.buffers[1], sum_rows(masked), sum_rows(masked * conv), number)
    outs.send(1)


def forward_kernel(sz, last, info, ins, outs):
    GOT, CONV, SMALL, WEIGHTS, FIELD = range(5)
    small = ins[SMALL]
    total, square, count = take_sums(sz, ins[GOT])
    center = total / count
    variance = square / count - center * center
    inverse = lax.rsqrt(variance + 1e-05)
    outs.put(8, jnp.concatenate(
        [
            fill_lanes(sz, center),
            fill_lanes(sz, inverse),
            fill_lanes(sz, variance * count / (count - 1.0)),
            jnp.zeros((1, sz.lanes), F32) + count,
            jnp.zeros((4, sz.lanes), F32),
        ],
        axis=0,
    ))
    scaled = (ins[CONV][...] - center) * inverse
    normed = (
        scaled * row_of(sz, small, ROW_BN_GAIN) + row_of(sz, small, ROW_BN_BIAS)
    ).astype(BF16)
    outs.put(5, normed)
    mix_h, mix_w = mixers(sz, small, False)
    pick_i, pick_j = pick_rows(sz)
    bias = small[ROW_MIX_BIAS : ROW_MIX_BIAS + 1]
    bias_h = jnp.sum(jnp.where(pick_i, bias[:, : sz.pad], 0.0), axis=1, keepdims=True)
    bias_w = jnp.sum(
        jnp.where(pick_j, bias[:, LANES : LANES + sz.pad], 0.0), axis=1, keepdims=True
    )
    rows_mixed = by_image(sz, normed, lambda part: (dot(mix_h, part) + bias_h).astype(BF16))
    cols_mixed = by_image(sz, normed, lambda part: (dot(mix_w, part) + bias_w).astype(BF16))
    outs.put(6, rows_mixed)
    outs.put(7, cols_mixed)
    weights_ref = ins[WEIGHTS]
    hidden = ins[FIELD][...].astype(F32) + (
        dot_nt(normed, weights_ref[:, sz.unite(0)])
        + dot_nt(rows_mixed, weights_ref[:, sz.unite(1)])
        + dot_nt(cols_mixed, weights_ref[:, sz.unite(2)])
        + row_of(sz, small, ROW_UNITE_B)
    )
    offset = hidden - mean_lanes(hidden)
    spread = lax.rsqrt(mean_lanes(offset * offset) + 1e-06)
    unit = offset * spread
    outs.put(3, unit)
    outs.put(4, spread)
    lnormed = (
        unit * row_of(sz, small, ROW_LN_GAIN) + row_of(sz, small, ROW_LN_BIAS)
    ).astype(BF16)
    branch = jnp.zeros((sz.tokens, sz.chans), F32)
    lanes_in = [small[ROW_B_IN + k : ROW_B_IN + k + 1] for k in range(-(-sz.hid // sz.lanes))]
    b_in = jnp.concatenate(lanes_in, axis=1)
    root = 0.7978845608028654
    cubic = 0.044715
    for k in range(0, sz.hid, HID_STEP):
        before = dot(lnormed, weights_ref[:, k : k + HID_STEP]) + b_in[:, k : k + HID_STEP]
        squared = before * before
        bent = jnp.tanh(before * (root + (root * cubic) * squared))
        half = 0.5 + 0.5 * bent
        active = (before * half).astype(BF16)
        slope = half + (before * (half * (1.0 - bent))) * (
            root + (3.0 * root * cubic) * squared
        )
        outs.buffers[1][:, k : k + HID_STEP] = active
        outs.buffers[2][:, k : k + HID_STEP] = slope.astype(BF16)
        branch = branch + dot_nt(
            active, weights_ref[:, sz.hid + k : sz.hid + k + HID_STEP]
        )
    outs.send(1)
    outs.send(2)
    mask = token_mask(sz, info[0])
    result = (mask * (hidden + (branch + row_of(sz, small, ROW_B_OUT)))).astype(BF16)
    outs.put(0, result)
    if not last:
        conv = depthwise(sz, result.astype(F32), taps_of(sz, ins[5]))
        outs.put(9, conv)
        masked = mask * conv
        number = (info[0] * (sz.side * sz.side)).astype(F32)
        put_sums(sz, outs.buffers[10], sum_rows(masked), sum_rows(masked * conv), number)
        outs.send(10)


def finish_layer(sz, info, ins, outs, first_out):
    GOT, STAT, SMALL, NORMED_GRAD, CONV, HIDDEN_GRAD, FIELD = range(7)
    small = ins[SMALL]
    stat = ins[STAT]
    taps = taps_of(sz, small)
    sum_dz, sum_dzx, _ = take_sums(sz, ins[GOT])
    count = stat[3:4, 0:1]
    center = stat[0:1, : sz.chans]
    inverse = stat[1:2, : sz.chans]
    scaled = (ins[CONV][...] - center) * inverse
    conv_grad = (token_mask(sz, info[0]) * (inverse * row_of(sz, small, ROW_BN_GAIN))) * (
        ins[NORMED_GRAD][...] - sum_dz / count - scaled * (sum_dzx / count)
    )
    grad = ins[HIDDEN_GRAD][...] + depthwise_back(sz, conv_grad, taps)
    grad = grad.astype(BF16)
    outs.put(first_out, grad)
    field = ins[FIELD][...].astype(F32)
    across = [from_left(sz, field), field, from_right(sz, field)]
    along = [from_below(sz, conv_grad), conv_grad, from_above(sz, conv_grad)]
    rows = [sum_rows(along[p] * across[q]) for p in range(3) for q in range(3)]
    pieces = [center, stat[2:3, : sz.chans], sum_dz, sum_dzx] + rows
    outs.put(first_out + 1, jnp.concatenate(
        [fill_lanes(sz, piece) for piece in pieces]
        + [jnp.zeros((CLOSE_ROWS - len(pieces), sz.lanes), F32)],
        axis=0,
    ))
    return grad


def finish_kernel(sz, info, ins, outs):
    finish_layer(sz, info, ins, outs, 0)


def backward_kernel(sz, first, info, ins, outs, pack_ref, pack_sems):
    base = 1 if first else 7
    SMALL, WEIGHTS, SLOPE, UNIT, SPREAD, ACTIVE, NORMED, ROWS, COLS, STAT, CONV = range(
        base, base + 11
    )
    core = info[1] & 1

    def put(block, value):
        half, row = sz.place(block)
        pack_ref[half ^ core, row : row + sz.chans] = value

    if first:
        upstream = ins[0][...]
    else:
        upstream = finish_layer(sz, info, ins, outs, 5)
    small = ins[SMALL]
    chans, tokens = sz.chans, sz.tokens
    out_grad = token_mask(sz, info[0]) * upstream.astype(F32)
    branch_grad = out_grad.astype(BF16)
    unit = ins[UNIT][...]
    ln_gain = row_of(sz, small, ROW_LN_GAIN)
    lnormed = (unit * ln_gain + row_of(sz, small, ROW_LN_BIAS)).astype(BF16)
    weights_ref, slope_ref, active_ref = ins[WEIGHTS], ins[SLOPE], ins[ACTIVE]
    norm_grad = jnp.zeros((tokens, chans), F32)
    in_pieces = []
    for k in range(0, sz.hid, HID_STEP):
        step = slice(k, k + HID_STEP)
        active_grad = dot(branch_grad, weights_ref[:, sz.hid + k : sz.hid + k + HID_STEP])
        before_grad = (active_grad * slope_ref[:, step].astype(F32)).astype(BF16)
        norm_grad = norm_grad + dot_nt(before_grad, weights_ref[:, step])
        grad_in = dot_tn(lnormed, before_grad).astype(BF16)
        grad_out = dot_tn(branch_grad, active_ref[:, step]).astype(BF16)
        for lane in range(0, HID_STEP, LANES):
            block = (k + lane) // LANES
            put(block, grad_in[:, lane : lane + LANES])
            put(sz.hid_blocks + block, grad_out[:, lane : lane + LANES])
        step_sum = sum_rows(before_grad.astype(F32))
        in_pieces += [step_sum[:, lane : lane + LANES] for lane in range(0, HID_STEP, LANES)]
    unit_grad = norm_grad * ln_gain
    hidden_grad = out_grad + ins[SPREAD][...] * (
        unit_grad - mean_lanes(unit_grad) - unit * mean_lanes(unit_grad * unit)
    )
    outs.put(3, hidden_grad)
    token_grad = hidden_grad.astype(BF16)
    normed, rows_mixed, cols_mixed = ins[NORMED][...], ins[ROWS][...], ins[COLS][...]
    direct = dot(token_grad, weights_ref[:, sz.unite(0)])
    rows_grad = dot(token_grad, weights_ref[:, sz.unite(1)]).astype(BF16)
    cols_grad = dot(token_grad, weights_ref[:, sz.unite(2)]).astype(BF16)
    block = 2 * sz.hid_blocks
    leftovers = []
    for joined in (normed, rows_mixed, cols_mixed):
        part = dot_tn(token_grad, joined).astype(BF16)
        for lane in range(0, sz.full * LANES, LANES):
            put(block, part[:, lane : lane + LANES])
            block += 1
        if sz.rest:
            leftovers.append(part[:, sz.full * LANES :])
    if sz.rest:
        left = jnp.concatenate(leftovers, axis=1)
        fill = wide(left.shape[1]) - left.shape[1]
        if fill:
            left = jnp.concatenate([left, jnp.zeros((chans, fill), BF16)], axis=1)
        for lane in range(0, left.shape[1], LANES):
            put(block, left[:, lane : lane + LANES])
            block += 1
    turned_h, turned_w = mixers(sz, small, True)
    back = jnp.concatenate(
        [
            dot(turned_h, rows_grad[n * sz.image : (n + 1) * sz.image])
            + dot(turned_w, cols_grad[n * sz.image : (n + 1) * sz.image])
            for n in range(sz.batch)
        ],
        axis=0,
    )
    normed_grad = direct + back
    outs.put(2, normed_grad)
    stat = ins[STAT]
    scaled = (ins[CONV][...] - stat[0:1, :chans]) * stat[1:2, :chans]
    put_sums(
        sz,
        outs.buffers[4],
        sum_rows(normed_grad),
        sum_rows(normed_grad * scaled),
        0.0,
    )
    outs.send(4)
    pick_i, pick_j = pick_rows(sz)
    same_j, same_i = same_masks(sz)
    mix_pieces, bias_pieces = [], []
    for grads, pick, same in ((rows_grad, pick_i, same_j), (cols_grad, pick_j, same_i)):
        pairs = jnp.zeros((sz.image, sz.image), F32)
        sums = jnp.zeros((sz.image, 1), F32)
        for n in range(sz.batch):
            part = slice(n * sz.image, (n + 1) * sz.image)
            pairs = pairs + dot_nt(grads[part], normed[part])
            sums = sums + jnp.sum(grads[part].astype(F32), axis=1, keepdims=True)
        picked = pick.astype(F32)
        near = dot_exact(jnp.where(same, pairs, 0.0), picked)
        small_grad = lax.dot_general(
            picked,
            near,
            (((0,), (0,)), ((), ())),
            preferred_element_type=F32,
            precision=lax.Precision.HIGHEST,
        )
        gap = LANES - sz.pad
        mix_pieces.append(
            jnp.concatenate([small_grad, jnp.zeros((sz.pad, gap), F32)], axis=1)
        )
        bias_pieces.append(
            jnp.concatenate([sum_rows(picked * sums), jnp.zeros((1, gap), F32)], axis=1)
        )
    pieces = (
        lane_rows(sz, sum_rows(token_grad.astype(F32)))
        + lane_rows(sz, sum_rows(norm_grad * unit))
        + lane_rows(sz, sum_rows(norm_grad))
        + lane_rows(sz, sum_rows(branch_grad.astype(F32)))
        + in_pieces
        + bias_pieces
        + mix_pieces
    )
    used = sum(piece.shape[0] for piece in pieces)
    pieces.append(jnp.zeros((EXTRA - used, LANES), F32))
    place = sz.half_blocks * chans
    pack_ref[core, place : place + EXTRA] = jnp.concatenate(pieces, axis=0).astype(BF16)
    pack_ref[1 - core, place : place + EXTRA] = jnp.zeros((EXTRA, LANES), BF16)
    copies = [
        pltpu.make_async_copy(pack_ref.at[slot], outs.targets[slot], pack_sems.at[slot])
        for slot in range(2)
    ]
    for copy in copies:
        copy.start()
    for copy in copies:
        copy.wait()


def closing_kernel(sz, info, mine_ref, got_ref, close_ref, taps_got_ref, mean_ref, var_ref, *outs):
    (
        taps_ref,
        gain_ref,
        bias_ref,
        mix_h_ref,
        mix_h_bias_ref,
        mix_w_ref,
        mix_w_bias_ref,
        unite_ref,
        unite_b_ref,
        ln_gain_ref,
        ln_bias_ref,
        in_ref,
        b_in_ref,
        w_out_ref,
        b_out_ref,
        new_mean_ref,
        new_var_ref,
    ) = outs
    chans = sz.chans
    first_half = (info[1] & 1) == 0

    def take(half, row, rows):
        mine, got = mine_ref[row : row + rows], got_ref[row : row + rows]
        chosen = jnp.where(first_half, mine, got) if half == 0 else jnp.where(first_half, got, mine)
        return chosen.astype(F32)

    mean, var = mean_ref[...], var_ref[...]
    dz = jnp.zeros((1, sz.lanes), F32)
    dzx = jnp.zeros((1, sz.lanes), F32)
    for m in range(close_ref.shape[0]):
        block = close_ref[m]
        mean = 0.9 * mean + 0.1 * block[0:1, :chans]
        var = 0.9 * var + 0.1 * block[1:2, :chans]
        dz = dz + block[2:3]
        dzx = dzx + block[3:4]
    new_mean_ref[...] = mean
    new_var_ref[...] = var
    bias_ref[...] = dz[:, :chans]
    gain_ref[...] = dzx[:, :chans]
    for block in range(sz.hid_blocks):
        lanes = slice(block * LANES, (block + 1) * LANES)
        in_ref[:, lanes] = take(*sz.place(block), chans)
        w_out_ref[:, lanes] = take(*sz.place(sz.hid_blocks + block), chans)
    block = 2 * sz.hid_blocks
    parts = [[] for _ in range(3)]
    for part in range(3):
        for k in range(sz.full):
            parts[part].append(take(*sz.place(block), chans))
            block += 1
    if sz.rest:
        left = jnp.concatenate(
            [take(*sz.place(b), chans) for b in range(block, sz.blocks)], axis=1
        )
        for part in range(3):
            parts[part].append(left[:, part * sz.rest : (part + 1) * sz.rest])
    unite_ref[...] = jnp.concatenate([piece for part in parts for piece in part], axis=1)
    small = take(0, sz.half_blocks * chans, EXTRA)
    count = sz.lanes // LANES

    def joined(first, number, size):
        row = jnp.concatenate([small[first + k : first + k + 1] for k in range(number)], axis=1)
        return row[:, :size]

    unite_b_ref[...] = joined(0, count, chans)
    ln_gain_ref[...] = joined(count, count, chans)
    ln_bias_ref[...] = joined(2 * count, count, chans)
    b_out_ref[...] = joined(3 * count, count, chans)
    first = 4 * count
    b_in_ref[...] = joined(first, sz.hid_blocks, sz.hid)
    first += sz.hid_blocks
    mix_h_bias_ref[...] = small[first : first + 1, : sz.side]
    mix_w_bias_ref[...] = small[first + 1 : first + 2, : sz.side]
    first += 2
    for ref in (mix_h_ref, mix_w_ref):
        for i in range(sz.side):
            ref[i] = small[first + i : first + i + 1, : sz.side]
        first += sz.pad
    taps = taps_got_ref[0]
    for index in range(1, sz.n_dp):
        taps = taps + taps_got_ref[index]
    for p in range(3):
        for q in range(3):
            taps_ref[p, q] = taps[3 * p + q : 3 * p + q + 1, :chans]


def settings(cost):
    return {
        "compiler_params": pltpu.CompilerParams(vmem_limit_bytes=VMEM_BYTES),
        "cost_estimate": pl.CostEstimate(
            flops=0, bytes_accessed=int(cost * 3.0e6), transcendentals=0
        ),
    }


def run_whole(body, outs, info, flat, name, cost):
    def whole(item):
        return pl.BlockSpec(item.shape, lambda step, rank=len(item.shape): (0,) * rank)

    return pl.pallas_call(
        body,
        grid=(1,),
        out_shape=tuple(outs),
        in_specs=[pl.BlockSpec(memory_space=pltpu.SMEM)] + [whole(item) for item in flat],
        out_specs=tuple(whole(item) for item in outs),
        name=name,
        **settings(cost),
    )(info, *flat)


def run(body, outs, info, flat, name, cost, scratch=(), direct=0):
    layers = [item[0] if isinstance(item, tuple) else None for item in flat]
    args, spots, buffers = [], [], []

    def add(item):
        args.append(item)
        return len(args) - 1

    for item in flat:
        held = item[1] if isinstance(item, tuple) else (item,)
        spots.append(
            [tuple(add(one) for one in part) if isinstance(part, tuple) else add(part) for part in held]
        )
        buffers.append(pltpu.VMEM(held[0].shape, held[0].dtype))
    out_buffers = [pltpu.VMEM(item.shape, item.dtype) for item in outs[direct:]]

    def kernel(info_ref, *refs):
        sources, refs = refs[: len(args)], refs[len(args) :]
        targets, refs = refs[: len(outs)], refs[len(outs) :]
        ins_held, refs = refs[: len(buffers)], refs[len(buffers) :]
        outs_held, refs = refs[: len(out_buffers)], refs[len(out_buffers) :]
        in_sems, out_sems = refs[:2]
        picked = []
        for layer, spot in zip(layers, spots):
            found = [
                tuple(sources[one] for one in part) if isinstance(part, tuple) else sources[part]
                for part in spot
            ]
            picked.append(found[0] if layer is None else found)
        ins = Arrivals(
            picked, ins_held, in_sems, lambda layer: info_ref[1] ^ layer, info_ref[2], layers
        )
        held = (None,) * direct + tuple(outs_held)
        departures = Departures(targets, held, out_sems, direct)
        body(info_ref, ins, departures, *refs[2:])
        ins.close()
        departures.close()

    return pl.pallas_call(
        kernel,
        out_shape=tuple(outs),
        in_specs=[pl.BlockSpec(memory_space=pltpu.SMEM)]
        + [pl.BlockSpec(memory_space=pl.ANY) for _ in args],
        out_specs=tuple(pl.BlockSpec(memory_space=pl.ANY) for _ in outs),
        scratch_shapes=buffers
        + out_buffers
        + [pltpu.SemaphoreType.DMA((len(flat), 2)), pltpu.SemaphoreType.DMA((len(outs),))]
        + list(scratch),
        name=name,
        **settings(cost),
    )(info, *args)


def swap(block, axis, size, bit):
    return lax.ppermute(block, axis, [(i, i ^ bit) for i in range(size)])


def tie(first, second):
    first = tuple(first)
    return lax.optimization_barrier(first + tuple(second))[: len(first)]


def add_low(left, right):
    return (left.astype(F32) + right.astype(F32)).astype(BF16)


class Ring:
    def __init__(self, n_dp, n_pipe, dp, core):
        bits = [1 << k for k in range(n_dp.bit_length() - 1)]
        self.orders = (bits, bits[1:] + bits[:1])
        self.steps = len(bits)
        self.n_dp, self.n_pipe, self.dp, self.core = n_dp, n_pipe, dp, core

    def swap(self, block, step):
        route = []
        for d in range(self.n_dp):
            for p in range(self.n_pipe):
                there = d ^ self.orders[p & 1][step]
                route.append((d * self.n_pipe + p, there * self.n_pipe + p))
        return lax.ppermute(block, ("dp", "pipe"), route)

    def upper(self, step):
        bit = jnp.where(self.core == 0, self.orders[0][step], self.orders[1][step])
        return (self.dp & bit) != 0

    def halve(self, block, step):
        side = jnp.where(self.upper(step), 1, 0)
        parts = block.reshape((2, block.shape[0] // 2) + block.shape[1:])
        kept = lax.dynamic_index_in_dim(parts, side, 0, keepdims=False)
        sent = lax.dynamic_index_in_dim(parts, 1 - side, 0, keepdims=False)
        return add_low(kept, self.swap(sent, step))

    def double(self, block, step):
        got = self.swap(block, step)
        side = jnp.where(self.upper(step), 1, 0)
        rows = block.shape[0]
        whole = jnp.zeros((2 * rows,) + block.shape[1:], block.dtype)
        whole = lax.dynamic_update_slice_in_dim(whole, block, side * rows, 0)
        return lax.dynamic_update_slice_in_dim(whole, got, (1 - side) * rows, 0)


def shards(
    images,
    image_counts,
    conv_kernel,
    bn_gain,
    bn_bias,
    mix_h,
    mix_h_bias,
    mix_w,
    mix_w_bias,
    unite_w,
    unite_b,
    ln_gain,
    ln_bias,
    w_in,
    b_in,
    w_out,
    b_out,
    running_mean,
    running_var,
    cotangent,
):
    n_dp, n_pipe = lax.axis_size("dp"), lax.axis_size("pipe")
    dp, pipe = lax.axis_index("dp"), lax.axis_index("pipe")
    layers = n_pipe
    batch = images.shape[0] // n_pipe
    side, chans, hid = images.shape[1], images.shape[3], w_in.shape[2]
    sz = Sizes(batch, side, chans, hid, n_dp)
    core, plane = pipe & 1, pipe >> 1
    tokens = sz.tokens

    def shape(*dims, dtype=F32):
        return jax.ShapeDtypeStruct(dims, dtype)

    valid = jnp.clip(image_counts[0] - pipe * batch, 0, batch).astype(jnp.int32)
    info = jnp.stack([valid, pipe.astype(jnp.int32), (dp & 1).astype(jnp.int32)])

    own, own_half, small_own = run_whole(
        functools.partial(prepare_kernel, sz),
        (
            shape(chans, sz.weight_lanes, dtype=BF16),
            shape(chans // 2, sz.weight_lanes, dtype=BF16),
            shape(SMALL_ROWS, sz.lanes),
        ),
        info,
        (
            conv_kernel[0],
            bn_gain,
            bn_bias,
            mix_h[0],
            mix_h_bias,
            mix_w[0],
            mix_w_bias,
            unite_w[0].T,
            unite_b,
            ln_gain,
            ln_bias,
            w_in[0],
            b_in,
            w_out[0].T,
            b_out,
        ),
        "prepare",
        2,
    )
    small_across = swap(small_own, "pipe", n_pipe, 2)
    small_beside = swap(small_own, "pipe", n_pipe, 1)
    small_far = swap(small_across, "pipe", n_pipe, 1)
    smalls = (small_own, small_beside, small_across, small_far)
    (half_sent,) = tie((own_half,), (small_across,))
    beside = swap(own, "pipe", n_pipe, 1)

    def across_plane(half, cores):
        return lax.ppermute(half, "pipe", [(p, p ^ 2) for p in cores])

    def to_beside(half, cores):
        return lax.ppermute(half, "pipe", [(p, p ^ 1) for p in cores])

    def to_neighbour(half, cores):
        route = [
            (d * n_pipe + p, (d ^ 1) * n_pipe + p) for d in range(n_dp) for p in cores
        ]
        return lax.ppermute(half, ("dp", "pipe"), route)

    first = across_plane(half_sent, (0, 2))

    def micro(array):
        block = lax.dynamic_slice_in_dim(array, pipe * batch, batch, 0)
        block = jnp.pad(block, ((0, 0), (0, 0), (0, sz.pad - side), (0, 0)))
        return block.reshape(tokens, chans)

    sums_shape = shape(n_dp, 8, LANES)
    plain = shape(tokens, chans)
    low = shape(tokens, chans, dtype=BF16)

    field = micro(images)
    conv, sums = run(
        functools.partial(start_kernel, sz),
        (plain, sums_shape),
        info,
        (field, (0, smalls)),
        "start",
        2,
    )
    got = lax.all_to_all(sums, "dp", 0, 0)
    (first,) = tie((first,), (sums,))
    first_beside, second = to_beside(first, (0, 2)), to_neighbour(first, (0, 2))
    (second,) = tie((second,), (got,))
    (half_late,) = tie((own_half,), (first_beside,))
    first_odd = across_plane(half_late, (1, 3))
    second_beside = to_beside(second, (0, 2))
    even = (own, beside, (first, second), (first_beside, second_beside))

    fields, convs, saved, stats, weights = [field], [conv], [], [], [even]
    for depth in range(layers):
        if depth:
            got = lax.all_to_all(sums, "dp", 0, 0)
        last = depth + 1 == layers
        outs = (
            low,
            shape(tokens, hid, dtype=BF16),
            shape(tokens, hid, dtype=BF16),
            plain,
            shape(tokens, 1),
            low,
            low,
            low,
            shape(8, sz.lanes),
        )
        flat = (got, convs[depth], (depth, smalls), (depth, weights[depth & 1]), fields[depth])
        if not last:
            outs += (plain, sums_shape)
            flat += ((depth + 1, smalls),)
        results = run(
            functools.partial(forward_kernel, sz, last),
            outs,
            info,
            flat,
            f"layer_{depth}_forward",
            6,
        )
        fields.append(results[0])
        if depth == 0:
            (first_odd,) = tie((first_odd,), (second_beside,))
            first_odd_beside = to_beside(first_odd, (1, 3))
            second_odd = to_neighbour(first_odd, (1, 3))
            (second_odd,) = tie((second_odd,), (results[0],))
            second_odd_beside = to_beside(second_odd, (1, 3))
            weights.append(
                (own, beside, (first_odd, second_odd), (first_odd_beside, second_odd_beside))
            )
        saved.append(results[1:8])
        stats.append(results[8])
        if not last:
            convs.append(results[9])
            sums = results[10]

    def to_owners(parts):
        sent = [lax.select_n(pipe ^ bit, *parts) for bit in range(n_pipe)]
        return sent[:1] + [swap(sent[bit], "pipe", n_pipe, bit) for bit in range(1, n_pipe)]

    def collect(parts):
        whole = jnp.zeros((n_pipe, batch, side, side, chans), BF16)
        for bit, part in enumerate(parts):
            part = part.reshape(1, batch, side, sz.pad, chans)[:, :, :, :side]
            whole = lax.dynamic_update_slice(whole, part, (pipe ^ bit, 0, 0, 0, 0))
        return whole.reshape(1, n_pipe * batch, side, side, chans)

    half_shape = shape(sz.half_rows, LANES, dtype=BF16)
    halves, ends = [None] * layers, [None] * 2
    grads, closes = [None] * layers, [None] * layers
    behind = None
    outputs = to_owners(fields[1:])
    for depth in reversed(range(layers)):
        outs = (half_shape, half_shape, plain, plain, sums_shape)
        if behind is None:
            front = (micro(cotangent),)
        else:
            front = behind
            outs += (low, shape(CLOSE_ROWS, sz.lanes))
            if depth > 0:
                front = tie(front[:1], outputs[1:2] + outputs[4 - depth : 5 - depth]) + front[1:]
        active, slope, unit, spread, normed, rows_mixed, cols_mixed = saved[depth]
        results = run(
            functools.partial(backward_kernel, sz, behind is None),
            outs,
            info,
            front
            + ((depth, smalls), (depth, weights[depth & 1]), slope, unit, spread, active)
            + (normed, rows_mixed, cols_mixed, stats[depth], convs[depth]),
            f"layer_{depth}_backward",
            12,
            scratch=[
                pltpu.VMEM((2,) + half_shape.shape, BF16),
                pltpu.SemaphoreType.DMA((2,)),
            ],
            direct=2,
        )
        kept, sent, normed_grad, hidden_grad, sums = results[:5]
        if behind is not None:
            grads[depth + 1], closes[depth + 1] = results[5:]
        halves[depth] = add_low(kept, swap(sent, "pipe", n_pipe, 1))
        if depth == 0:
            ends[1] = add_low(*tie(ends[1], (sums,)))
            (sums,) = tie((sums,), (ends[1],))
        if depth < 2:
            mine = jnp.where(plane == 0, halves[depth], halves[depth + 2])
            other = jnp.where(plane == 0, halves[depth + 2], halves[depth])
            ends[depth] = (mine, swap(other, "pipe", n_pipe, 2))
        got = lax.all_to_all(sums, "dp", 0, 0)
        (got,) = tie((got,), (halves[depth],))
        behind = (
            got,
            stats[depth],
            (depth, smalls),
            normed_grad,
            convs[depth],
            hidden_grad,
            fields[depth],
        )
    ring = Ring(n_dp, n_pipe, dp, core)
    odd, even = ends[1], add_low(*ends[0])
    layer_outputs = collect(outputs)
    for step in range(ring.steps):
        odd = ring.halve(odd, step)
    behind = tie(behind[:1], (even, odd, layer_outputs)) + behind[1:]
    grads[0], closes[0] = run(
        functools.partial(finish_kernel, sz),
        (low, shape(CLOSE_ROWS, sz.lanes)),
        info,
        behind,
        "finish",
        4,
    )
    closing = lax.all_to_all(jnp.stack(closes), "pipe", 0, 0)
    grad_parts = to_owners(grads)
    for step in range(ring.steps):
        even = ring.halve(even, step)
        odd = ring.double(odd, ring.steps - 1 - step)
        if step == 0:
            even, odd = tie((even, odd), (grads[0],))
        elif step == 1:
            even, odd = tie((even, odd), (closing,))
            taps = jnp.sum(closing[:, 4:13], axis=0)
            taps = lax.all_to_all(
                jnp.broadcast_to(taps[None], (n_dp,) + taps.shape), "dp", 0, 0
            )
        else:
            even, odd = tie((even, odd), ())
    input_grads = collect(grad_parts)
    for step in reversed(range(ring.steps)):
        even = ring.double(even, step)
        if step == ring.steps - 1:
            (even,) = tie((even,), (taps,))
        if step == 1:
            (even,) = tie((even,), (input_grads,))
    parts = [odd, even]
    mine = jnp.where(core == 0, parts[1], parts[0])
    other = jnp.where(core == 0, parts[0], parts[1])
    got = swap(other, "pipe", n_pipe, 1)
    row = shape(1, chans)
    outs = (
        shape(3, 3, 1, chans),
        row,
        row,
        shape(side, 1, side),
        shape(1, side),
        shape(side, 1, side),
        shape(1, side),
        shape(chans, 3 * chans),
        row,
        row,
        row,
        shape(chans, hid),
        shape(1, hid),
        shape(chans, hid),
        row,
        row,
        row,
    )
    finished = list(
        run_whole(
            functools.partial(closing_kernel, sz),
            outs,
            info,
            (mine, got, closing, taps, running_mean, running_var),
            "closing",
            4,
        )
    )
    finished[0] = jnp.transpose(finished[0], (2, 0, 1, 3))
    for k in (3, 5):
        finished[k] = jnp.transpose(finished[k], (1, 0, 2))
    for k in (7, 13):
        finished[k] = finished[k].T[None]
    finished[11] = finished[11][None]
    return (layer_outputs, input_grads) + tuple(finished)


def solution(mesh):
    four = P("pipe", None, None, None)
    three = P("pipe", None, None)
    two = P("pipe", None)
    images = P("dp", None, None, None)
    in_specs = (
        images, P("dp"), four, two, two, three, two, three, two, three, two, two, two,
        three, two, three, two, two, two, images,
    )
    stacked = P("pipe", "dp", None, None, None)
    out_specs = (
        stacked, stacked, four, two, two, three, two, three, two, three, two, two, two,
        three, two, three, two, two, two,
    )
    return jax.shard_map(
        shards, mesh=mesh, in_specs=in_specs, out_specs=out_specs, check_vma=False
    )
```

```python
import functools

import jax
import jax.numpy as jnp
from jax import lax
from jax.experimental import pallas as pl
from jax.experimental.pallas import tpu as pltpu
from jax.sharding import PartitionSpec as P

F32 = jnp.float32
BF16 = jnp.bfloat16
LANES = 128
HID_STEP = 256
ROW_STEP = 64
LN_STEP = 32
VMEM_BYTES = 58 * 1024 * 1024
EXTRA = 128
ROW_BN_GAIN, ROW_BN_BIAS, ROW_UNITE_B, ROW_LN_GAIN, ROW_LN_BIAS, ROW_B_OUT = range(9, 15)
ROW_MIX_BIAS, ROW_B_IN, ROW_MIX = 15, 16, 24
SMALL_ROWS = 40
CLOSE_ROWS = 16
GRAD_ROWS = 64


def wide(value):
    return -(-value // LANES) * LANES


def tall(value):
    return -(-value // 16) * 16


def dot(left, right):
    return lax.dot_general(left, right, (((1,), (0,)), ((), ())), preferred_element_type=F32)


def dot_nt(left, right):
    return lax.dot_general(left, right, (((1,), (1,)), ((), ())), preferred_element_type=F32)


def dot_exact(left, right):
    return lax.dot_general(
        left,
        right,
        (((1,), (0,)), ((), ())),
        preferred_element_type=F32,
        precision=lax.Precision.HIGHEST,
    )


class Sizes:
    def __init__(self, batch, side, chans, hid, n_dp):
        self.batch, self.side, self.chans, self.hid, self.n_dp = batch, side, chans, hid, n_dp
        self.pad = tall(side)
        self.image = side * self.pad
        self.tokens = batch * self.image
        self.lanes = wide(chans)
        self.full = chans // LANES
        self.rest = chans - self.full * LANES
        self.hid_blocks = hid // LANES
        left_blocks = -(-3 * self.rest // LANES)
        self.unite_blocks = 3 * self.full + left_blocks
        self.blocks = 2 * self.hid_blocks + self.unite_blocks
        self.half_blocks = self.blocks // 2
        self.half_rows = self.half_blocks * chans + EXTRA
        self.weight_lanes = 2 * hid + 3 * self.lanes

    def place(self, block):
        half, place = divmod(block, self.half_blocks)
        return half, place * self.chans

    def unite(self, part):
        first = 2 * self.hid + part * self.lanes
        return slice(first, first + self.chans)


def token_mask(sz, valid):
    row = lax.broadcasted_iota(jnp.int32, (sz.tokens, 1), 0)
    return ((row < valid * sz.image) & (row % sz.pad < sz.side)).astype(F32)


def taps_of(sz, small):
    return [small[k : k + 1, : sz.chans] for k in range(9)]


def row_of(sz, small, index):
    return small[index : index + 1, : sz.chans]


def fill_lanes(sz, row):
    if sz.lanes == sz.chans:
        return row
    return jnp.concatenate([row, jnp.zeros((1, sz.lanes - sz.chans), F32)], axis=1)


def lane_rows(sz, row):
    row = fill_lanes(sz, row)
    return [row[:, k * LANES : (k + 1) * LANES] for k in range(sz.lanes // LANES)]


def put_sums(sz, ref, first, second, number):
    pieces = lane_rows(sz, first) + lane_rows(sz, second)
    pieces.append(jnp.zeros((1, LANES), F32) + number)
    pieces.append(jnp.zeros((8 - len(pieces), LANES), F32))
    block = jnp.concatenate(pieces, axis=0)
    for index in range(sz.n_dp):
        ref[index] = block


def take_sums(sz, ref):
    total = ref[0]
    for index in range(1, sz.n_dp):
        total = total + ref[index]
    count = sz.lanes // LANES
    first = jnp.concatenate([total[k : k + 1] for k in range(count)], axis=1)
    second = jnp.concatenate([total[count + k : count + k + 1] for k in range(count)], axis=1)
    return first[:, : sz.chans], second[:, : sz.chans], total[2 * count : 2 * count + 1, 0:1]


def sum_rows(value):
    return jnp.sum(value, axis=0, keepdims=True)


def mean_lanes(value):
    return jnp.mean(value, axis=1, keepdims=True)


def pick_rows(sz):
    row = lax.broadcasted_iota(jnp.int32, (sz.image, sz.pad), 0)
    col = lax.broadcasted_iota(jnp.int32, (sz.image, sz.pad), 1)
    return (row // sz.pad == col), (row % sz.pad == col)


def same_masks(sz):
    row = lax.broadcasted_iota(jnp.int32, (sz.image, sz.image), 0)
    col = lax.broadcasted_iota(jnp.int32, (sz.image, sz.image), 1)
    return (row % sz.pad == col % sz.pad), (row // sz.pad == col // sz.pad)


def mixers(sz, small, turned):
    pick_i, pick_j = pick_rows(sz)
    same_j, same_i = same_masks(sz)
    product = dot_nt if turned else dot
    found = []
    for pick, same, lane in ((pick_i, same_j, 0), (pick_j, same_i, LANES)):
        mix = small[ROW_MIX : ROW_MIX + sz.pad, lane : lane + sz.pad].astype(BF16)
        pick = pick.astype(BF16)
        spread = dot_nt(product(pick, mix).astype(BF16), pick)
        found.append(jnp.where(same, spread, 0.0).astype(BF16))
    return found


class Arrivals:
    def __init__(self, sources, buffers, sems, role_of, bit, layers):
        self.buffers, self.copies = buffers, []
        for k, (source, buffer) in enumerate(zip(sources, buffers)):
            if layers[k] is None:
                copies = [pltpu.make_async_copy(source, buffer, sems.at[k, 0])]
                copies[0].start()
            else:
                halved = isinstance(source[-1], tuple)
                rows = buffer.shape[0] // 2 if halved else buffer.shape[0]
                spots = [pl.ds(0, rows), pl.ds(rows, rows)] if halved else [pl.ds(0, rows)]
                copies = [
                    pltpu.make_async_copy(source[0].at[spot], buffer.at[spot], sems.at[k, h])
                    for h, spot in enumerate(spots)
                ]
                for place, held in enumerate(source):

                    @pl.when(role_of(layers[k]) == place)
                    def _(held=held, buffer=buffer, k=k, spots=spots, rows=rows):
                        for h, spot in enumerate(spots):
                            if isinstance(held, tuple):
                                piece = held[h]
                                at = h ^ bit
                                spot = pl.ds(pl.multiple_of(at * rows, 16), rows)
                            else:
                                piece = held.at[spot]
                            pltpu.make_async_copy(piece, buffer.at[spot], sems.at[k, h]).start()

            self.copies.append(copies)

    def __getitem__(self, k):
        if self.copies[k] is not None:
            for copy in self.copies[k]:
                copy.wait()
            self.copies[k] = None
        return self.buffers[k]

    def close(self):
        for k in range(len(self.copies)):
            self[k]


class Departures:
    def __init__(self, targets, buffers, sems, direct):
        self.buffers, self.targets = buffers, targets
        self.copies = [
            None if k < direct else pltpu.make_async_copy(buffer, target, sems.at[k])
            for k, (target, buffer) in enumerate(zip(targets, buffers))
        ]
        self.started, self.parts = [False] * len(self.copies), []

    def put(self, k, value):
        self.buffers[k][...] = value
        self.send(k)

    def send(self, k):
        self.copies[k].start()
        self.started[k] = True

    def send_part(self, k, lanes, sem):
        spot = (slice(None), lanes)
        copy = pltpu.make_async_copy(self.buffers[k].at[spot], self.targets[k].at[spot], sem)
        copy.start()
        self.parts.append(copy)

    def close(self):
        for copy, started in zip(self.copies, self.started):
            if started:
                copy.wait()
        for copy in self.parts:
            copy.wait()


def prepare_kernel(
    sz,
    info,
    taps_ref,
    bn_gain_ref,
    bn_bias_ref,
    mix_h_ref,
    mix_h_bias_ref,
    mix_w_ref,
    mix_w_bias_ref,
    unite_ref,
    unite_b_ref,
    ln_gain_ref,
    ln_bias_ref,
    in_ref,
    b_in_ref,
    w_out_ref,
    b_out_ref,
    weights_ref,
    half_ref,
    small_ref,
):
    chans, hid = sz.chans, sz.hid
    weights_ref[:, :hid] = in_ref[...]
    weights_ref[:, hid : 2 * hid] = w_out_ref[...]
    gap = jnp.zeros((chans, sz.lanes - chans), BF16)
    for part in range(3):
        first = 2 * hid + part * sz.lanes
        weights_ref[:, first : first + sz.lanes] = jnp.concatenate(
            [unite_ref[:, part * chans : (part + 1) * chans], gap], axis=1
        )
    rows = half_ref.shape[0]
    half_ref[...] = weights_ref[pl.ds(pl.multiple_of(info[2] * rows, 16), rows)]
    small_ref[...] = jnp.zeros(small_ref.shape, F32)
    for p in range(3):
        small_ref[3 * p : 3 * p + 3, :chans] = taps_ref[p].astype(F32)
    rows = (bn_gain_ref, bn_bias_ref, unite_b_ref, ln_gain_ref, ln_bias_ref, b_out_ref)
    for place, ref in zip(range(ROW_BN_GAIN, ROW_MIX_BIAS), rows):
        small_ref[place : place + 1, :chans] = ref[...]
    place = ROW_MIX_BIAS
    small_ref[place : place + 1, : sz.side] = mix_h_bias_ref[...]
    small_ref[place : place + 1, LANES : LANES + sz.side] = mix_w_bias_ref[...]
    for k, lane in enumerate(range(0, hid, sz.lanes)):
        wide_part = min(sz.lanes, hid - lane)
        small_ref[ROW_B_IN + k : ROW_B_IN + k + 1, :wide_part] = b_in_ref[
            :, lane : lane + wide_part
        ]
    rows = slice(ROW_MIX, ROW_MIX + sz.side)
    small_ref[rows, : sz.side] = mix_h_ref[...].astype(F32)
    small_ref[rows, LANES : LANES + sz.side] = mix_w_ref[...].astype(F32)


def steps(size, step):
    return [slice(first, min(first + step, size)) for first in range(0, size, step)]


def fold(value):
    total = value[:8]
    for first in range(8, value.shape[0], 8):
        total = total + value[first : first + 8]
    return total


def conv_rows(sz, rows, taps, back=False):
    order = (2, 1, 0) if back else (0, 1, 2)
    parts = []
    for row in rows:
        near = (pltpu.roll(row, 1, 0), row, pltpu.roll(row, sz.pad - 1, 0))
        near = [near[q] for q in order]
        parts.append(
            [taps[3 * p] * near[0] + taps[3 * p + 1] * near[1] + taps[3 * p + 2] * near[2] for p in order]
        )
    found = []
    for i in range(len(rows)):
        total = parts[i][1]
        if i > 0:
            total = total + parts[i - 1][0]
        if i + 1 < len(rows):
            total = total + parts[i + 1][2]
        found.append(total)
    return found


def next_conv(sz, rows, taps, masks, conv_ref, sums_ref, number):
    first = jnp.zeros((8, sz.chans), F32)
    second = jnp.zeros((8, sz.chans), F32)
    for n in range(sz.batch):
        part = range(n * sz.side, (n + 1) * sz.side)
        for i, conv in zip(part, conv_rows(sz, [rows[i] for i in part], taps)):
            conv_ref[i * sz.pad : (i + 1) * sz.pad] = conv
            masked = masks[i] * conv
            first = first + fold(masked)
            second = second + fold(masked * conv)
    put_sums(sz, sums_ref, sum_rows(first), sum_rows(second), number)


def row_masks(sz, valid):
    mask = token_mask(sz, valid)
    return [mask[i : i + sz.pad] for i in range(0, sz.tokens, sz.pad)]


def start_kernel(sz, info, ins, outs):
    field = ins[0]
    kernel = ins[1]
    taps = [kernel[p, q : q + 1].astype(F32) for p in range(3) for q in range(3)]
    rows = [field[i : i + sz.pad].astype(F32) for i in range(0, sz.tokens, sz.pad)]
    number = (info[0] * (sz.side * sz.side)).astype(F32)
    masks = row_masks(sz, info[0])
    next_conv(sz, rows, taps, masks, outs.buffers[0], outs.buffers[1], number)
    outs.send(0)
    outs.send(1)


def forward_kernel(sz, last, info, ins, outs, part_sems):
    GOT, CONV, SMALL, WEIGHTS, FIELD = range(5)
    OUT, ACTIVE, SLOPE, UNIT, SPREAD, JOINED, STAT, CONV_NEXT, SUMS = range(9)
    small = ins[SMALL]
    total, square, count = take_sums(sz, ins[GOT])
    center = total / count
    variance = square / count - center * center
    inverse = lax.rsqrt(variance + 1e-05)
    stat = [
        fill_lanes(sz, center),
        fill_lanes(sz, inverse),
        fill_lanes(sz, variance * count / (count - 1.0)),
        jnp.zeros((1, sz.lanes), F32) + count,
        jnp.zeros((4, sz.lanes), F32),
    ]
    outs.put(STAT, jnp.concatenate(stat, axis=0))
    gain = inverse * row_of(sz, small, ROW_BN_GAIN)
    shift = row_of(sz, small, ROW_BN_BIAS)
    conv, joined = ins[CONV], outs.buffers[JOINED]
    chans, lanes = sz.chans, sz.lanes
    for rows in steps(sz.tokens, ROW_STEP):
        normed = ((conv[rows] - center) * gain + shift).astype(BF16)
        gap = jnp.zeros((normed.shape[0], lanes - chans), BF16)
        joined[rows, :lanes] = jnp.concatenate([normed, gap], axis=1)
    mix_h, mix_w = mixers(sz, small, False)
    pick_i, pick_j = pick_rows(sz)
    bias = small[ROW_MIX_BIAS : ROW_MIX_BIAS + 1]
    bias_h = jnp.sum(jnp.where(pick_i, bias[:, : sz.pad], 0.0), axis=1, keepdims=True)
    bias_w = jnp.sum(
        jnp.where(pick_j, bias[:, LANES : LANES + sz.pad], 0.0), axis=1, keepdims=True
    )
    for n in range(sz.batch):
        normed = joined[n * sz.image : (n + 1) * sz.image, :lanes]
        for mix, add, place in ((mix_h, bias_h, 1), (mix_w, bias_w, 2)):
            mixed = dot(mix, normed)
            for rows in steps(sz.image, ROW_STEP):
                there = slice(n * sz.image + rows.start, n * sz.image + rows.stop)
                joined[there, place * lanes : (place + 1) * lanes] = (
                    mixed[rows] + add[rows]
                ).astype(BF16)
    outs.send(JOINED)
    weights_ref = ins[WEIGHTS]
    field = ins[FIELD]
    united = dot_nt(joined[...], weights_ref[:, 2 * sz.hid :])
    unite_b = row_of(sz, small, ROW_UNITE_B)
    ln_gain, ln_bias = row_of(sz, small, ROW_LN_GAIN), row_of(sz, small, ROW_LN_BIAS)
    hidden, lnormed = [], []
    for rows in steps(sz.tokens, LN_STEP):
        part = field[rows].astype(F32) + (united[rows] + unite_b)
        offset = part - mean_lanes(part)
        spread = lax.rsqrt(mean_lanes(offset * offset) + 1e-06)
        unit = offset * spread
        outs.buffers[UNIT][rows] = unit
        outs.buffers[SPREAD][rows] = spread
        hidden.append(part)
        lnormed.append((unit * ln_gain + ln_bias).astype(BF16))
    hidden = jnp.concatenate(hidden, axis=0)
    lnormed = jnp.concatenate(lnormed, axis=0)
    outs.send(UNIT)
    outs.send(SPREAD)
    lanes_in = [small[ROW_B_IN + k : ROW_B_IN + k + 1] for k in range(-(-sz.hid // lanes))]
    b_in = jnp.concatenate(lanes_in, axis=1)
    root = 0.7978845608028654
    cubic = 0.044715
    for part in steps(sz.hid, HID_STEP):
        product = dot(lnormed, weights_ref[:, part])
        for rows in steps(sz.tokens, ROW_STEP):
            before = product[rows] + b_in[:, part]
            squared = before * before
            bent = jnp.tanh(before * (root + (root * cubic) * squared))
            half = 0.5 + 0.5 * bent
            active = before * half
            slope = half + (active * (1.0 - bent)) * (root + (3.0 * root * cubic) * squared)
            outs.buffers[ACTIVE][rows, part] = active.astype(BF16)
            outs.buffers[SLOPE][rows, part] = slope.astype(BF16)
        index = part.start // HID_STEP
        outs.send_part(ACTIVE, part, part_sems.at[0, index])
        outs.send_part(SLOPE, part, part_sems.at[1, index])
    branch = dot_nt(outs.buffers[ACTIVE][...], weights_ref[:, sz.hid : 2 * sz.hid])
    masks = row_masks(sz, info[0])
    b_out = row_of(sz, small, ROW_B_OUT)
    results = []
    for i, mask in enumerate(masks):
        rows = slice(i * sz.pad, (i + 1) * sz.pad)
        result = (mask * (hidden[rows] + (branch[rows] + b_out))).astype(BF16)
        outs.buffers[OUT][rows] = result
        results.append(result.astype(F32))
    outs.send(OUT)
    if not last:
        number = (info[0] * (sz.side * sz.side)).astype(F32)
        taps = taps_of(sz, ins[5])
        next_conv(
            sz, results, taps, masks, outs.buffers[CONV_NEXT], outs.buffers[SUMS], number
        )
        outs.send(SUMS)
        outs.send(CONV_NEXT)


def finish_layer(sz, info, ins, outs, first_out):
    GOT, STAT, SMALL, NORMED_GRAD, CONV, HIDDEN_GRAD, FIELD = range(7)
    small, stat = ins[SMALL], ins[STAT]
    chans = sz.chans
    taps = taps_of(sz, small)
    sum_dz, sum_dzx, _ = take_sums(sz, ins[GOT])
    count = stat[3:4, 0:1]
    center, inverse = stat[0:1, :chans], stat[1:2, :chans]
    scale = inverse * row_of(sz, small, ROW_BN_GAIN)
    mean_dz, mean_dzx = sum_dz / count, inverse * (sum_dzx / count)
    normed_grad, conv, hidden_grad, field = (
        ins[k] for k in (NORMED_GRAD, CONV, HIDDEN_GRAD, FIELD)
    )
    masks = row_masks(sz, info[0])
    sums = [jnp.zeros((8, chans), F32) for _ in range(9)]
    grads = []
    for n in range(sz.batch):
        spots = [
            slice(i * sz.pad, (i + 1) * sz.pad) for i in range(n * sz.side, (n + 1) * sz.side)
        ]
        conv_grads = [
            (masks[n * sz.side + i] * scale)
            * (normed_grad[rows] - mean_dz - (conv[rows] - center) * mean_dzx)
            for i, rows in enumerate(spots)
        ]
        for rows, back in zip(spots, conv_rows(sz, conv_grads, taps, back=True)):
            grad = (hidden_grad[rows] + back).astype(BF16)
            outs.buffers[first_out][rows] = grad
            grads.append(grad)
        for i, rows in enumerate(spots):
            row = field[rows].astype(F32)
            near = (pltpu.roll(row, 1, 0), row, pltpu.roll(row, sz.pad - 1, 0))
            for p in range(3):
                there = i + 1 - p
                if 0 <= there < sz.side:
                    for q in range(3):
                        sums[3 * p + q] = sums[3 * p + q] + fold(conv_grads[there] * near[q])
    outs.send(first_out)
    pieces = [center, stat[2:3, :chans], sum_dz, sum_dzx] + [sum_rows(item) for item in sums]
    block = [fill_lanes(sz, piece) for piece in pieces]
    block.append(jnp.zeros((CLOSE_ROWS - len(pieces), sz.lanes), F32))
    outs.put(first_out + 1, jnp.concatenate(block, axis=0))
    return grads


def finish_kernel(sz, info, ins, outs):
    finish_layer(sz, info, ins, outs, 0)


def backward_kernel(sz, first, info, ins, outs, pack_ref, before_ref, pack_sems):
    base = 1 if first else 7
    SMALL, WEIGHTS, SLOPE, UNIT, SPREAD, ACTIVE, JOINED, STAT, CONV = range(base, base + 9)
    core = info[1] & 1
    chans, tokens, lanes = sz.chans, sz.tokens, sz.lanes
    shipped = []

    def put(block, value):
        half, row = sz.place(block)
        pack_ref[half ^ core, row : row + chans] = value

    def ship(half, first_row, rows):
        spot, sem = pl.ds(first_row, rows), pack_sems.at[len(shipped)]
        for place in range(2):

            @pl.when(half ^ core == place)
            def _(place=place):
                pltpu.make_async_copy(
                    pack_ref.at[place, spot], outs.targets[place].at[spot], sem
                ).start()

        shipped.append(
            pltpu.make_async_copy(pack_ref.at[0, spot], outs.targets[0].at[spot], sem)
        )

    if first:
        upstream = [ins[0][i : i + sz.pad] for i in range(0, tokens, sz.pad)]
    else:
        upstream = finish_layer(sz, info, ins, outs, 5)
    small = ins[SMALL]
    masks = row_masks(sz, info[0])
    out_grads = [mask * grad.astype(F32) for mask, grad in zip(masks, upstream)]
    branch_grad = jnp.concatenate([item.astype(BF16) for item in out_grads], axis=0)
    out_sum = fold(out_grads[0])
    for item in out_grads[1:]:
        out_sum = out_sum + fold(item)
    out_grads = jnp.concatenate(out_grads, axis=0)
    unit = ins[UNIT]
    ln_gain, ln_bias = row_of(sz, small, ROW_LN_GAIN), row_of(sz, small, ROW_LN_BIAS)
    lnormed = [
        (unit[rows] * ln_gain + ln_bias).astype(BF16) for rows in steps(tokens, ROW_STEP)
    ]
    lnormed = jnp.concatenate(lnormed, axis=0)
    turned_ln = jnp.concatenate([lnormed.T, jnp.ones((16, tokens), BF16)], axis=0)
    turned_branch = branch_grad.T
    weights_ref, slope_ref, active_ref = ins[WEIGHTS], ins[SLOPE], ins[ACTIVE]
    in_pieces = []
    for k in range(0, sz.hid, HID_STEP):
        part = slice(k, k + HID_STEP)
        active_grad = dot(branch_grad, weights_ref[:, sz.hid + k : sz.hid + k + HID_STEP])
        for rows in steps(tokens, ROW_STEP):
            before_ref[rows, part] = (
                active_grad[rows] * slope_ref[rows, part].astype(F32)
            ).astype(BF16)
        grad_in = dot(turned_ln, before_ref[:, part])
        grad_out = dot(turned_branch, active_ref[:, part])
        for lane in range(0, HID_STEP, LANES):
            block = (k + lane) // LANES
            put(block, grad_in[:chans, lane : lane + LANES].astype(BF16))
            put(sz.hid_blocks + block, grad_out[:, lane : lane + LANES].astype(BF16))
            in_pieces.append(grad_in[chans : chans + 1, lane : lane + LANES])
    norm_grad = dot_nt(before_ref[...], weights_ref[:, : sz.hid])
    ship(0, 0, sz.half_blocks * chans)
    spread = ins[SPREAD]
    token_grad = []
    token_sum, gain_sum, bias_sum = (jnp.zeros((8, chans), F32) for _ in range(3))
    for rows in steps(tokens, LN_STEP):
        grad, part = norm_grad[rows], unit[rows]
        product = grad * part
        gain_sum = gain_sum + fold(product)
        bias_sum = bias_sum + fold(grad)
        scaled = grad * ln_gain
        hidden_grad = out_grads[rows] + spread[rows] * (
            scaled - mean_lanes(scaled) - part * mean_lanes(product * ln_gain)
        )
        outs.buffers[3][rows] = hidden_grad
        token = hidden_grad.astype(BF16)
        token_grad.append(token)
        token_sum = token_sum + fold(token.astype(F32))
    token_grad = jnp.concatenate(token_grad, axis=0)
    outs.send(3)
    joined = ins[JOINED]
    joined_grad = dot(token_grad, weights_ref[:, 2 * sz.hid :])
    rows_grad = joined_grad[:, lanes : lanes + chans].astype(BF16)
    cols_grad = joined_grad[:, 2 * lanes : 2 * lanes + chans].astype(BF16)
    turned_h, turned_w = mixers(sz, small, True)
    stat, conv = ins[STAT], ins[CONV]
    center, inverse = stat[0:1, :chans], stat[1:2, :chans]
    sum_dz, sum_dzx = (jnp.zeros((8, chans), F32) for _ in range(2))
    for n in range(sz.batch):
        image = slice(n * sz.image, (n + 1) * sz.image)
        back_h = dot(turned_h, rows_grad[image])
        back_w = dot(turned_w, cols_grad[image])
        for rows in steps(sz.image, ROW_STEP):
            there = slice(image.start + rows.start, image.start + rows.stop)
            normed_grad = joined_grad[there, :chans] + (back_h[rows] + back_w[rows])
            outs.buffers[2][there] = normed_grad
            sum_dz = sum_dz + fold(normed_grad)
            sum_dzx = sum_dzx + fold(normed_grad * ((conv[there] - center) * inverse))
    put_sums(sz, outs.buffers[4], sum_rows(sum_dz), sum_rows(sum_dzx), 0.0)
    outs.send(4)
    outs.send(2)
    grad_unite = dot(token_grad.T, joined[...]).astype(BF16)
    block = 2 * sz.hid_blocks
    leftovers = []
    for part in range(3):
        for k in range(sz.full):
            lane = part * lanes + k * LANES
            put(block, grad_unite[:, lane : lane + LANES])
            block += 1
        if sz.rest:
            lane = part * lanes + sz.full * LANES
            leftovers.append(grad_unite[:, lane : lane + sz.rest])
    if sz.rest:
        left = jnp.concatenate(leftovers, axis=1)
        fill = wide(left.shape[1]) - left.shape[1]
        if fill:
            left = jnp.concatenate([left, jnp.zeros((chans, fill), BF16)], axis=1)
        for lane in range(0, left.shape[1], LANES):
            put(block, left[:, lane : lane + LANES])
            block += 1
    ship(1, 0, sz.half_blocks * chans)
    pick_i, pick_j = pick_rows(sz)
    same_j, same_i = same_masks(sz)
    mix_pieces, bias_pieces = [], []
    for grads, pick, same in ((rows_grad, pick_i, same_j), (cols_grad, pick_j, same_i)):
        pairs = jnp.zeros((sz.image, sz.image), F32)
        sums = jnp.zeros((sz.image, 1), F32)
        for n in range(sz.batch):
            image = slice(n * sz.image, (n + 1) * sz.image)
            pairs = pairs + dot_nt(grads[image], joined[image, :chans])
            sums = sums + jnp.sum(grads[image].astype(F32), axis=1, keepdims=True)
        pairs = jnp.where(same, pairs, 0.0)
        picked = pick.astype(F32)
        groups = [pairs[i : i + sz.pad] for i in range(0, sz.image, sz.pad)]
        if pick is pick_i:
            near = [sum_rows(group) for group in groups]
            near.append(jnp.zeros((sz.pad - sz.side, sz.image), F32))
            near = jnp.concatenate(near, axis=0)
        else:
            near = groups[0]
            for group in groups[1:]:
                near = near + group
        small_grad = dot_exact(near, picked)
        gap = LANES - sz.pad
        mix_pieces.append(
            jnp.concatenate([small_grad, jnp.zeros((sz.pad, gap), F32)], axis=1)
        )
        bias_pieces.append(
            jnp.concatenate([sum_rows(picked * sums), jnp.zeros((1, gap), F32)], axis=1)
        )
    pieces = (
        lane_rows(sz, sum_rows(token_sum))
        + lane_rows(sz, sum_rows(gain_sum))
        + lane_rows(sz, sum_rows(bias_sum))
        + lane_rows(sz, sum_rows(out_sum))
        + in_pieces
        + bias_pieces
        + mix_pieces
    )
    used = sum(piece.shape[0] for piece in pieces)
    pieces.append(jnp.zeros((EXTRA - used, LANES), F32))
    place = sz.half_blocks * chans
    pack_ref[core, place : place + EXTRA] = jnp.concatenate(pieces, axis=0).astype(BF16)
    pack_ref[1 - core, place : place + EXTRA] = jnp.zeros((EXTRA, LANES), BF16)
    ship(0, place, EXTRA)
    ship(1, place, EXTRA)
    for copy in shipped:
        copy.wait()


def closing_kernel(sz, info, mine_ref, got_ref, close_ref, taps_got_ref, mean_ref, var_ref, *outs):
    (
        taps_ref,
        gain_ref,
        bias_ref,
        mix_h_ref,
        mix_h_bias_ref,
        mix_w_ref,
        mix_w_bias_ref,
        unite_ref,
        unite_b_ref,
        ln_gain_ref,
        ln_bias_ref,
        in_ref,
        b_in_ref,
        w_out_ref,
        b_out_ref,
        new_mean_ref,
        new_var_ref,
    ) = outs
    chans = sz.chans
    first_half = (info[1] & 1) == 0

    def take(half, row, rows):
        mine, got = mine_ref[row : row + rows], got_ref[row : row + rows]
        chosen = jnp.where(first_half, mine, got) if half == 0 else jnp.where(first_half, got, mine)
        return chosen.astype(F32)

    mean, var = mean_ref[...], var_ref[...]
    dz = jnp.zeros((1, sz.lanes), F32)
    dzx = jnp.zeros((1, sz.lanes), F32)
    for m in range(close_ref.shape[0]):
        block = close_ref[m]
        mean = 0.9 * mean + 0.1 * block[0:1, :chans]
        var = 0.9 * var + 0.1 * block[1:2, :chans]
        dz = dz + block[2:3]
        dzx = dzx + block[3:4]
    new_mean_ref[...] = mean
    new_var_ref[...] = var
    bias_ref[...] = dz[:, :chans]
    gain_ref[...] = dzx[:, :chans]
    for block in range(sz.hid_blocks):
        lanes = slice(block * LANES, (block + 1) * LANES)
        in_ref[:, lanes] = take(*sz.place(block), chans)
        w_out_ref[:, lanes] = take(*sz.place(sz.hid_blocks + block), chans)
    block = 2 * sz.hid_blocks
    parts = [[] for _ in range(3)]
    for part in range(3):
        for k in range(sz.full):
            parts[part].append(take(*sz.place(block), chans))
            block += 1
    if sz.rest:
        left = jnp.concatenate(
            [take(*sz.place(b), chans) for b in range(block, sz.blocks)], axis=1
        )
        for part in range(3):
            parts[part].append(left[:, part * sz.rest : (part + 1) * sz.rest])
    unite_ref[...] = jnp.concatenate([piece for part in parts for piece in part], axis=1)
    small = take(0, sz.half_blocks * chans, EXTRA)
    count = sz.lanes // LANES

    def joined(first, number, size):
        row = jnp.concatenate([small[first + k : first + k + 1] for k in range(number)], axis=1)
        return row[:, :size]

    unite_b_ref[...] = joined(0, count, chans)
    ln_gain_ref[...] = joined(count, count, chans)
    ln_bias_ref[...] = joined(2 * count, count, chans)
    b_out_ref[...] = joined(3 * count, count, chans)
    first = 4 * count
    b_in_ref[...] = joined(first, sz.hid_blocks, sz.hid)
    first += sz.hid_blocks
    mix_h_bias_ref[...] = small[first : first + 1, : sz.side]
    mix_w_bias_ref[...] = small[first + 1 : first + 2, : sz.side]
    first += 2
    for ref in (mix_h_ref, mix_w_ref):
        for i in range(sz.side):
            ref[i] = small[first + i : first + i + 1, : sz.side]
        first += sz.pad
    taps = taps_got_ref[0]
    for index in range(1, sz.n_dp):
        taps = taps + taps_got_ref[index]
    for p in range(3):
        for q in range(3):
            taps_ref[p, q] = taps[3 * p + q : 3 * p + q + 1, :chans]


def settings(cost):
    return {
        "compiler_params": pltpu.CompilerParams(vmem_limit_bytes=VMEM_BYTES),
        "cost_estimate": pl.CostEstimate(
            flops=0, bytes_accessed=int(cost * 3.0e6), transcendentals=0
        ),
    }


def run_whole(body, outs, info, flat, name, cost):
    def whole(item):
        return pl.BlockSpec(item.shape, lambda step, rank=len(item.shape): (0,) * rank)

    return pl.pallas_call(
        body,
        grid=(1,),
        out_shape=tuple(outs),
        in_specs=[pl.BlockSpec(memory_space=pltpu.SMEM)] + [whole(item) for item in flat],
        out_specs=tuple(whole(item) for item in outs),
        name=name,
        **settings(cost),
    )(info, *flat)


def run(body, outs, info, flat, name, cost, scratch=(), direct=0):
    layers = [item[0] if isinstance(item, tuple) else None for item in flat]
    args, spots, buffers = [], [], []

    def add(item):
        args.append(item)
        return len(args) - 1

    for item in flat:
        held = item[1] if isinstance(item, tuple) else (item,)
        spots.append(
            [tuple(add(one) for one in part) if isinstance(part, tuple) else add(part) for part in held]
        )
        buffers.append(pltpu.VMEM(held[0].shape, held[0].dtype))
    out_buffers = [pltpu.VMEM(item.shape, item.dtype) for item in outs[direct:]]

    def kernel(info_ref, *refs):
        sources, refs = refs[: len(args)], refs[len(args) :]
        targets, refs = refs[: len(outs)], refs[len(outs) :]
        ins_held, refs = refs[: len(buffers)], refs[len(buffers) :]
        outs_held, refs = refs[: len(out_buffers)], refs[len(out_buffers) :]
        in_sems, out_sems = refs[:2]
        picked = []
        for layer, spot in zip(layers, spots):
            found = [
                tuple(sources[one] for one in part) if isinstance(part, tuple) else sources[part]
                for part in spot
            ]
            picked.append(found[0] if layer is None else found)
        ins = Arrivals(
            picked, ins_held, in_sems, lambda layer: info_ref[1] ^ layer, info_ref[2], layers
        )
        held = (None,) * direct + tuple(outs_held)
        departures = Departures(targets, held, out_sems, direct)
        body(info_ref, ins, departures, *refs[2:])
        ins.close()
        departures.close()

    return pl.pallas_call(
        kernel,
        out_shape=tuple(outs),
        in_specs=[pl.BlockSpec(memory_space=pltpu.SMEM)]
        + [pl.BlockSpec(memory_space=pl.ANY) for _ in args],
        out_specs=tuple(pl.BlockSpec(memory_space=pl.ANY) for _ in outs),
        scratch_shapes=buffers
        + out_buffers
        + [pltpu.SemaphoreType.DMA((len(flat), 2)), pltpu.SemaphoreType.DMA((len(outs),))]
        + list(scratch),
        name=name,
        **settings(cost),
    )(info, *args)


def swap(block, axis, size, bit):
    return lax.ppermute(block, axis, [(i, i ^ bit) for i in range(size)])


def tie(first, second):
    first = tuple(first)
    return lax.optimization_barrier(first + tuple(second))[: len(first)]


def add_low(left, right):
    return (left.astype(F32) + right.astype(F32)).astype(BF16)


class Ring:
    def __init__(self, n_dp, n_pipe, dp, core):
        bits = [1 << k for k in range(n_dp.bit_length() - 1)]
        self.orders = (bits, bits[1:] + bits[:1])
        self.steps = len(bits)
        self.n_dp, self.n_pipe, self.dp, self.core = n_dp, n_pipe, dp, core

    def swap(self, block, step):
        route = []
        for d in range(self.n_dp):
            for p in range(self.n_pipe):
                there = d ^ self.orders[p & 1][step]
                route.append((d * self.n_pipe + p, there * self.n_pipe + p))
        return lax.ppermute(block, ("dp", "pipe"), route)

    def upper(self, step):
        bit = jnp.where(self.core == 0, self.orders[0][step], self.orders[1][step])
        return (self.dp & bit) != 0

    def halve(self, block, step):
        side = jnp.where(self.upper(step), 1, 0)
        parts = block.reshape((2, block.shape[0] // 2) + block.shape[1:])
        kept = lax.dynamic_index_in_dim(parts, side, 0, keepdims=False)
        sent = lax.dynamic_index_in_dim(parts, 1 - side, 0, keepdims=False)
        return add_low(kept, self.swap(sent, step))

    def double(self, block, step):
        got = self.swap(block, step)
        side = jnp.where(self.upper(step), 1, 0)
        rows = block.shape[0]
        whole = jnp.zeros((2 * rows,) + block.shape[1:], block.dtype)
        whole = lax.dynamic_update_slice_in_dim(whole, block, side * rows, 0)
        return lax.dynamic_update_slice_in_dim(whole, got, (1 - side) * rows, 0)


def shards(
    images,
    image_counts,
    conv_kernel,
    bn_gain,
    bn_bias,
    mix_h,
    mix_h_bias,
    mix_w,
    mix_w_bias,
    unite_w,
    unite_b,
    ln_gain,
    ln_bias,
    w_in,
    b_in,
    w_out,
    b_out,
    running_mean,
    running_var,
    cotangent,
):
    n_dp, n_pipe = lax.axis_size("dp"), lax.axis_size("pipe")
    dp, pipe = lax.axis_index("dp"), lax.axis_index("pipe")
    layers = n_pipe
    batch = images.shape[0] // n_pipe
    side, chans, hid = images.shape[1], images.shape[3], w_in.shape[2]
    sz = Sizes(batch, side, chans, hid, n_dp)
    core, plane = pipe & 1, pipe >> 1
    tokens = sz.tokens

    def shape(*dims, dtype=F32):
        return jax.ShapeDtypeStruct(dims, dtype)

    valid = jnp.clip(image_counts[0] - pipe * batch, 0, batch).astype(jnp.int32)
    info = jnp.stack([valid, pipe.astype(jnp.int32), (dp & 1).astype(jnp.int32)])

    def to_all(block):
        over = swap(block, "pipe", n_pipe, 2)
        return (block, swap(block, "pipe", n_pipe, 1), over, swap(over, "pipe", n_pipe, 1))

    first_taps = to_all(conv_kernel[0])
    own, own_half, small_own = run_whole(
        functools.partial(prepare_kernel, sz),
        (
            shape(chans, sz.weight_lanes, dtype=BF16),
            shape(chans // 2, sz.weight_lanes, dtype=BF16),
            shape(SMALL_ROWS, sz.lanes),
        ),
        info,
        (
            conv_kernel[0],
            bn_gain,
            bn_bias,
            mix_h[0],
            mix_h_bias,
            mix_w[0],
            mix_w_bias,
            unite_w[0].T,
            unite_b,
            ln_gain,
            ln_bias,
            w_in[0],
            b_in,
            w_out[0].T,
            b_out,
        ),
        "prepare",
        2,
    )
    beside = swap(own, "pipe", n_pipe, 1)

    def across_plane(block, cores):
        return lax.ppermute(block, "pipe", [(p, p ^ 2) for p in cores])

    def to_beside(block, cores):
        return lax.ppermute(block, "pipe", [(p, p ^ 1) for p in cores])

    def to_neighbour(block, cores):
        route = [
            (d * n_pipe + p, (d ^ 1) * n_pipe + p) for d in range(n_dp) for p in cores
        ]
        return lax.ppermute(block, ("dp", "pipe"), route)

    (half_sent,) = tie((own_half,), (first_taps[2],))
    first = across_plane(half_sent, (0, 2))

    def micro(array):
        block = lax.dynamic_slice_in_dim(array, pipe * batch, batch, 0)
        block = jnp.pad(block, ((0, 0), (0, 0), (0, sz.pad - side), (0, 0)))
        return block.reshape(tokens, chans)

    sums_shape = shape(n_dp, 8, LANES)
    plain = shape(tokens, chans)
    low = shape(tokens, chans, dtype=BF16)

    field = micro(images)
    conv, sums = run(
        functools.partial(start_kernel, sz),
        (plain, sums_shape),
        info,
        (field, (0, first_taps)),
        "start",
        2,
    )
    got = lax.all_to_all(sums, "dp", 0, 0)
    (small_own,) = tie((small_own,), (first,))
    smalls = to_all(small_own)
    (first,) = tie((first,), (sums,))
    first_beside, second = to_beside(first, (0, 2)), to_neighbour(first, (0, 2))
    (second,) = tie((second,), (got,))
    (half_late,) = tie((own_half,), (first_beside, smalls[2]))
    first_odd = across_plane(half_late, (1, 3))
    second_beside = to_beside(second, (0, 2))
    even = (own, beside, (first, second), (first_beside, second_beside))

    fields, convs, saved, stats, weights = [field], [conv], [], [], [even]
    for depth in range(layers):
        if depth:
            got = lax.all_to_all(sums, "dp", 0, 0)
        last = depth + 1 == layers
        outs = (
            low,
            shape(tokens, hid, dtype=BF16),
            shape(tokens, hid, dtype=BF16),
            plain,
            shape(tokens, 1),
            shape(tokens, 3 * sz.lanes, dtype=BF16),
            shape(8, sz.lanes),
        )
        flat = (got, convs[depth], (depth, smalls), (depth, weights[depth & 1]), fields[depth])
        if not last:
            outs += (plain, sums_shape)
            flat += ((depth + 1, smalls),)
        results = run(
            functools.partial(forward_kernel, sz, last),
            outs,
            info,
            flat,
            f"layer_{depth}_forward",
            6,
            scratch=[pltpu.SemaphoreType.DMA((2, -(-hid // HID_STEP)))],
        )
        fields.append(results[0])
        if depth == 0:
            (first_odd,) = tie((first_odd,), (second_beside,))
            first_odd_beside = to_beside(first_odd, (1, 3))
            second_odd = to_neighbour(first_odd, (1, 3))
            (second_odd,) = tie((second_odd,), (results[0],))
            second_odd_beside = to_beside(second_odd, (1, 3))
            weights.append(
                (own, beside, (first_odd, second_odd), (first_odd_beside, second_odd_beside))
            )
        saved.append(results[1:6])
        stats.append(results[6])
        if not last:
            convs.append(results[7])
            sums = results[8]

    def to_owners(parts):
        sent = [lax.select_n(pipe ^ bit, *parts) for bit in range(n_pipe)]
        return sent[:1] + [swap(sent[bit], "pipe", n_pipe, bit) for bit in range(1, n_pipe)]

    def collect(parts):
        whole = jnp.zeros((n_pipe, batch, side, side, chans), BF16)
        for bit, part in enumerate(parts):
            part = part.reshape(1, batch, side, sz.pad, chans)[:, :, :, :side]
            whole = lax.dynamic_update_slice(whole, part, (pipe ^ bit, 0, 0, 0, 0))
        return whole.reshape(1, n_pipe * batch, side, side, chans)

    half_shape = shape(sz.half_rows, LANES, dtype=BF16)
    halves, ends = [None] * layers, [None] * 2
    grads, closes = [None] * layers, [None] * layers
    behind = None
    for depth in reversed(range(layers)):
        outs = (half_shape, half_shape, plain, plain, sums_shape)
        if behind is None:
            front = (micro(cotangent),)
        else:
            front = behind
            outs += (low, shape(CLOSE_ROWS, sz.lanes))
        active, slope, unit, spread, joined = saved[depth]
        results = run(
            functools.partial(backward_kernel, sz, behind is None),
            outs,
            info,
            front
            + ((depth, smalls), (depth, weights[depth & 1]), slope, unit, spread, active)
            + (joined, stats[depth], convs[depth]),
            f"layer_{depth}_backward",
            12,
            scratch=[
                pltpu.VMEM((2,) + half_shape.shape, BF16),
                pltpu.VMEM((tokens, hid), BF16),
                pltpu.SemaphoreType.DMA((4,)),
            ],
            direct=2,
        )
        kept, sent, normed_grad, hidden_grad, sums = results[:5]
        if behind is not None:
            grads[depth + 1], closes[depth + 1] = results[5:]
        halves[depth] = add_low(kept, swap(sent, "pipe", n_pipe, 1))
        if depth == 0:
            (sums,) = tie((sums,), (ends[1],))
        if depth < 2:
            mine = jnp.where(plane == 0, halves[depth], halves[depth + 2])
            other = jnp.where(plane == 0, halves[depth + 2], halves[depth])
            ends[depth] = add_low(mine, swap(other, "pipe", n_pipe, 2))
        got = lax.all_to_all(sums, "dp", 0, 0)
        (got,) = tie((got,), (halves[depth],))
        behind = (
            got,
            stats[depth],
            (depth, smalls),
            normed_grad,
            convs[depth],
            hidden_grad,
            fields[depth],
        )
    ring = Ring(n_dp, n_pipe, dp, core)
    odd, even = ends[1], ends[0]
    odd = ring.halve(odd, 0)
    behind = tie(behind[:1], (odd,)) + behind[1:]
    grads[0], closes[0] = run(
        functools.partial(finish_kernel, sz),
        (low, shape(CLOSE_ROWS, sz.lanes)),
        info,
        behind,
        "finish",
        4,
    )
    for step in range(1, ring.steps):
        odd = ring.halve(odd, step)
    even = ring.halve(even, 0)
    (closed,) = tie((jnp.stack(closes),), (odd, even))
    closing = lax.all_to_all(closed, "pipe", 0, 0)
    tied = tie(tuple(fields[1:]) + tuple(grads), (even,))
    output_parts, grad_parts = to_owners(tied[:layers]), to_owners(tied[layers:])
    for step in range(1, ring.steps):
        odd, even = tie((odd, even), () if step == 1 else (closing,))
        odd = ring.double(odd, ring.steps - step)
        even = ring.halve(even, step)
    taps = jnp.sum(closing[:, 4:13], axis=0)
    taps = lax.all_to_all(jnp.broadcast_to(taps[None], (n_dp,) + taps.shape), "dp", 0, 0)
    layer_outputs, input_grads = collect(output_parts), collect(grad_parts)
    odd, even = tie((odd, even), ())
    odd = ring.double(odd, 0)
    for step in reversed(range(ring.steps)):
        even = ring.double(even, step)
        if step == ring.steps - 1:
            odd, even = tie((odd, even), (taps, layer_outputs))
        if step == 1:
            (even,) = tie((even,), (input_grads,))
    parts = [odd, even]
    mine = jnp.where(core == 0, parts[1], parts[0])
    other = jnp.where(core == 0, parts[0], parts[1])
    got = swap(other, "pipe", n_pipe, 1)
    row = shape(1, chans)
    outs = (
        shape(3, 3, 1, chans),
        row,
        row,
        shape(side, 1, side),
        shape(1, side),
        shape(side, 1, side),
        shape(1, side),
        shape(chans, 3 * chans),
        row,
        row,
        row,
        shape(chans, hid),
        shape(1, hid),
        shape(chans, hid),
        row,
        row,
        row,
    )
    finished = list(
        run_whole(
            functools.partial(closing_kernel, sz),
            outs,
            info,
            (mine, got, closing, taps, running_mean, running_var),
            "closing",
            4,
        )
    )
    finished[0] = jnp.transpose(finished[0], (2, 0, 1, 3))
    for k in (3, 5):
        finished[k] = jnp.transpose(finished[k], (1, 0, 2))
    for k in (7, 13):
        finished[k] = finished[k].T[None]
    finished[11] = finished[11][None]
    return (layer_outputs, input_grads) + tuple(finished)


def solution(mesh):
    four = P("pipe", None, None, None)
    three = P("pipe", None, None)
    two = P("pipe", None)
    images = P("dp", None, None, None)
    in_specs = (
        images, P("dp"), four, two, two, three, two, three, two, three, two, two, two,
        three, two, three, two, two, two, images,
    )
    stacked = P("pipe", "dp", None, None, None)
    out_specs = (
        stacked, stacked, four, two, two, three, two, three, two, three, two, two, two,
        three, two, three, two, two, two,
    )
    return jax.shard_map(
        shards, mesh=mesh, in_specs=in_specs, out_specs=out_specs, check_vma=False
    )
```

```python
import functools

import jax
import jax.numpy as jnp
from jax import lax
from jax.experimental import pallas as pl
from jax.experimental.pallas import tpu as pltpu
from jax.sharding import PartitionSpec as P

F32 = jnp.float32
BF16 = jnp.bfloat16
LANES = 128
HID_STEP = 256
ROW_STEP = 64
LN_STEP = 32
VMEM_BYTES = 58 * 1024 * 1024
EXTRA = 128
ROW_BN_GAIN, ROW_BN_BIAS, ROW_UNITE_B, ROW_LN_GAIN, ROW_LN_BIAS, ROW_B_OUT = range(9, 15)
ROW_MIX_BIAS, ROW_B_IN, ROW_MIX = 15, 16, 24
SMALL_ROWS = 40
CLOSE_ROWS = 16
GRAD_ROWS = 64


def wide(value):
    return -(-value // LANES) * LANES


def tall(value):
    return -(-value // 16) * 16


def dot(left, right):
    return lax.dot_general(left, right, (((1,), (0,)), ((), ())), preferred_element_type=F32)


def dot_nt(left, right):
    return lax.dot_general(left, right, (((1,), (1,)), ((), ())), preferred_element_type=F32)


def dot_exact(left, right):
    return lax.dot_general(
        left,
        right,
        (((1,), (0,)), ((), ())),
        preferred_element_type=F32,
        precision=lax.Precision.HIGHEST,
    )


class Sizes:
    def __init__(self, batch, side, chans, hid, n_dp):
        self.batch, self.side, self.chans, self.hid, self.n_dp = batch, side, chans, hid, n_dp
        self.pad = tall(side)
        self.image = side * self.pad
        self.tokens = batch * self.image
        self.lanes = wide(chans)
        self.full = chans // LANES
        self.rest = chans - self.full * LANES
        self.hid_blocks = hid // LANES
        left_blocks = -(-3 * self.rest // LANES)
        self.unite_blocks = 3 * self.full + left_blocks
        self.blocks = 2 * self.hid_blocks + self.unite_blocks
        self.half_blocks = self.blocks // 2
        self.half_rows = self.half_blocks * chans + EXTRA
        self.weight_lanes = 2 * hid + 3 * self.lanes

    def place(self, block):
        half, place = divmod(block, self.half_blocks)
        return half, place * self.chans

    def unite(self, part):
        first = 2 * self.hid + part * self.lanes
        return slice(first, first + self.chans)


def token_mask(sz, valid):
    row = lax.broadcasted_iota(jnp.int32, (sz.tokens, 1), 0)
    return ((row < valid * sz.image) & (row % sz.pad < sz.side)).astype(F32)


def taps_of(sz, small):
    return [small[k : k + 1, : sz.chans] for k in range(9)]


def row_of(sz, small, index):
    return small[index : index + 1, : sz.chans]


def fill_lanes(sz, row):
    if sz.lanes == sz.chans:
        return row
    return jnp.concatenate([row, jnp.zeros((1, sz.lanes - sz.chans), F32)], axis=1)


def lane_rows(sz, row):
    row = fill_lanes(sz, row)
    return [row[:, k * LANES : (k + 1) * LANES] for k in range(sz.lanes // LANES)]


def put_sums(sz, ref, first, second, number):
    pieces = lane_rows(sz, first) + lane_rows(sz, second)
    pieces.append(jnp.zeros((1, LANES), F32) + number)
    pieces.append(jnp.zeros((8 - len(pieces), LANES), F32))
    block = jnp.concatenate(pieces, axis=0)
    for index in range(sz.n_dp):
        ref[index] = block


def take_sums(sz, ref):
    total = ref[0]
    for index in range(1, sz.n_dp):
        total = total + ref[index]
    count = sz.lanes // LANES
    first = jnp.concatenate([total[k : k + 1] for k in range(count)], axis=1)
    second = jnp.concatenate([total[count + k : count + k + 1] for k in range(count)], axis=1)
    return first[:, : sz.chans], second[:, : sz.chans], total[2 * count : 2 * count + 1, 0:1]


def sum_rows(value):
    return jnp.sum(value, axis=0, keepdims=True)


def mean_lanes(value):
    return jnp.mean(value, axis=1, keepdims=True)


def pick_rows(sz):
    row = lax.broadcasted_iota(jnp.int32, (sz.image, sz.pad), 0)
    col = lax.broadcasted_iota(jnp.int32, (sz.image, sz.pad), 1)
    return (row // sz.pad == col), (row % sz.pad == col)


def same_masks(sz):
    row = lax.broadcasted_iota(jnp.int32, (sz.image, sz.image), 0)
    col = lax.broadcasted_iota(jnp.int32, (sz.image, sz.image), 1)
    return (row % sz.pad == col % sz.pad), (row // sz.pad == col // sz.pad)


def mixers(sz, small, turned):
    pick_i, pick_j = pick_rows(sz)
    same_j, same_i = same_masks(sz)
    product = dot_nt if turned else dot
    found = []
    for pick, same, lane in ((pick_i, same_j, 0), (pick_j, same_i, LANES)):
        mix = small[ROW_MIX : ROW_MIX + sz.pad, lane : lane + sz.pad].astype(BF16)
        pick = pick.astype(BF16)
        spread = dot_nt(product(pick, mix).astype(BF16), pick)
        found.append(jnp.where(same, spread, 0.0).astype(BF16))
    return found


class Arrivals:
    def __init__(self, sources, buffers, sems, role_of, bit, layers):
        self.buffers, self.copies = buffers, []
        for k, (source, buffer) in enumerate(zip(sources, buffers)):
            if layers[k] is None:
                copies = [pltpu.make_async_copy(source, buffer, sems.at[k, 0])]
                copies[0].start()
            else:
                halved = isinstance(source[-1], tuple)
                rows = buffer.shape[0] // 2 if halved else buffer.shape[0]
                spots = [pl.ds(0, rows), pl.ds(rows, rows)] if halved else [pl.ds(0, rows)]
                copies = [
                    pltpu.make_async_copy(source[0].at[spot], buffer.at[spot], sems.at[k, h])
                    for h, spot in enumerate(spots)
                ]
                for place, held in enumerate(source):

                    @pl.when(role_of(layers[k]) == place)
                    def _(held=held, buffer=buffer, k=k, spots=spots, rows=rows):
                        for h, spot in enumerate(spots):
                            if isinstance(held, tuple):
                                piece = held[h]
                                at = h ^ bit
                                spot = pl.ds(pl.multiple_of(at * rows, 16), rows)
                            else:
                                piece = held.at[spot]
                            pltpu.make_async_copy(piece, buffer.at[spot], sems.at[k, h]).start()

            self.copies.append(copies)

    def __getitem__(self, k):
        if self.copies[k] is not None:
            for copy in self.copies[k]:
                copy.wait()
            self.copies[k] = None
        return self.buffers[k]

    def close(self):
        for k in range(len(self.copies)):
            self[k]


class Departures:
    def __init__(self, targets, buffers, sems, direct):
        self.buffers, self.targets = buffers, targets
        self.copies = [
            None if k < direct else pltpu.make_async_copy(buffer, target, sems.at[k])
            for k, (target, buffer) in enumerate(zip(targets, buffers))
        ]
        self.started, self.parts = [False] * len(self.copies), []

    def put(self, k, value):
        self.buffers[k][...] = value
        self.send(k)

    def send(self, k):
        self.copies[k].start()
        self.started[k] = True

    def send_part(self, k, lanes, sem):
        spot = (slice(None), lanes)
        copy = pltpu.make_async_copy(self.buffers[k].at[spot], self.targets[k].at[spot], sem)
        copy.start()
        self.parts.append(copy)

    def close(self):
        for copy, started in zip(self.copies, self.started):
            if started:
                copy.wait()
        for copy in self.parts:
            copy.wait()


def prepare_kernel(
    sz,
    info,
    taps_ref,
    bn_gain_ref,
    bn_bias_ref,
    mix_h_ref,
    mix_h_bias_ref,
    mix_w_ref,
    mix_w_bias_ref,
    unite_ref,
    unite_b_ref,
    ln_gain_ref,
    ln_bias_ref,
    in_ref,
    b_in_ref,
    w_out_ref,
    b_out_ref,
    weights_ref,
    half_ref,
    small_ref,
):
    chans, hid = sz.chans, sz.hid
    weights_ref[:, :hid] = in_ref[...]
    weights_ref[:, hid : 2 * hid] = w_out_ref[...]
    gap = jnp.zeros((chans, sz.lanes - chans), BF16)
    for part in range(3):
        first = 2 * hid + part * sz.lanes
        weights_ref[:, first : first + sz.lanes] = jnp.concatenate(
            [unite_ref[:, part * chans : (part + 1) * chans], gap], axis=1
        )
    rows = half_ref.shape[0]
    half_ref[...] = weights_ref[pl.ds(pl.multiple_of(info[2] * rows, 16), rows)]
    small_ref[...] = jnp.zeros(small_ref.shape, F32)
    for p in range(3):
        small_ref[3 * p : 3 * p + 3, :chans] = taps_ref[p].astype(F32)
    rows = (bn_gain_ref, bn_bias_ref, unite_b_ref, ln_gain_ref, ln_bias_ref, b_out_ref)
    for place, ref in zip(range(ROW_BN_GAIN, ROW_MIX_BIAS), rows):
        small_ref[place : place + 1, :chans] = ref[...]
    place = ROW_MIX_BIAS
    small_ref[place : place + 1, : sz.side] = mix_h_bias_ref[...]
    small_ref[place : place + 1, LANES : LANES + sz.side] = mix_w_bias_ref[...]
    for k, lane in enumerate(range(0, hid, sz.lanes)):
        wide_part = min(sz.lanes, hid - lane)
        small_ref[ROW_B_IN + k : ROW_B_IN + k + 1, :wide_part] = b_in_ref[
            :, lane : lane + wide_part
        ]
    rows = slice(ROW_MIX, ROW_MIX + sz.side)
    small_ref[rows, : sz.side] = mix_h_ref[...].astype(F32)
    small_ref[rows, LANES : LANES + sz.side] = mix_w_ref[...].astype(F32)


def steps(size, step):
    return [slice(first, min(first + step, size)) for first in range(0, size, step)]


def fold(value):
    total = value[:8]
    for first in range(8, value.shape[0], 8):
        total = total + value[first : first + 8]
    return total


def conv_rows(sz, rows, taps, back=False):
    order = (2, 1, 0) if back else (0, 1, 2)
    parts = []
    for row in rows:
        near = (pltpu.roll(row, 1, 0), row, pltpu.roll(row, sz.pad - 1, 0))
        near = [near[q] for q in order]
        parts.append(
            [taps[3 * p] * near[0] + taps[3 * p + 1] * near[1] + taps[3 * p + 2] * near[2] for p in order]
        )
    found = []
    for i in range(len(rows)):
        total = parts[i][1]
        if i > 0:
            total = total + parts[i - 1][0]
        if i + 1 < len(rows):
            total = total + parts[i + 1][2]
        found.append(total)
    return found


def next_conv(sz, rows, taps, masks, conv_ref, sums_ref, number):
    first = jnp.zeros((8, sz.chans), F32)
    second = jnp.zeros((8, sz.chans), F32)
    for n in range(sz.batch):
        part = range(n * sz.side, (n + 1) * sz.side)
        for i, conv in zip(part, conv_rows(sz, [rows[i] for i in part], taps)):
            conv_ref[i * sz.pad : (i + 1) * sz.pad] = conv
            masked = masks[i] * conv
            first = first + fold(masked)
            second = second + fold(masked * conv)
    put_sums(sz, sums_ref, sum_rows(first), sum_rows(second), number)


def row_masks(sz, valid):
    mask = token_mask(sz, valid)
    return [mask[i : i + sz.pad] for i in range(0, sz.tokens, sz.pad)]


def start_kernel(sz, info, ins, outs):
    field = ins[0]
    kernel = ins[1]
    taps = [kernel[p, q : q + 1].astype(F32) for p in range(3) for q in range(3)]
    rows = [field[i : i + sz.pad].astype(F32) for i in range(0, sz.tokens, sz.pad)]
    number = (info[0] * (sz.side * sz.side)).astype(F32)
    masks = row_masks(sz, info[0])
    next_conv(sz, rows, taps, masks, outs.buffers[0], outs.buffers[1], number)
    outs.send(0)
    outs.send(1)


def forward_kernel(sz, last, info, ins, outs, part_sems):
    GOT, CONV, SMALL, WEIGHTS, FIELD = range(5)
    OUT, ACTIVE, SLOPE, UNIT, SPREAD, JOINED, STAT, CONV_NEXT, SUMS = range(9)
    small = ins[SMALL]
    total, square, count = take_sums(sz, ins[GOT])
    center = total / count
    variance = square / count - center * center
    inverse = lax.rsqrt(variance + 1e-05)
    stat = [
        fill_lanes(sz, center),
        fill_lanes(sz, inverse),
        fill_lanes(sz, variance * count / (count - 1.0)),
        jnp.zeros((1, sz.lanes), F32) + count,
        jnp.zeros((4, sz.lanes), F32),
    ]
    outs.put(STAT, jnp.concatenate(stat, axis=0))
    gain = inverse * row_of(sz, small, ROW_BN_GAIN)
    shift = row_of(sz, small, ROW_BN_BIAS)
    conv, joined = ins[CONV], outs.buffers[JOINED]
    chans, lanes = sz.chans, sz.lanes
    for rows in steps(sz.tokens, ROW_STEP):
        normed = ((conv[rows] - center) * gain + shift).astype(BF16)
        gap = jnp.zeros((normed.shape[0], lanes - chans), BF16)
        joined[rows, :lanes] = jnp.concatenate([normed, gap], axis=1)
    mix_h, mix_w = mixers(sz, small, False)
    pick_i, pick_j = pick_rows(sz)
    bias = small[ROW_MIX_BIAS : ROW_MIX_BIAS + 1]
    bias_h = jnp.sum(jnp.where(pick_i, bias[:, : sz.pad], 0.0), axis=1, keepdims=True)
    bias_w = jnp.sum(
        jnp.where(pick_j, bias[:, LANES : LANES + sz.pad], 0.0), axis=1, keepdims=True
    )
    for n in range(sz.batch):
        normed = joined[n * sz.image : (n + 1) * sz.image, :lanes]
        for mix, add, place in ((mix_h, bias_h, 1), (mix_w, bias_w, 2)):
            mixed = dot(mix, normed)
            for rows in steps(sz.image, ROW_STEP):
                there = slice(n * sz.image + rows.start, n * sz.image + rows.stop)
                joined[there, place * lanes : (place + 1) * lanes] = (
                    mixed[rows] + add[rows]
                ).astype(BF16)
    outs.send(JOINED)
    weights_ref = ins[WEIGHTS]
    field = ins[FIELD]
    united = dot_nt(joined[...], weights_ref[:, 2 * sz.hid :])
    unite_b = row_of(sz, small, ROW_UNITE_B)
    ln_gain, ln_bias = row_of(sz, small, ROW_LN_GAIN), row_of(sz, small, ROW_LN_BIAS)
    hidden, lnormed = [], []
    for rows in steps(sz.tokens, LN_STEP):
        part = field[rows].astype(F32) + (united[rows] + unite_b)
        offset = part - mean_lanes(part)
        spread = lax.rsqrt(mean_lanes(offset * offset) + 1e-06)
        unit = offset * spread
        outs.buffers[UNIT][rows] = unit
        outs.buffers[SPREAD][rows] = spread
        hidden.append(part)
        lnormed.append((unit * ln_gain + ln_bias).astype(BF16))
    hidden = jnp.concatenate(hidden, axis=0)
    lnormed = jnp.concatenate(lnormed, axis=0)
    outs.send(UNIT)
    outs.send(SPREAD)
    lanes_in = [small[ROW_B_IN + k : ROW_B_IN + k + 1] for k in range(-(-sz.hid // lanes))]
    b_in = jnp.concatenate(lanes_in, axis=1)
    root = 0.7978845608028654
    cubic = 0.044715
    for part in steps(sz.hid, HID_STEP):
        product = dot(lnormed, weights_ref[:, part])
        for rows in steps(sz.tokens, ROW_STEP):
            before = product[rows] + b_in[:, part]
            squared = before * before
            bent = jnp.tanh(before * (root + (root * cubic) * squared))
            half = 0.5 + 0.5 * bent
            active = before * half
            slope = half + (active * (1.0 - bent)) * (root + (3.0 * root * cubic) * squared)
            outs.buffers[ACTIVE][rows, part] = active.astype(BF16)
            outs.buffers[SLOPE][rows, part] = slope.astype(BF16)
        index = part.start // HID_STEP
        outs.send_part(ACTIVE, part, part_sems.at[0, index])
        outs.send_part(SLOPE, part, part_sems.at[1, index])
    branch = dot_nt(outs.buffers[ACTIVE][...], weights_ref[:, sz.hid : 2 * sz.hid])
    masks = row_masks(sz, info[0])
    b_out = row_of(sz, small, ROW_B_OUT)
    results = []
    for i, mask in enumerate(masks):
        rows = slice(i * sz.pad, (i + 1) * sz.pad)
        result = (mask * (hidden[rows] + (branch[rows] + b_out))).astype(BF16)
        outs.buffers[OUT][rows] = result
        results.append(result.astype(F32))
    outs.send(OUT)
    if not last:
        number = (info[0] * (sz.side * sz.side)).astype(F32)
        taps = taps_of(sz, ins[5])
        next_conv(
            sz, results, taps, masks, outs.buffers[CONV_NEXT], outs.buffers[SUMS], number
        )
        outs.send(SUMS)
        outs.send(CONV_NEXT)


def finish_layer(sz, info, ins, outs, first_out):
    GOT, STAT, SMALL, NORMED_GRAD, CONV, HIDDEN_GRAD, FIELD = range(7)
    small, stat = ins[SMALL], ins[STAT]
    chans = sz.chans
    taps = taps_of(sz, small)
    sum_dz, sum_dzx, _ = take_sums(sz, ins[GOT])
    count = stat[3:4, 0:1]
    center, inverse = stat[0:1, :chans], stat[1:2, :chans]
    scale = inverse * row_of(sz, small, ROW_BN_GAIN)
    mean_dz, mean_dzx = sum_dz / count, inverse * (sum_dzx / count)
    normed_grad, conv, hidden_grad, field = (
        ins[k] for k in (NORMED_GRAD, CONV, HIDDEN_GRAD, FIELD)
    )
    masks = row_masks(sz, info[0])
    sums = [jnp.zeros((8, chans), F32) for _ in range(9)]
    grads = []
    for n in range(sz.batch):
        spots = [
            slice(i * sz.pad, (i + 1) * sz.pad) for i in range(n * sz.side, (n + 1) * sz.side)
        ]
        conv_grads = [
            (masks[n * sz.side + i] * scale)
            * (normed_grad[rows] - mean_dz - (conv[rows] - center) * mean_dzx)
            for i, rows in enumerate(spots)
        ]
        for rows, back in zip(spots, conv_rows(sz, conv_grads, taps, back=True)):
            grad = (hidden_grad[rows] + back).astype(BF16)
            outs.buffers[first_out][rows] = grad
            grads.append(grad)
        for i, rows in enumerate(spots):
            row = field[rows].astype(F32)
            near = (pltpu.roll(row, 1, 0), row, pltpu.roll(row, sz.pad - 1, 0))
            for p in range(3):
                there = i + 1 - p
                if 0 <= there < sz.side:
                    for q in range(3):
                        sums[3 * p + q] = sums[3 * p + q] + fold(conv_grads[there] * near[q])
    outs.send(first_out)
    pieces = [center, stat[2:3, :chans], sum_dz, sum_dzx] + [sum_rows(item) for item in sums]
    block = [fill_lanes(sz, piece) for piece in pieces]
    block.append(jnp.zeros((CLOSE_ROWS - len(pieces), sz.lanes), F32))
    outs.put(first_out + 1, jnp.concatenate(block, axis=0))
    return grads


def finish_kernel(sz, info, ins, outs):
    finish_layer(sz, info, ins, outs, 0)


def backward_kernel(sz, first, info, ins, outs, pack_ref, before_ref, pack_sems):
    base = 1 if first else 7
    SMALL, WEIGHTS, SLOPE, UNIT, SPREAD, ACTIVE, JOINED, STAT, CONV = range(base, base + 9)
    core = info[1] & 1
    chans, tokens, lanes = sz.chans, sz.tokens, sz.lanes
    shipped = []

    def put(block, value):
        half, row = sz.place(block)
        pack_ref[half ^ core, row : row + chans] = value

    def ship(half, first_row, rows):
        spot, sem = pl.ds(first_row, rows), pack_sems.at[len(shipped)]
        for place in range(2):

            @pl.when(half ^ core == place)
            def _(place=place):
                pltpu.make_async_copy(
                    pack_ref.at[place, spot], outs.targets[place].at[spot], sem
                ).start()

        shipped.append(
            pltpu.make_async_copy(pack_ref.at[0, spot], outs.targets[0].at[spot], sem)
        )

    if first:
        upstream = [ins[0][i : i + sz.pad] for i in range(0, tokens, sz.pad)]
    else:
        upstream = finish_layer(sz, info, ins, outs, 5)
    small = ins[SMALL]
    masks = row_masks(sz, info[0])
    out_grads = [mask * grad.astype(F32) for mask, grad in zip(masks, upstream)]
    branch_grad = jnp.concatenate([item.astype(BF16) for item in out_grads], axis=0)
    out_sum = fold(out_grads[0])
    for item in out_grads[1:]:
        out_sum = out_sum + fold(item)
    out_grads = jnp.concatenate(out_grads, axis=0)
    unit = ins[UNIT]
    ln_gain, ln_bias = row_of(sz, small, ROW_LN_GAIN), row_of(sz, small, ROW_LN_BIAS)
    lnormed = [
        (unit[rows] * ln_gain + ln_bias).astype(BF16) for rows in steps(tokens, ROW_STEP)
    ]
    lnormed = jnp.concatenate(lnormed, axis=0)
    turned_ln = jnp.concatenate([lnormed.T, jnp.ones((16, tokens), BF16)], axis=0)
    turned_branch = branch_grad.T
    weights_ref, slope_ref, active_ref = ins[WEIGHTS], ins[SLOPE], ins[ACTIVE]
    in_pieces = []
    for k in range(0, sz.hid, HID_STEP):
        part = slice(k, k + HID_STEP)
        active_grad = dot(branch_grad, weights_ref[:, sz.hid + k : sz.hid + k + HID_STEP])
        for rows in steps(tokens, ROW_STEP):
            before_ref[rows, part] = (
                active_grad[rows] * slope_ref[rows, part].astype(F32)
            ).astype(BF16)
        grad_in = dot(turned_ln, before_ref[:, part])
        grad_out = dot(turned_branch, active_ref[:, part])
        for lane in range(0, HID_STEP, LANES):
            block = (k + lane) // LANES
            put(block, grad_in[:chans, lane : lane + LANES].astype(BF16))
            put(sz.hid_blocks + block, grad_out[:, lane : lane + LANES].astype(BF16))
            in_pieces.append(grad_in[chans : chans + 1, lane : lane + LANES])
    norm_grad = dot_nt(before_ref[...], weights_ref[:, : sz.hid])
    ship(0, 0, sz.half_blocks * chans)
    spread = ins[SPREAD]
    token_grad = []
    token_sum, gain_sum, bias_sum = (jnp.zeros((8, chans), F32) for _ in range(3))
    for rows in steps(tokens, LN_STEP):
        grad, part = norm_grad[rows], unit[rows]
        product = grad * part
        gain_sum = gain_sum + fold(product)
        bias_sum = bias_sum + fold(grad)
        scaled = grad * ln_gain
        hidden_grad = out_grads[rows] + spread[rows] * (
            scaled - mean_lanes(scaled) - part * mean_lanes(product * ln_gain)
        )
        outs.buffers[3][rows] = hidden_grad
        token = hidden_grad.astype(BF16)
        token_grad.append(token)
        token_sum = token_sum + fold(token.astype(F32))
    token_grad = jnp.concatenate(token_grad, axis=0)
    outs.send(3)
    joined = ins[JOINED]
    joined_grad = dot(token_grad, weights_ref[:, 2 * sz.hid :])
    rows_grad = joined_grad[:, lanes : lanes + chans].astype(BF16)
    cols_grad = joined_grad[:, 2 * lanes : 2 * lanes + chans].astype(BF16)
    turned_h, turned_w = mixers(sz, small, True)
    stat, conv = ins[STAT], ins[CONV]
    center, inverse = stat[0:1, :chans], stat[1:2, :chans]
    sum_dz, sum_dzx = (jnp.zeros((8, chans), F32) for _ in range(2))
    for n in range(sz.batch):
        image = slice(n * sz.image, (n + 1) * sz.image)
        back_h = dot(turned_h, rows_grad[image])
        back_w = dot(turned_w, cols_grad[image])
        for rows in steps(sz.image, ROW_STEP):
            there = slice(image.start + rows.start, image.start + rows.stop)
            normed_grad = joined_grad[there, :chans] + (back_h[rows] + back_w[rows])
            outs.buffers[2][there] = normed_grad
            sum_dz = sum_dz + fold(normed_grad)
            sum_dzx = sum_dzx + fold(normed_grad * ((conv[there] - center) * inverse))
    put_sums(sz, outs.buffers[4], sum_rows(sum_dz), sum_rows(sum_dzx), 0.0)
    outs.send(4)
    outs.send(2)
    grad_unite = dot(token_grad.T, joined[...]).astype(BF16)
    block = 2 * sz.hid_blocks
    leftovers = []
    for part in range(3):
        for k in range(sz.full):
            lane = part * lanes + k * LANES
            put(block, grad_unite[:, lane : lane + LANES])
            block += 1
        if sz.rest:
            lane = part * lanes + sz.full * LANES
            leftovers.append(grad_unite[:, lane : lane + sz.rest])
    if sz.rest:
        left = jnp.concatenate(leftovers, axis=1)
        fill = wide(left.shape[1]) - left.shape[1]
        if fill:
            left = jnp.concatenate([left, jnp.zeros((chans, fill), BF16)], axis=1)
        for lane in range(0, left.shape[1], LANES):
            put(block, left[:, lane : lane + LANES])
            block += 1
    ship(1, 0, sz.half_blocks * chans)
    pick_i, pick_j = pick_rows(sz)
    same_j, same_i = same_masks(sz)
    mix_pieces, bias_pieces = [], []
    for grads, pick, same in ((rows_grad, pick_i, same_j), (cols_grad, pick_j, same_i)):
        pairs = jnp.zeros((sz.image, sz.image), F32)
        sums = jnp.zeros((sz.image, 1), F32)
        for n in range(sz.batch):
            image = slice(n * sz.image, (n + 1) * sz.image)
            pairs = pairs + dot_nt(grads[image], joined[image, :chans])
            sums = sums + jnp.sum(grads[image].astype(F32), axis=1, keepdims=True)
        pairs = jnp.where(same, pairs, 0.0)
        picked = pick.astype(F32)
        groups = [pairs[i : i + sz.pad] for i in range(0, sz.image, sz.pad)]
        if pick is pick_i:
            near = [sum_rows(group) for group in groups]
            near.append(jnp.zeros((sz.pad - sz.side, sz.image), F32))
            near = jnp.concatenate(near, axis=0)
        else:
            near = groups[0]
            for group in groups[1:]:
                near = near + group
        small_grad = dot_exact(near, picked)
        gap = LANES - sz.pad
        mix_pieces.append(
            jnp.concatenate([small_grad, jnp.zeros((sz.pad, gap), F32)], axis=1)
        )
        bias_pieces.append(
            jnp.concatenate([sum_rows(picked * sums), jnp.zeros((1, gap), F32)], axis=1)
        )
    pieces = (
        lane_rows(sz, sum_rows(token_sum))
        + lane_rows(sz, sum_rows(gain_sum))
        + lane_rows(sz, sum_rows(bias_sum))
        + lane_rows(sz, sum_rows(out_sum))
        + in_pieces
        + bias_pieces
        + mix_pieces
    )
    used = sum(piece.shape[0] for piece in pieces)
    pieces.append(jnp.zeros((EXTRA - used, LANES), F32))
    place = sz.half_blocks * chans
    pack_ref[core, place : place + EXTRA] = jnp.concatenate(pieces, axis=0).astype(BF16)
    pack_ref[1 - core, place : place + EXTRA] = jnp.zeros((EXTRA, LANES), BF16)
    ship(0, place, EXTRA)
    ship(1, place, EXTRA)
    for copy in shipped:
        copy.wait()


def closing_kernel(sz, info, mine_ref, got_ref, close_ref, taps_got_ref, mean_ref, var_ref, *outs):
    (
        taps_ref,
        gain_ref,
        bias_ref,
        mix_h_ref,
        mix_h_bias_ref,
        mix_w_ref,
        mix_w_bias_ref,
        unite_ref,
        unite_b_ref,
        ln_gain_ref,
        ln_bias_ref,
        in_ref,
        b_in_ref,
        w_out_ref,
        b_out_ref,
        new_mean_ref,
        new_var_ref,
    ) = outs
    chans = sz.chans
    first_half = (info[1] & 1) == 0

    def take(half, row, rows):
        mine, got = mine_ref[row : row + rows], got_ref[row : row + rows]
        chosen = jnp.where(first_half, mine, got) if half == 0 else jnp.where(first_half, got, mine)
        return chosen.astype(F32)

    mean, var = mean_ref[...], var_ref[...]
    dz = jnp.zeros((1, sz.lanes), F32)
    dzx = jnp.zeros((1, sz.lanes), F32)
    for m in range(close_ref.shape[0]):
        block = close_ref[m]
        mean = 0.9 * mean + 0.1 * block[0:1, :chans]
        var = 0.9 * var + 0.1 * block[1:2, :chans]
        dz = dz + block[2:3]
        dzx = dzx + block[3:4]
    new_mean_ref[...] = mean
    new_var_ref[...] = var
    bias_ref[...] = dz[:, :chans]
    gain_ref[...] = dzx[:, :chans]
    for block in range(sz.hid_blocks):
        lanes = slice(block * LANES, (block + 1) * LANES)
        in_ref[:, lanes] = take(*sz.place(block), chans)
        w_out_ref[:, lanes] = take(*sz.place(sz.hid_blocks + block), chans)
    block = 2 * sz.hid_blocks
    parts = [[] for _ in range(3)]
    for part in range(3):
        for k in range(sz.full):
            parts[part].append(take(*sz.place(block), chans))
            block += 1
    if sz.rest:
        left = jnp.concatenate(
            [take(*sz.place(b), chans) for b in range(block, sz.blocks)], axis=1
        )
        for part in range(3):
            parts[part].append(left[:, part * sz.rest : (part + 1) * sz.rest])
    unite_ref[...] = jnp.concatenate([piece for part in parts for piece in part], axis=1)
    small = take(0, sz.half_blocks * chans, EXTRA)
    count = sz.lanes // LANES

    def joined(first, number, size):
        row = jnp.concatenate([small[first + k : first + k + 1] for k in range(number)], axis=1)
        return row[:, :size]

    unite_b_ref[...] = joined(0, count, chans)
    ln_gain_ref[...] = joined(count, count, chans)
    ln_bias_ref[...] = joined(2 * count, count, chans)
    b_out_ref[...] = joined(3 * count, count, chans)
    first = 4 * count
    b_in_ref[...] = joined(first, sz.hid_blocks, sz.hid)
    first += sz.hid_blocks
    mix_h_bias_ref[...] = small[first : first + 1, : sz.side]
    mix_w_bias_ref[...] = small[first + 1 : first + 2, : sz.side]
    first += 2
    for ref in (mix_h_ref, mix_w_ref):
        for i in range(sz.side):
            ref[i] = small[first + i : first + i + 1, : sz.side]
        first += sz.pad
    taps = taps_got_ref[0]
    for index in range(1, sz.n_dp):
        taps = taps + taps_got_ref[index]
    for p in range(3):
        for q in range(3):
            taps_ref[p, q] = taps[3 * p + q : 3 * p + q + 1, :chans]


def settings(cost):
    return {
        "compiler_params": pltpu.CompilerParams(vmem_limit_bytes=VMEM_BYTES),
        "cost_estimate": pl.CostEstimate(
            flops=0, bytes_accessed=int(cost * 3.0e6), transcendentals=0
        ),
    }


def run_whole(body, outs, info, flat, name, cost):
    def whole(item):
        return pl.BlockSpec(item.shape, lambda step, rank=len(item.shape): (0,) * rank)

    return pl.pallas_call(
        body,
        grid=(1,),
        out_shape=tuple(outs),
        in_specs=[pl.BlockSpec(memory_space=pltpu.SMEM)] + [whole(item) for item in flat],
        out_specs=tuple(whole(item) for item in outs),
        name=name,
        **settings(cost),
    )(info, *flat)


def run(body, outs, info, flat, name, cost, scratch=(), direct=0):
    layers = [item[0] if isinstance(item, tuple) else None for item in flat]
    args, spots, buffers = [], [], []

    def add(item):
        args.append(item)
        return len(args) - 1

    for item in flat:
        held = item[1] if isinstance(item, tuple) else (item,)
        spots.append(
            [tuple(add(one) for one in part) if isinstance(part, tuple) else add(part) for part in held]
        )
        buffers.append(pltpu.VMEM(held[0].shape, held[0].dtype))
    out_buffers = [pltpu.VMEM(item.shape, item.dtype) for item in outs[direct:]]

    def kernel(info_ref, *refs):
        sources, refs = refs[: len(args)], refs[len(args) :]
        targets, refs = refs[: len(outs)], refs[len(outs) :]
        ins_held, refs = refs[: len(buffers)], refs[len(buffers) :]
        outs_held, refs = refs[: len(out_buffers)], refs[len(out_buffers) :]
        in_sems, out_sems = refs[:2]
        picked = []
        for layer, spot in zip(layers, spots):
            found = [
                tuple(sources[one] for one in part) if isinstance(part, tuple) else sources[part]
                for part in spot
            ]
            picked.append(found[0] if layer is None else found)
        ins = Arrivals(
            picked, ins_held, in_sems, lambda layer: info_ref[1] ^ layer, info_ref[2], layers
        )
        held = (None,) * direct + tuple(outs_held)
        departures = Departures(targets, held, out_sems, direct)
        body(info_ref, ins, departures, *refs[2:])
        ins.close()
        departures.close()

    return pl.pallas_call(
        kernel,
        out_shape=tuple(outs),
        in_specs=[pl.BlockSpec(memory_space=pltpu.SMEM)]
        + [pl.BlockSpec(memory_space=pl.ANY) for _ in args],
        out_specs=tuple(pl.BlockSpec(memory_space=pl.ANY) for _ in outs),
        scratch_shapes=buffers
        + out_buffers
        + [pltpu.SemaphoreType.DMA((len(flat), 2)), pltpu.SemaphoreType.DMA((len(outs),))]
        + list(scratch),
        name=name,
        **settings(cost),
    )(info, *args)


def swap(block, axis, size, bit):
    return lax.ppermute(block, axis, [(i, i ^ bit) for i in range(size)])


def tie(first, second):
    first = tuple(first)
    return lax.optimization_barrier(first + tuple(second))[: len(first)]


def add_low(left, right):
    return (left.astype(F32) + right.astype(F32)).astype(BF16)


class Ring:
    def __init__(self, n_dp, n_pipe, dp, core):
        bits = [1 << k for k in range(n_dp.bit_length() - 1)]
        self.orders = (bits, bits[1:] + bits[:1])
        self.steps = len(bits)
        self.n_dp, self.n_pipe, self.dp, self.core = n_dp, n_pipe, dp, core

    def swap(self, block, step):
        route = []
        for d in range(self.n_dp):
            for p in range(self.n_pipe):
                there = d ^ self.orders[p & 1][step]
                route.append((d * self.n_pipe + p, there * self.n_pipe + p))
        return lax.ppermute(block, ("dp", "pipe"), route)

    def upper(self, step):
        bit = jnp.where(self.core == 0, self.orders[0][step], self.orders[1][step])
        return (self.dp & bit) != 0

    def halve(self, block, step):
        side = jnp.where(self.upper(step), 1, 0)
        parts = block.reshape((2, block.shape[0] // 2) + block.shape[1:])
        kept = lax.dynamic_index_in_dim(parts, side, 0, keepdims=False)
        sent = lax.dynamic_index_in_dim(parts, 1 - side, 0, keepdims=False)
        return add_low(kept, self.swap(sent, step))

    def double(self, block, step):
        got = self.swap(block, step)
        side = jnp.where(self.upper(step), 1, 0)
        rows = block.shape[0]
        whole = jnp.zeros((2 * rows,) + block.shape[1:], block.dtype)
        whole = lax.dynamic_update_slice_in_dim(whole, block, side * rows, 0)
        return lax.dynamic_update_slice_in_dim(whole, got, (1 - side) * rows, 0)


def shards(
    images,
    image_counts,
    conv_kernel,
    bn_gain,
    bn_bias,
    mix_h,
    mix_h_bias,
    mix_w,
    mix_w_bias,
    unite_w,
    unite_b,
    ln_gain,
    ln_bias,
    w_in,
    b_in,
    w_out,
    b_out,
    running_mean,
    running_var,
    cotangent,
):
    n_dp, n_pipe = lax.axis_size("dp"), lax.axis_size("pipe")
    dp, pipe = lax.axis_index("dp"), lax.axis_index("pipe")
    layers = n_pipe
    batch = images.shape[0] // n_pipe
    side, chans, hid = images.shape[1], images.shape[3], w_in.shape[2]
    sz = Sizes(batch, side, chans, hid, n_dp)
    core, plane = pipe & 1, pipe >> 1
    tokens = sz.tokens

    def shape(*dims, dtype=F32):
        return jax.ShapeDtypeStruct(dims, dtype)

    valid = jnp.clip(image_counts[0] - pipe * batch, 0, batch).astype(jnp.int32)
    info = jnp.stack([valid, pipe.astype(jnp.int32), (dp & 1).astype(jnp.int32)])

    def to_all(block):
        over = swap(block, "pipe", n_pipe, 2)
        return (block, swap(block, "pipe", n_pipe, 1), over, swap(over, "pipe", n_pipe, 1))

    first_taps = to_all(conv_kernel[0])
    own, own_half, small_own = run_whole(
        functools.partial(prepare_kernel, sz),
        (
            shape(chans, sz.weight_lanes, dtype=BF16),
            shape(chans // 2, sz.weight_lanes, dtype=BF16),
            shape(SMALL_ROWS, sz.lanes),
        ),
        info,
        (
            conv_kernel[0],
            bn_gain,
            bn_bias,
            mix_h[0],
            mix_h_bias,
            mix_w[0],
            mix_w_bias,
            unite_w[0].T,
            unite_b,
            ln_gain,
            ln_bias,
            w_in[0],
            b_in,
            w_out[0].T,
            b_out,
        ),
        "prepare",
        2,
    )
    beside = swap(own, "pipe", n_pipe, 1)

    def across_plane(block, cores):
        return lax.ppermute(block, "pipe", [(p, p ^ 2) for p in cores])

    def to_beside(block, cores):
        return lax.ppermute(block, "pipe", [(p, p ^ 1) for p in cores])

    def to_neighbour(block, cores):
        route = [
            (d * n_pipe + p, (d ^ 1) * n_pipe + p) for d in range(n_dp) for p in cores
        ]
        return lax.ppermute(block, ("dp", "pipe"), route)

    (half_sent,) = tie((own_half,), (first_taps[2],))
    first = across_plane(half_sent, (0, 2))

    def micro(array):
        block = lax.dynamic_slice_in_dim(array, pipe * batch, batch, 0)
        block = jnp.pad(block, ((0, 0), (0, 0), (0, sz.pad - side), (0, 0)))
        return block.reshape(tokens, chans)

    sums_shape = shape(n_dp, 8, LANES)
    plain = shape(tokens, chans)
    low = shape(tokens, chans, dtype=BF16)

    field = micro(images)
    conv, sums = run(
        functools.partial(start_kernel, sz),
        (plain, sums_shape),
        info,
        (field, (0, first_taps)),
        "start",
        2,
    )
    got = lax.all_to_all(sums, "dp", 0, 0)
    (small_own,) = tie((small_own,), (first,))
    smalls = to_all(small_own)
    (first,) = tie((first,), (sums,))
    first_beside, second = to_beside(first, (0, 2)), to_neighbour(first, (0, 2))
    (second,) = tie((second,), (got,))
    (half_late,) = tie((own_half,), (first_beside, smalls[2]))
    first_odd = across_plane(half_late, (1, 3))
    second_beside = to_beside(second, (0, 2))
    even = (own, beside, (first, second), (first_beside, second_beside))

    fields, convs, saved, stats, weights = [field], [conv], [], [], [even]
    for depth in range(layers):
        if depth:
            got = lax.all_to_all(sums, "dp", 0, 0)
        last = depth + 1 == layers
        outs = (
            low,
            shape(tokens, hid, dtype=BF16),
            shape(tokens, hid, dtype=BF16),
            plain,
            shape(tokens, 1),
            shape(tokens, 3 * sz.lanes, dtype=BF16),
            shape(8, sz.lanes),
        )
        flat = (got, convs[depth], (depth, smalls), (depth, weights[depth & 1]), fields[depth])
        if not last:
            outs += (plain, sums_shape)
            flat += ((depth + 1, smalls),)
        results = run(
            functools.partial(forward_kernel, sz, last),
            outs,
            info,
            flat,
            f"layer_{depth}_forward",
            6,
            scratch=[pltpu.SemaphoreType.DMA((2, -(-hid // HID_STEP)))],
        )
        fields.append(results[0])
        if depth == 0:
            (first_odd,) = tie((first_odd,), (second_beside,))
            first_odd_beside = to_beside(first_odd, (1, 3))
            second_odd = to_neighbour(first_odd, (1, 3))
            (second_odd,) = tie((second_odd,), (results[0],))
            second_odd_beside = to_beside(second_odd, (1, 3))
            weights.append(
                (own, beside, (first_odd, second_odd), (first_odd_beside, second_odd_beside))
            )
        saved.append(results[1:6])
        stats.append(results[6])
        if not last:
            convs.append(results[7])
            sums = results[8]

    def to_owners(parts):
        sent = [lax.select_n(pipe ^ bit, *parts) for bit in range(n_pipe)]
        return sent[:1] + [swap(sent[bit], "pipe", n_pipe, bit) for bit in range(1, n_pipe)]

    def collect(parts):
        whole = jnp.zeros((n_pipe, batch, side, side, chans), BF16)
        for bit, part in enumerate(parts):
            part = part.reshape(1, batch, side, sz.pad, chans)[:, :, :, :side]
            whole = lax.dynamic_update_slice(whole, part, (pipe ^ bit, 0, 0, 0, 0))
        return whole.reshape(1, n_pipe * batch, side, side, chans)

    half_shape = shape(sz.half_rows, LANES, dtype=BF16)
    halves, ends = [None] * layers, [None] * 2
    grads, closes = [None] * layers, [None] * layers
    behind = None
    for depth in reversed(range(layers)):
        outs = (half_shape, half_shape, plain, plain, sums_shape)
        if behind is None:
            front = (micro(cotangent),)
        else:
            front = behind
            outs += (low, shape(CLOSE_ROWS, sz.lanes))
        active, slope, unit, spread, joined = saved[depth]
        results = run(
            functools.partial(backward_kernel, sz, behind is None),
            outs,
            info,
            front
            + ((depth, smalls), (depth, weights[depth & 1]), slope, unit, spread, active)
            + (joined, stats[depth], convs[depth]),
            f"layer_{depth}_backward",
            12,
            scratch=[
                pltpu.VMEM((2,) + half_shape.shape, BF16),
                pltpu.VMEM((tokens, hid), BF16),
                pltpu.SemaphoreType.DMA((4,)),
            ],
            direct=2,
        )
        kept, sent, normed_grad, hidden_grad, sums = results[:5]
        if behind is not None:
            grads[depth + 1], closes[depth + 1] = results[5:]
        halves[depth] = add_low(kept, swap(sent, "pipe", n_pipe, 1))
        if depth == 0:
            (sums,) = tie((sums,), (ends[1],))
        if depth < 2:
            mine = jnp.where(plane == 0, halves[depth], halves[depth + 2])
            other = jnp.where(plane == 0, halves[depth + 2], halves[depth])
            ends[depth] = add_low(mine, swap(other, "pipe", n_pipe, 2))
        got = lax.all_to_all(sums, "dp", 0, 0)
        (got,) = tie((got,), (halves[depth],))
        behind = (
            got,
            stats[depth],
            (depth, smalls),
            normed_grad,
            convs[depth],
            hidden_grad,
            fields[depth],
        )
    ring = Ring(n_dp, n_pipe, dp, core)
    (odd,), even = tie((ends[1],), (sums,)), ends[0]
    moves = [functools.partial(ring.halve, step=step) for step in range(ring.steps)]
    moves += [functools.partial(ring.double, step=step) for step in reversed(range(ring.steps))]
    odd_moves, even_moves = iter(moves), iter(moves)
    odd = next(odd_moves)(odd)

    def beside_step(function, *held):
        return function(*tie(held, (even, odd)))

    def step_on(*held):
        nonlocal even, odd
        even = next(even_moves)(even)
        odd_move = next(odd_moves, None)
        odd = odd if odd_move is None else odd_move(odd)
        even, odd, *held = tie((even, odd) + held, ())
        return held

    def end_chain(got):
        return run(
            functools.partial(finish_kernel, sz),
            (low, shape(CLOSE_ROWS, sz.lanes)),
            info,
            (got,) + behind[1:],
            "finish",
            4,
        )

    def add_taps(closing):
        taps = jnp.sum(closing[:, 4:13], axis=0)
        return lax.all_to_all(
            jnp.broadcast_to(taps[None], (n_dp,) + taps.shape), "dp", 0, 0
        )

    grads[0], closes[0] = beside_step(end_chain, behind[0])
    grads[0], closes[0] = step_on(grads[0], closes[0])
    closing = beside_step(
        lambda *held: lax.all_to_all(jnp.stack(held), "pipe", 0, 0), *closes
    )
    (closing,) = step_on(closing)
    output_parts = beside_step(lambda *held: to_owners(held), *fields[1:])
    grad_parts = beside_step(lambda *held: to_owners(held), *grads)
    for _ in range(2, ring.steps):
        step_on()
    taps = beside_step(add_taps, closing)
    for _ in range(2, ring.steps):
        step_on()
    layer_outputs = beside_step(lambda *held: collect(held), *output_parts)
    layer_outputs, taps = step_on(layer_outputs, taps)
    input_grads = beside_step(lambda *held: collect(held), *grad_parts)
    (input_grads,) = step_on(input_grads)
    parts = [odd, even]
    mine = jnp.where(core == 0, parts[1], parts[0])
    other = jnp.where(core == 0, parts[0], parts[1])
    got = swap(other, "pipe", n_pipe, 1)
    row = shape(1, chans)
    outs = (
        shape(3, 3, 1, chans),
        row,
        row,
        shape(side, 1, side),
        shape(1, side),
        shape(side, 1, side),
        shape(1, side),
        shape(chans, 3 * chans),
        row,
        row,
        row,
        shape(chans, hid),
        shape(1, hid),
        shape(chans, hid),
        row,
        row,
        row,
    )
    finished = list(
        run_whole(
            functools.partial(closing_kernel, sz),
            outs,
            info,
            (mine, got, closing, taps, running_mean, running_var),
            "closing",
            4,
        )
    )
    finished[0] = jnp.transpose(finished[0], (2, 0, 1, 3))
    for k in (3, 5):
        finished[k] = jnp.transpose(finished[k], (1, 0, 2))
    for k in (7, 13):
        finished[k] = finished[k].T[None]
    finished[11] = finished[11][None]
    return (layer_outputs, input_grads) + tuple(finished)


def solution(mesh):
    four = P("pipe", None, None, None)
    three = P("pipe", None, None)
    two = P("pipe", None)
    images = P("dp", None, None, None)
    in_specs = (
        images, P("dp"), four, two, two, three, two, three, two, three, two, two, two,
        three, two, three, two, two, two, images,
    )
    stacked = P("pipe", "dp", None, None, None)
    out_specs = (
        stacked, stacked, four, two, two, three, two, three, two, three, two, two, two,
        three, two, three, two, two, two,
    )
    return jax.shard_map(
        shards, mesh=mesh, in_specs=in_specs, out_specs=out_specs, check_vma=False
    )
```

```python
import functools

import jax
import jax.numpy as jnp
from jax import lax
from jax.experimental import pallas as pl
from jax.experimental.pallas import tpu as pltpu
from jax.sharding import PartitionSpec as P

F32 = jnp.float32
BF16 = jnp.bfloat16
LANES = 128
HID_STEP = 256
ROW_STEP = 64
LN_STEP = 32
VMEM_BYTES = 58 * 1024 * 1024
EXTRA = 128
ROW_BN_GAIN, ROW_BN_BIAS, ROW_UNITE_B, ROW_LN_GAIN, ROW_LN_BIAS, ROW_B_OUT = range(9, 15)
ROW_MIX_BIAS, ROW_B_IN, ROW_MIX = 15, 16, 24
SMALL_ROWS = 40
CLOSE_ROWS = 16
GRAD_ROWS = 64


def wide(value):
    return -(-value // LANES) * LANES


def tall(value):
    return -(-value // 16) * 16


def dot(left, right):
    return lax.dot_general(left, right, (((1,), (0,)), ((), ())), preferred_element_type=F32)


def dot_nt(left, right):
    return lax.dot_general(left, right, (((1,), (1,)), ((), ())), preferred_element_type=F32)


def dot_exact(left, right):
    return lax.dot_general(
        left,
        right,
        (((1,), (0,)), ((), ())),
        preferred_element_type=F32,
        precision=lax.Precision.HIGHEST,
    )


class Sizes:
    def __init__(self, batch, side, chans, hid, n_dp):
        self.batch, self.side, self.chans, self.hid, self.n_dp = batch, side, chans, hid, n_dp
        self.pad = tall(side)
        self.image = side * self.pad
        self.tokens = batch * self.image
        self.lanes = wide(chans)
        self.full = chans // LANES
        self.rest = chans - self.full * LANES
        self.hid_blocks = hid // LANES
        left_blocks = -(-3 * self.rest // LANES)
        self.unite_blocks = 3 * self.full + left_blocks
        self.blocks = 2 * self.hid_blocks + self.unite_blocks
        self.half_blocks = self.blocks // 2
        self.half_rows = self.half_blocks * chans + EXTRA
        self.weight_lanes = 2 * hid + 3 * self.lanes

    def place(self, block):
        half, place = divmod(block, self.half_blocks)
        return half, place * self.chans

    def unite(self, part):
        first = 2 * self.hid + part * self.lanes
        return slice(first, first + self.chans)


def token_mask(sz, valid):
    row = lax.broadcasted_iota(jnp.int32, (sz.tokens, 1), 0)
    return ((row < valid * sz.image) & (row % sz.pad < sz.side)).astype(F32)


def taps_of(sz, small):
    return [small[k : k + 1, : sz.chans] for k in range(9)]


def row_of(sz, small, index):
    return small[index : index + 1, : sz.chans]


def fill_lanes(sz, row):
    if sz.lanes == sz.chans:
        return row
    return jnp.concatenate([row, jnp.zeros((1, sz.lanes - sz.chans), F32)], axis=1)


def lane_rows(sz, row):
    row = fill_lanes(sz, row)
    return [row[:, k * LANES : (k + 1) * LANES] for k in range(sz.lanes // LANES)]


def put_sums(sz, ref, first, second, number):
    pieces = lane_rows(sz, first) + lane_rows(sz, second)
    pieces.append(jnp.zeros((1, LANES), F32) + number)
    pieces.append(jnp.zeros((8 - len(pieces), LANES), F32))
    block = jnp.concatenate(pieces, axis=0)
    for index in range(sz.n_dp):
        ref[index] = block


def take_sums(sz, ref):
    total = ref[0]
    for index in range(1, sz.n_dp):
        total = total + ref[index]
    count = sz.lanes // LANES
    first = jnp.concatenate([total[k : k + 1] for k in range(count)], axis=1)
    second = jnp.concatenate([total[count + k : count + k + 1] for k in range(count)], axis=1)
    return first[:, : sz.chans], second[:, : sz.chans], total[2 * count : 2 * count + 1, 0:1]


def sum_rows(value):
    return jnp.sum(value, axis=0, keepdims=True)


def mean_lanes(value):
    return jnp.mean(value, axis=1, keepdims=True)


def pick_rows(sz):
    row = lax.broadcasted_iota(jnp.int32, (sz.image, sz.pad), 0)
    col = lax.broadcasted_iota(jnp.int32, (sz.image, sz.pad), 1)
    return (row // sz.pad == col), (row % sz.pad == col)


def same_masks(sz):
    row = lax.broadcasted_iota(jnp.int32, (sz.image, sz.image), 0)
    col = lax.broadcasted_iota(jnp.int32, (sz.image, sz.image), 1)
    return (row % sz.pad == col % sz.pad), (row // sz.pad == col // sz.pad)


def mixers(sz, small, turned):
    pick_i, pick_j = pick_rows(sz)
    same_j, same_i = same_masks(sz)
    product = dot_nt if turned else dot
    found = []
    for pick, same, lane in ((pick_i, same_j, 0), (pick_j, same_i, LANES)):
        mix = small[ROW_MIX : ROW_MIX + sz.pad, lane : lane + sz.pad].astype(BF16)
        pick = pick.astype(BF16)
        spread = dot_nt(product(pick, mix).astype(BF16), pick)
        found.append(jnp.where(same, spread, 0.0).astype(BF16))
    return found


class Arrivals:
    def __init__(self, sources, buffers, sems, role_of, bit, layers):
        self.buffers, self.copies = buffers, []
        for k, (source, buffer) in enumerate(zip(sources, buffers)):
            if layers[k] is None:
                copies = [pltpu.make_async_copy(source, buffer, sems.at[k, 0])]
                copies[0].start()
            else:
                halved = isinstance(source[-1], tuple)
                rows = buffer.shape[0] // 2 if halved else buffer.shape[0]
                spots = [pl.ds(0, rows), pl.ds(rows, rows)] if halved else [pl.ds(0, rows)]
                copies = [
                    pltpu.make_async_copy(source[0].at[spot], buffer.at[spot], sems.at[k, h])
                    for h, spot in enumerate(spots)
                ]
                for place, held in enumerate(source):

                    @pl.when(role_of(layers[k]) == place)
                    def _(held=held, buffer=buffer, k=k, spots=spots, rows=rows):
                        for h, spot in enumerate(spots):
                            if isinstance(held, tuple):
                                piece = held[h]
                                at = h ^ bit
                                spot = pl.ds(pl.multiple_of(at * rows, 16), rows)
                            else:
                                piece = held.at[spot]
                            pltpu.make_async_copy(piece, buffer.at[spot], sems.at[k, h]).start()

            self.copies.append(copies)

    def __getitem__(self, k):
        if self.copies[k] is not None:
            for copy in self.copies[k]:
                copy.wait()
            self.copies[k] = None
        return self.buffers[k]

    def close(self):
        for k in range(len(self.copies)):
            self[k]


class Departures:
    def __init__(self, targets, buffers, sems, direct):
        self.buffers, self.targets = buffers, targets
        self.copies = [
            None if k < direct else pltpu.make_async_copy(buffer, target, sems.at[k])
            for k, (target, buffer) in enumerate(zip(targets, buffers))
        ]
        self.started, self.parts = [False] * len(self.copies), []

    def put(self, k, value):
        self.buffers[k][...] = value
        self.send(k)

    def send(self, k):
        self.copies[k].start()
        self.started[k] = True

    def send_part(self, k, lanes, sem):
        spot = (slice(None), lanes)
        copy = pltpu.make_async_copy(self.buffers[k].at[spot], self.targets[k].at[spot], sem)
        copy.start()
        self.parts.append(copy)

    def close(self):
        for copy, started in zip(self.copies, self.started):
            if started:
                copy.wait()
        for copy in self.parts:
            copy.wait()


def prepare_kernel(
    sz,
    info,
    taps_ref,
    bn_gain_ref,
    bn_bias_ref,
    mix_h_ref,
    mix_h_bias_ref,
    mix_w_ref,
    mix_w_bias_ref,
    unite_ref,
    unite_b_ref,
    ln_gain_ref,
    ln_bias_ref,
    in_ref,
    b_in_ref,
    w_out_ref,
    b_out_ref,
    weights_ref,
    half_ref,
    small_ref,
):
    chans, hid = sz.chans, sz.hid
    weights_ref[:, :hid] = in_ref[...]
    weights_ref[:, hid : 2 * hid] = w_out_ref[...]
    gap = jnp.zeros((chans, sz.lanes - chans), BF16)
    for part in range(3):
        first = 2 * hid + part * sz.lanes
        weights_ref[:, first : first + sz.lanes] = jnp.concatenate(
            [unite_ref[:, part * chans : (part + 1) * chans], gap], axis=1
        )
    rows = half_ref.shape[0]
    half_ref[...] = weights_ref[pl.ds(pl.multiple_of(info[2] * rows, 16), rows)]
    small_ref[...] = jnp.zeros(small_ref.shape, F32)
    for p in range(3):
        small_ref[3 * p : 3 * p + 3, :chans] = taps_ref[p].astype(F32)
    rows = (bn_gain_ref, bn_bias_ref, unite_b_ref, ln_gain_ref, ln_bias_ref, b_out_ref)
    for place, ref in zip(range(ROW_BN_GAIN, ROW_MIX_BIAS), rows):
        small_ref[place : place + 1, :chans] = ref[...]
    place = ROW_MIX_BIAS
    small_ref[place : place + 1, : sz.side] = mix_h_bias_ref[...]
    small_ref[place : place + 1, LANES : LANES + sz.side] = mix_w_bias_ref[...]
    for k, lane in enumerate(range(0, hid, sz.lanes)):
        wide_part = min(sz.lanes, hid - lane)
        small_ref[ROW_B_IN + k : ROW_B_IN + k + 1, :wide_part] = b_in_ref[
            :, lane : lane + wide_part
        ]
    rows = slice(ROW_MIX, ROW_MIX + sz.side)
    small_ref[rows, : sz.side] = mix_h_ref[...].astype(F32)
    small_ref[rows, LANES : LANES + sz.side] = mix_w_ref[...].astype(F32)


def steps(size, step):
    return [slice(first, min(first + step, size)) for first in range(0, size, step)]


def fold(value):
    total = value[:8]
    for first in range(8, value.shape[0], 8):
        total = total + value[first : first + 8]
    return total


def conv_rows(sz, rows, taps, back=False):
    order = (2, 1, 0) if back else (0, 1, 2)
    parts = []
    for row in rows:
        near = (pltpu.roll(row, 1, 0), row, pltpu.roll(row, sz.pad - 1, 0))
        near = [near[q] for q in order]
        parts.append(
            [taps[3 * p] * near[0] + taps[3 * p + 1] * near[1] + taps[3 * p + 2] * near[2] for p in order]
        )
    found = []
    for i in range(len(rows)):
        total = parts[i][1]
        if i > 0:
            total = total + parts[i - 1][0]
        if i + 1 < len(rows):
            total = total + parts[i + 1][2]
        found.append(total)
    return found


def next_conv(sz, rows, taps, masks, conv_ref, sums_ref, number):
    first = jnp.zeros((8, sz.chans), F32)
    second = jnp.zeros((8, sz.chans), F32)
    for n in range(sz.batch):
        part = range(n * sz.side, (n + 1) * sz.side)
        for i, conv in zip(part, conv_rows(sz, [rows[i] for i in part], taps)):
            conv_ref[i * sz.pad : (i + 1) * sz.pad] = conv
            masked = masks[i] * conv
            first = first + fold(masked)
            second = second + fold(masked * conv)
    put_sums(sz, sums_ref, sum_rows(first), sum_rows(second), number)


def row_masks(sz, valid):
    mask = token_mask(sz, valid)
    return [mask[i : i + sz.pad] for i in range(0, sz.tokens, sz.pad)]


def start_kernel(sz, info, ins, outs):
    field = ins[0]
    kernel = ins[1]
    taps = [kernel[p, q : q + 1].astype(F32) for p in range(3) for q in range(3)]
    rows = [field[i : i + sz.pad].astype(F32) for i in range(0, sz.tokens, sz.pad)]
    number = (info[0] * (sz.side * sz.side)).astype(F32)
    masks = row_masks(sz, info[0])
    next_conv(sz, rows, taps, masks, outs.buffers[0], outs.buffers[1], number)
    outs.send(0)
    outs.send(1)


def forward_kernel(sz, last, info, ins, outs, part_sems):
    GOT, CONV, SMALL, WEIGHTS, FIELD = range(5)
    OUT, ACTIVE, SLOPE, UNIT, SPREAD, JOINED, STAT, CONV_NEXT, SUMS = range(9)
    small = ins[SMALL]
    total, square, count = take_sums(sz, ins[GOT])
    center = total / count
    variance = square / count - center * center
    inverse = lax.rsqrt(variance + 1e-05)
    stat = [
        fill_lanes(sz, center),
        fill_lanes(sz, inverse),
        fill_lanes(sz, variance * count / (count - 1.0)),
        jnp.zeros((1, sz.lanes), F32) + count,
        jnp.zeros((4, sz.lanes), F32),
    ]
    outs.put(STAT, jnp.concatenate(stat, axis=0))
    gain = inverse * row_of(sz, small, ROW_BN_GAIN)
    shift = row_of(sz, small, ROW_BN_BIAS)
    conv, joined = ins[CONV], outs.buffers[JOINED]
    chans, lanes = sz.chans, sz.lanes
    for rows in steps(sz.tokens, ROW_STEP):
        normed = ((conv[rows] - center) * gain + shift).astype(BF16)
        gap = jnp.zeros((normed.shape[0], lanes - chans), BF16)
        joined[rows, :lanes] = jnp.concatenate([normed, gap], axis=1)
    mix_h, mix_w = mixers(sz, small, False)
    pick_i, pick_j = pick_rows(sz)
    bias = small[ROW_MIX_BIAS : ROW_MIX_BIAS + 1]
    bias_h = jnp.sum(jnp.where(pick_i, bias[:, : sz.pad], 0.0), axis=1, keepdims=True)
    bias_w = jnp.sum(
        jnp.where(pick_j, bias[:, LANES : LANES + sz.pad], 0.0), axis=1, keepdims=True
    )
    for n in range(sz.batch):
        normed = joined[n * sz.image : (n + 1) * sz.image, :lanes]
        for mix, add, place in ((mix_h, bias_h, 1), (mix_w, bias_w, 2)):
            mixed = dot(mix, normed)
            for rows in steps(sz.image, ROW_STEP):
                there = slice(n * sz.image + rows.start, n * sz.image + rows.stop)
                joined[there, place * lanes : (place + 1) * lanes] = (
                    mixed[rows] + add[rows]
                ).astype(BF16)
    outs.send(JOINED)
    weights_ref = ins[WEIGHTS]
    field = ins[FIELD]
    united = dot_nt(joined[...], weights_ref[:, 2 * sz.hid :])
    unite_b = row_of(sz, small, ROW_UNITE_B)
    ln_gain, ln_bias = row_of(sz, small, ROW_LN_GAIN), row_of(sz, small, ROW_LN_BIAS)
    hidden, lnormed = [], []
    for rows in steps(sz.tokens, LN_STEP):
        part = field[rows].astype(F32) + (united[rows] + unite_b)
        offset = part - mean_lanes(part)
        spread = lax.rsqrt(mean_lanes(offset * offset) + 1e-06)
        unit = offset * spread
        outs.buffers[UNIT][rows] = unit
        outs.buffers[SPREAD][rows] = spread
        hidden.append(part)
        lnormed.append((unit * ln_gain + ln_bias).astype(BF16))
    hidden = jnp.concatenate(hidden, axis=0)
    lnormed = jnp.concatenate(lnormed, axis=0)
    outs.send(UNIT)
    outs.send(SPREAD)
    lanes_in = [small[ROW_B_IN + k : ROW_B_IN + k + 1] for k in range(-(-sz.hid // lanes))]
    b_in = jnp.concatenate(lanes_in, axis=1)
    root = 0.7978845608028654
    cubic = 0.044715
    for part in steps(sz.hid, HID_STEP):
        product = dot(lnormed, weights_ref[:, part])
        for rows in steps(sz.tokens, ROW_STEP):
            before = product[rows] + b_in[:, part]
            squared = before * before
            bent = jnp.tanh(before * (root + (root * cubic) * squared))
            half = 0.5 + 0.5 * bent
            active = before * half
            slope = half + (active * (1.0 - bent)) * (root + (3.0 * root * cubic) * squared)
            outs.buffers[ACTIVE][rows, part] = active.astype(BF16)
            outs.buffers[SLOPE][rows, part] = slope.astype(BF16)
        index = part.start // HID_STEP
        if not last:
            outs.send_part(ACTIVE, part, part_sems.at[0, index])
            outs.send_part(SLOPE, part, part_sems.at[1, index])
    branch = dot_nt(outs.buffers[ACTIVE][...], weights_ref[:, sz.hid : 2 * sz.hid])
    masks = row_masks(sz, info[0])
    b_out = row_of(sz, small, ROW_B_OUT)
    results = []
    for i, mask in enumerate(masks):
        rows = slice(i * sz.pad, (i + 1) * sz.pad)
        result = (mask * (hidden[rows] + (branch[rows] + b_out))).astype(BF16)
        outs.buffers[OUT][rows] = result
        results.append(result.astype(F32))
    outs.send(OUT)
    if not last:
        number = (info[0] * (sz.side * sz.side)).astype(F32)
        taps = taps_of(sz, ins[5])
        next_conv(
            sz, results, taps, masks, outs.buffers[CONV_NEXT], outs.buffers[SUMS], number
        )
        outs.send(SUMS)
        outs.send(CONV_NEXT)


def finish_layer(sz, info, ins, outs, first_out):
    GOT, STAT, SMALL, NORMED_GRAD, CONV, HIDDEN_GRAD, FIELD = range(7)
    small, stat = ins[SMALL], ins[STAT]
    chans = sz.chans
    taps = taps_of(sz, small)
    sum_dz, sum_dzx, _ = take_sums(sz, ins[GOT])
    count = stat[3:4, 0:1]
    center, inverse = stat[0:1, :chans], stat[1:2, :chans]
    scale = inverse * row_of(sz, small, ROW_BN_GAIN)
    mean_dz, mean_dzx = sum_dz / count, inverse * (sum_dzx / count)
    normed_grad, conv, hidden_grad, field = (
        ins[k] for k in (NORMED_GRAD, CONV, HIDDEN_GRAD, FIELD)
    )
    masks = row_masks(sz, info[0])
    sums = [jnp.zeros((8, chans), F32) for _ in range(9)]
    grads = []
    for n in range(sz.batch):
        spots = [
            slice(i * sz.pad, (i + 1) * sz.pad) for i in range(n * sz.side, (n + 1) * sz.side)
        ]
        conv_grads = [
            (masks[n * sz.side + i] * scale)
            * (normed_grad[rows] - mean_dz - (conv[rows] - center) * mean_dzx)
            for i, rows in enumerate(spots)
        ]
        for rows, back in zip(spots, conv_rows(sz, conv_grads, taps, back=True)):
            grad = (hidden_grad[rows] + back).astype(BF16)
            outs.buffers[first_out][rows] = grad
            grads.append(grad)
        for i, rows in enumerate(spots):
            row = field[rows].astype(F32)
            near = (pltpu.roll(row, 1, 0), row, pltpu.roll(row, sz.pad - 1, 0))
            for p in range(3):
                there = i + 1 - p
                if 0 <= there < sz.side:
                    for q in range(3):
                        sums[3 * p + q] = sums[3 * p + q] + fold(conv_grads[there] * near[q])
    outs.send(first_out)
    pieces = [center, stat[2:3, :chans], sum_dz, sum_dzx] + [sum_rows(item) for item in sums]
    block = [fill_lanes(sz, piece) for piece in pieces]
    block.append(jnp.zeros((CLOSE_ROWS - len(pieces), sz.lanes), F32))
    outs.put(first_out + 1, jnp.concatenate(block, axis=0))
    return grads


def finish_kernel(sz, info, ins, outs):
    finish_layer(sz, info, ins, outs, 0)


def backward_kernel(sz, first, info, ins, outs, pack_ref, before_ref, pack_sems):
    base = 1 if first else 7
    SMALL, WEIGHTS, SLOPE, UNIT, SPREAD, ACTIVE, JOINED, STAT, CONV = range(base, base + 9)
    core = info[1] & 1
    chans, tokens, lanes = sz.chans, sz.tokens, sz.lanes
    shipped = []

    def put(block, value):
        half, row = sz.place(block)
        pack_ref[half ^ core, row : row + chans] = value

    def ship(half, first_row, rows):
        spot, sem = pl.ds(first_row, rows), pack_sems.at[len(shipped)]
        for place in range(2):

            @pl.when(half ^ core == place)
            def _(place=place):
                pltpu.make_async_copy(
                    pack_ref.at[place, spot], outs.targets[place].at[spot], sem
                ).start()

        shipped.append(
            pltpu.make_async_copy(pack_ref.at[0, spot], outs.targets[0].at[spot], sem)
        )

    if first:
        upstream = [ins[0][i : i + sz.pad] for i in range(0, tokens, sz.pad)]
    else:
        upstream = finish_layer(sz, info, ins, outs, 5)
    small = ins[SMALL]
    masks = row_masks(sz, info[0])
    out_grads = [mask * grad.astype(F32) for mask, grad in zip(masks, upstream)]
    branch_grad = jnp.concatenate([item.astype(BF16) for item in out_grads], axis=0)
    out_sum = fold(out_grads[0])
    for item in out_grads[1:]:
        out_sum = out_sum + fold(item)
    out_grads = jnp.concatenate(out_grads, axis=0)
    unit = ins[UNIT]
    ln_gain, ln_bias = row_of(sz, small, ROW_LN_GAIN), row_of(sz, small, ROW_LN_BIAS)
    lnormed = [
        (unit[rows] * ln_gain + ln_bias).astype(BF16) for rows in steps(tokens, ROW_STEP)
    ]
    lnormed = jnp.concatenate(lnormed, axis=0)
    turned_ln = jnp.concatenate([lnormed.T, jnp.ones((16, tokens), BF16)], axis=0)
    turned_branch = branch_grad.T
    weights_ref, slope_ref, active_ref = ins[WEIGHTS], ins[SLOPE], ins[ACTIVE]
    in_pieces = []
    for k in range(0, sz.hid, HID_STEP):
        part = slice(k, k + HID_STEP)
        active_grad = dot(branch_grad, weights_ref[:, sz.hid + k : sz.hid + k + HID_STEP])
        for rows in steps(tokens, ROW_STEP):
            before_ref[rows, part] = (
                active_grad[rows] * slope_ref[rows, part].astype(F32)
            ).astype(BF16)
        grad_in = dot(turned_ln, before_ref[:, part])
        grad_out = dot(turned_branch, active_ref[:, part])
        for lane in range(0, HID_STEP, LANES):
            block = (k + lane) // LANES
            put(block, grad_in[:chans, lane : lane + LANES].astype(BF16))
            put(sz.hid_blocks + block, grad_out[:, lane : lane + LANES].astype(BF16))
            in_pieces.append(grad_in[chans : chans + 1, lane : lane + LANES])
    norm_grad = dot_nt(before_ref[...], weights_ref[:, : sz.hid])
    ship(0, 0, sz.half_blocks * chans)
    spread = ins[SPREAD]
    token_grad = []
    token_sum, gain_sum, bias_sum = (jnp.zeros((8, chans), F32) for _ in range(3))
    for rows in steps(tokens, LN_STEP):
        grad, part = norm_grad[rows], unit[rows]
        product = grad * part
        gain_sum = gain_sum + fold(product)
        bias_sum = bias_sum + fold(grad)
        scaled = grad * ln_gain
        hidden_grad = out_grads[rows] + spread[rows] * (
            scaled - mean_lanes(scaled) - part * mean_lanes(product * ln_gain)
        )
        outs.buffers[3][rows] = hidden_grad
        token = hidden_grad.astype(BF16)
        token_grad.append(token)
        token_sum = token_sum + fold(token.astype(F32))
    token_grad = jnp.concatenate(token_grad, axis=0)
    outs.send(3)
    joined = ins[JOINED]
    joined_grad = dot(token_grad, weights_ref[:, 2 * sz.hid :])
    rows_grad = joined_grad[:, lanes : lanes + chans].astype(BF16)
    cols_grad = joined_grad[:, 2 * lanes : 2 * lanes + chans].astype(BF16)
    turned_h, turned_w = mixers(sz, small, True)
    stat, conv = ins[STAT], ins[CONV]
    center, inverse = stat[0:1, :chans], stat[1:2, :chans]
    sum_dz, sum_dzx = (jnp.zeros((8, chans), F32) for _ in range(2))
    for n in range(sz.batch):
        image = slice(n * sz.image, (n + 1) * sz.image)
        back_h = dot(turned_h, rows_grad[image])
        back_w = dot(turned_w, cols_grad[image])
        for rows in steps(sz.image, ROW_STEP):
            there = slice(image.start + rows.start, image.start + rows.stop)
            normed_grad = joined_grad[there, :chans] + (back_h[rows] + back_w[rows])
            outs.buffers[2][there] = normed_grad
            sum_dz = sum_dz + fold(normed_grad)
            sum_dzx = sum_dzx + fold(normed_grad * ((conv[there] - center) * inverse))
    put_sums(sz, outs.buffers[4], sum_rows(sum_dz), sum_rows(sum_dzx), 0.0)
    outs.send(4)
    outs.send(2)
    grad_unite = dot(token_grad.T, joined[...]).astype(BF16)
    block = 2 * sz.hid_blocks
    leftovers = []
    for part in range(3):
        for k in range(sz.full):
            lane = part * lanes + k * LANES
            put(block, grad_unite[:, lane : lane + LANES])
            block += 1
        if sz.rest:
            lane = part * lanes + sz.full * LANES
            leftovers.append(grad_unite[:, lane : lane + sz.rest])
    if sz.rest:
        left = jnp.concatenate(leftovers, axis=1)
        fill = wide(left.shape[1]) - left.shape[1]
        if fill:
            left = jnp.concatenate([left, jnp.zeros((chans, fill), BF16)], axis=1)
        for lane in range(0, left.shape[1], LANES):
            put(block, left[:, lane : lane + LANES])
            block += 1
    ship(1, 0, sz.half_blocks * chans)
    pick_i, pick_j = pick_rows(sz)
    same_j, same_i = same_masks(sz)
    mix_pieces, bias_pieces = [], []
    for grads, pick, same in ((rows_grad, pick_i, same_j), (cols_grad, pick_j, same_i)):
        pairs = jnp.zeros((sz.image, sz.image), F32)
        sums = jnp.zeros((sz.image, 1), F32)
        for n in range(sz.batch):
            image = slice(n * sz.image, (n + 1) * sz.image)
            pairs = pairs + dot_nt(grads[image], joined[image, :chans])
            sums = sums + jnp.sum(grads[image].astype(F32), axis=1, keepdims=True)
        pairs = jnp.where(same, pairs, 0.0)
        picked = pick.astype(F32)
        groups = [pairs[i : i + sz.pad] for i in range(0, sz.image, sz.pad)]
        if pick is pick_i:
            near = [sum_rows(group) for group in groups]
            near.append(jnp.zeros((sz.pad - sz.side, sz.image), F32))
            near = jnp.concatenate(near, axis=0)
        else:
            near = groups[0]
            for group in groups[1:]:
                near = near + group
        small_grad = dot_exact(near, picked)
        gap = LANES - sz.pad
        mix_pieces.append(
            jnp.concatenate([small_grad, jnp.zeros((sz.pad, gap), F32)], axis=1)
        )
        bias_pieces.append(
            jnp.concatenate([sum_rows(picked * sums), jnp.zeros((1, gap), F32)], axis=1)
        )
    pieces = (
        lane_rows(sz, sum_rows(token_sum))
        + lane_rows(sz, sum_rows(gain_sum))
        + lane_rows(sz, sum_rows(bias_sum))
        + lane_rows(sz, sum_rows(out_sum))
        + in_pieces
        + bias_pieces
        + mix_pieces
    )
    used = sum(piece.shape[0] for piece in pieces)
    pieces.append(jnp.zeros((EXTRA - used, LANES), F32))
    place = sz.half_blocks * chans
    pack_ref[core, place : place + EXTRA] = jnp.concatenate(pieces, axis=0).astype(BF16)
    pack_ref[1 - core, place : place + EXTRA] = jnp.zeros((EXTRA, LANES), BF16)
    ship(0, place, EXTRA)
    ship(1, place, EXTRA)
    for copy in shipped:
        copy.wait()


class Inner:
    def __init__(self, outs, places):
        leaves = [isinstance(place, int) for place in places]
        self.outs, self.places, self.leaves = outs, places, leaves
        self.buffers = [
            outs.buffers[place] if leave else place for place, leave in zip(places, leaves)
        ]

    def put(self, k, value):
        self.buffers[k][...] = value
        self.send(k)

    def send(self, k):
        if self.leaves[k]:
            self.outs.send(self.places[k])

    def send_part(self, k, part, sem):
        pass


class Inputs:
    def __init__(self, ins, places):
        self.ins, self.places = ins, places

    def __getitem__(self, k):
        place = self.places[k]
        return self.ins[place] if isinstance(place, int) else place


def turning_kernel(sz, info, ins, outs, active, slope, unit, spread, joined, *scratch):
    GOT, CONV, SMALL, WEIGHTS, FIELD, UPSTREAM = range(6)
    forward = Inner(outs, [5, active, slope, unit, spread, joined, 6])
    forward_kernel(sz, True, info, ins, forward, None)
    held = [UPSTREAM, SMALL, WEIGHTS, slope, unit, spread, active, joined]
    held += [outs.buffers[6], CONV]
    backward_kernel(sz, True, info, Inputs(ins, held), outs, *scratch)


def closing_kernel(sz, info, mine_ref, got_ref, close_ref, taps_got_ref, mean_ref, var_ref, *outs):
    (
        taps_ref,
        gain_ref,
        bias_ref,
        mix_h_ref,
        mix_h_bias_ref,
        mix_w_ref,
        mix_w_bias_ref,
        unite_ref,
        unite_b_ref,
        ln_gain_ref,
        ln_bias_ref,
        in_ref,
        b_in_ref,
        w_out_ref,
        b_out_ref,
        new_mean_ref,
        new_var_ref,
    ) = outs
    chans = sz.chans
    first_half = (info[1] & 1) == 0

    def take(half, row, rows):
        mine, got = mine_ref[row : row + rows], got_ref[row : row + rows]
        chosen = jnp.where(first_half, mine, got) if half == 0 else jnp.where(first_half, got, mine)
        return chosen.astype(F32)

    mean, var = mean_ref[...], var_ref[...]
    dz = jnp.zeros((1, sz.lanes), F32)
    dzx = jnp.zeros((1, sz.lanes), F32)
    for m in range(close_ref.shape[0]):
        block = close_ref[m]
        mean = 0.9 * mean + 0.1 * block[0:1, :chans]
        var = 0.9 * var + 0.1 * block[1:2, :chans]
        dz = dz + block[2:3]
        dzx = dzx + block[3:4]
    new_mean_ref[...] = mean
    new_var_ref[...] = var
    bias_ref[...] = dz[:, :chans]
    gain_ref[...] = dzx[:, :chans]
    for block in range(sz.hid_blocks):
        lanes = slice(block * LANES, (block + 1) * LANES)
        in_ref[:, lanes] = take(*sz.place(block), chans)
        w_out_ref[:, lanes] = take(*sz.place(sz.hid_blocks + block), chans)
    block = 2 * sz.hid_blocks
    parts = [[] for _ in range(3)]
    for part in range(3):
        for k in range(sz.full):
            parts[part].append(take(*sz.place(block), chans))
            block += 1
    if sz.rest:
        left = jnp.concatenate(
            [take(*sz.place(b), chans) for b in range(block, sz.blocks)], axis=1
        )
        for part in range(3):
            parts[part].append(left[:, part * sz.rest : (part + 1) * sz.rest])
    unite_ref[...] = jnp.concatenate([piece for part in parts for piece in part], axis=1)
    small = take(0, sz.half_blocks * chans, EXTRA)
    count = sz.lanes // LANES

    def joined(first, number, size):
        row = jnp.concatenate([small[first + k : first + k + 1] for k in range(number)], axis=1)
        return row[:, :size]

    unite_b_ref[...] = joined(0, count, chans)
    ln_gain_ref[...] = joined(count, count, chans)
    ln_bias_ref[...] = joined(2 * count, count, chans)
    b_out_ref[...] = joined(3 * count, count, chans)
    first = 4 * count
    b_in_ref[...] = joined(first, sz.hid_blocks, sz.hid)
    first += sz.hid_blocks
    mix_h_bias_ref[...] = small[first : first + 1, : sz.side]
    mix_w_bias_ref[...] = small[first + 1 : first + 2, : sz.side]
    first += 2
    for ref in (mix_h_ref, mix_w_ref):
        for i in range(sz.side):
            ref[i] = small[first + i : first + i + 1, : sz.side]
        first += sz.pad
    taps = taps_got_ref[0]
    for index in range(1, sz.n_dp):
        taps = taps + taps_got_ref[index]
    for p in range(3):
        for q in range(3):
            taps_ref[p, q] = taps[3 * p + q : 3 * p + q + 1, :chans]


def settings(cost):
    return {
        "compiler_params": pltpu.CompilerParams(vmem_limit_bytes=VMEM_BYTES),
        "cost_estimate": pl.CostEstimate(
            flops=0, bytes_accessed=int(cost * 3.0e6), transcendentals=0
        ),
    }


def run_whole(body, outs, info, flat, name, cost):
    def whole(item):
        return pl.BlockSpec(item.shape, lambda step, rank=len(item.shape): (0,) * rank)

    return pl.pallas_call(
        body,
        grid=(1,),
        out_shape=tuple(outs),
        in_specs=[pl.BlockSpec(memory_space=pltpu.SMEM)] + [whole(item) for item in flat],
        out_specs=tuple(whole(item) for item in outs),
        name=name,
        **settings(cost),
    )(info, *flat)


def run(body, outs, info, flat, name, cost, scratch=(), direct=0):
    layers = [item[0] if isinstance(item, tuple) else None for item in flat]
    args, spots, buffers = [], [], []

    def add(item):
        args.append(item)
        return len(args) - 1

    for item in flat:
        held = item[1] if isinstance(item, tuple) else (item,)
        spots.append(
            [tuple(add(one) for one in part) if isinstance(part, tuple) else add(part) for part in held]
        )
        buffers.append(pltpu.VMEM(held[0].shape, held[0].dtype))
    out_buffers = [pltpu.VMEM(item.shape, item.dtype) for item in outs[direct:]]

    def kernel(info_ref, *refs):
        sources, refs = refs[: len(args)], refs[len(args) :]
        targets, refs = refs[: len(outs)], refs[len(outs) :]
        ins_held, refs = refs[: len(buffers)], refs[len(buffers) :]
        outs_held, refs = refs[: len(out_buffers)], refs[len(out_buffers) :]
        in_sems, out_sems = refs[:2]
        picked = []
        for layer, spot in zip(layers, spots):
            found = [
                tuple(sources[one] for one in part) if isinstance(part, tuple) else sources[part]
                for part in spot
            ]
            picked.append(found[0] if layer is None else found)
        ins = Arrivals(
            picked, ins_held, in_sems, lambda layer: info_ref[1] ^ layer, info_ref[2], layers
        )
        held = (None,) * direct + tuple(outs_held)
        departures = Departures(targets, held, out_sems, direct)
        body(info_ref, ins, departures, *refs[2:])
        ins.close()
        departures.close()

    return pl.pallas_call(
        kernel,
        out_shape=tuple(outs),
        in_specs=[pl.BlockSpec(memory_space=pltpu.SMEM)]
        + [pl.BlockSpec(memory_space=pl.ANY) for _ in args],
        out_specs=tuple(pl.BlockSpec(memory_space=pl.ANY) for _ in outs),
        scratch_shapes=buffers
        + out_buffers
        + [pltpu.SemaphoreType.DMA((len(flat), 2)), pltpu.SemaphoreType.DMA((len(outs),))]
        + list(scratch),
        name=name,
        **settings(cost),
    )(info, *args)


def swap(block, axis, size, bit):
    return lax.ppermute(block, axis, [(i, i ^ bit) for i in range(size)])


def tie(first, second):
    first = tuple(first)
    return lax.optimization_barrier(first + tuple(second))[: len(first)]


def add_low(left, right):
    return (left.astype(F32) + right.astype(F32)).astype(BF16)


class Ring:
    def __init__(self, n_dp, n_pipe, dp, core):
        bits = [1 << k for k in range(n_dp.bit_length() - 1)]
        self.orders = (bits, bits[1:] + bits[:1])
        self.steps = len(bits)
        self.n_dp, self.n_pipe, self.dp, self.core = n_dp, n_pipe, dp, core

    def swap(self, block, step):
        route = []
        for d in range(self.n_dp):
            for p in range(self.n_pipe):
                there = d ^ self.orders[p & 1][step]
                route.append((d * self.n_pipe + p, there * self.n_pipe + p))
        return lax.ppermute(block, ("dp", "pipe"), route)

    def upper(self, step):
        bit = jnp.where(self.core == 0, self.orders[0][step], self.orders[1][step])
        return (self.dp & bit) != 0

    def halve(self, block, step):
        side = jnp.where(self.upper(step), 1, 0)
        parts = block.reshape((2, block.shape[0] // 2) + block.shape[1:])
        kept = lax.dynamic_index_in_dim(parts, side, 0, keepdims=False)
        sent = lax.dynamic_index_in_dim(parts, 1 - side, 0, keepdims=False)
        return add_low(kept, self.swap(sent, step))

    def double(self, block, step):
        got = self.swap(block, step)
        side = jnp.where(self.upper(step), 1, 0)
        rows = block.shape[0]
        whole = jnp.zeros((2 * rows,) + block.shape[1:], block.dtype)
        whole = lax.dynamic_update_slice_in_dim(whole, block, side * rows, 0)
        return lax.dynamic_update_slice_in_dim(whole, got, (1 - side) * rows, 0)


def shards(
    images,
    image_counts,
    conv_kernel,
    bn_gain,
    bn_bias,
    mix_h,
    mix_h_bias,
    mix_w,
    mix_w_bias,
    unite_w,
    unite_b,
    ln_gain,
    ln_bias,
    w_in,
    b_in,
    w_out,
    b_out,
    running_mean,
    running_var,
    cotangent,
):
    n_dp, n_pipe = lax.axis_size("dp"), lax.axis_size("pipe")
    dp, pipe = lax.axis_index("dp"), lax.axis_index("pipe")
    layers = n_pipe
    batch = images.shape[0] // n_pipe
    side, chans, hid = images.shape[1], images.shape[3], w_in.shape[2]
    sz = Sizes(batch, side, chans, hid, n_dp)
    core, plane = pipe & 1, pipe >> 1
    tokens = sz.tokens

    def shape(*dims, dtype=F32):
        return jax.ShapeDtypeStruct(dims, dtype)

    valid = jnp.clip(image_counts[0] - pipe * batch, 0, batch).astype(jnp.int32)
    info = jnp.stack([valid, pipe.astype(jnp.int32), (dp & 1).astype(jnp.int32)])

    def to_all(block):
        over = swap(block, "pipe", n_pipe, 2)
        return (block, swap(block, "pipe", n_pipe, 1), over, swap(over, "pipe", n_pipe, 1))

    first_taps = to_all(conv_kernel[0])
    own, own_half, small_own = run_whole(
        functools.partial(prepare_kernel, sz),
        (
            shape(chans, sz.weight_lanes, dtype=BF16),
            shape(chans // 2, sz.weight_lanes, dtype=BF16),
            shape(SMALL_ROWS, sz.lanes),
        ),
        info,
        (
            conv_kernel[0],
            bn_gain,
            bn_bias,
            mix_h[0],
            mix_h_bias,
            mix_w[0],
            mix_w_bias,
            unite_w[0].T,
            unite_b,
            ln_gain,
            ln_bias,
            w_in[0],
            b_in,
            w_out[0].T,
            b_out,
        ),
        "prepare",
        2,
    )
    beside = swap(own, "pipe", n_pipe, 1)

    def across_plane(block, cores):
        return lax.ppermute(block, "pipe", [(p, p ^ 2) for p in cores])

    def to_beside(block, cores):
        return lax.ppermute(block, "pipe", [(p, p ^ 1) for p in cores])

    def to_neighbour(block, cores):
        route = [
            (d * n_pipe + p, (d ^ 1) * n_pipe + p) for d in range(n_dp) for p in cores
        ]
        return lax.ppermute(block, ("dp", "pipe"), route)

    (half_sent,) = tie((own_half,), (first_taps[2],))
    first = across_plane(half_sent, (0, 2))

    def micro(array):
        block = lax.dynamic_slice_in_dim(array, pipe * batch, batch, 0)
        block = jnp.pad(block, ((0, 0), (0, 0), (0, sz.pad - side), (0, 0)))
        return block.reshape(tokens, chans)

    sums_shape = shape(n_dp, 8, LANES)
    plain = shape(tokens, chans)
    low = shape(tokens, chans, dtype=BF16)

    field = micro(images)
    conv, sums = run(
        functools.partial(start_kernel, sz),
        (plain, sums_shape),
        info,
        (field, (0, first_taps)),
        "start",
        2,
    )
    got = lax.all_to_all(sums, "dp", 0, 0)
    (small_own,) = tie((small_own,), (sums,))
    smalls = to_all(small_own)
    (first,) = tie((first,), (sums,))
    first_beside, second = to_beside(first, (0, 2)), to_neighbour(first, (0, 2))
    (second,) = tie((second,), (got,))
    (half_late,) = tie((own_half,), (first_beside, smalls[2]))
    first_odd = across_plane(half_late, (1, 3))
    second_beside = to_beside(second, (0, 2))
    even = (own, beside, (first, second), (first_beside, second_beside))

    fields, convs, saved, stats, weights = [field], [conv], [], [], [even]
    for depth in range(layers - 1):
        if depth:
            got = lax.all_to_all(sums, "dp", 0, 0)
        outs = (
            low,
            shape(tokens, hid, dtype=BF16),
            shape(tokens, hid, dtype=BF16),
            plain,
            shape(tokens, 1),
            shape(tokens, 3 * sz.lanes, dtype=BF16),
            shape(8, sz.lanes),
        )
        flat = (got, convs[depth], (depth, smalls), (depth, weights[depth & 1]), fields[depth])
        outs += (plain, sums_shape)
        flat += ((depth + 1, smalls),)
        results = run(
            functools.partial(forward_kernel, sz, False),
            outs,
            info,
            flat,
            f"layer_{depth}_forward",
            6,
            scratch=[pltpu.SemaphoreType.DMA((2, -(-hid // HID_STEP)))],
        )
        fields.append(results[0])
        if depth == 0:
            (first_odd,) = tie((first_odd,), (second_beside,))
            first_odd_beside = to_beside(first_odd, (1, 3))
            second_odd = to_neighbour(first_odd, (1, 3))
            (second_odd,) = tie((second_odd,), (results[0],))
            second_odd_beside = to_beside(second_odd, (1, 3))
            weights.append(
                (own, beside, (first_odd, second_odd), (first_odd_beside, second_odd_beside))
            )
        saved.append(results[1:6])
        stats.append(results[6])
        convs.append(results[7])
        sums = results[8]

    def to_owners(parts):
        sent = [lax.select_n(pipe ^ bit, *parts) for bit in range(n_pipe)]
        return sent[:1] + [swap(sent[bit], "pipe", n_pipe, bit) for bit in range(1, n_pipe)]

    def collect(parts):
        whole = jnp.zeros((n_pipe, batch, side, side, chans), BF16)
        for bit, part in enumerate(parts):
            part = part.reshape(1, batch, side, sz.pad, chans)[:, :, :, :side]
            whole = lax.dynamic_update_slice(whole, part, (pipe ^ bit, 0, 0, 0, 0))
        return whole.reshape(1, n_pipe * batch, side, side, chans)

    half_shape = shape(sz.half_rows, LANES, dtype=BF16)
    halves, ends = [None] * layers, [None] * 2
    grads, closes = [None] * layers, [None] * layers
    behind = None
    for depth in reversed(range(layers)):
        outs = (half_shape, half_shape, plain, plain, sums_shape)
        packing = [
            pltpu.VMEM((2,) + half_shape.shape, BF16),
            pltpu.VMEM((tokens, hid), BF16),
            pltpu.SemaphoreType.DMA((4,)),
        ]
        if behind is None:
            got = lax.all_to_all(sums, "dp", 0, 0)
            results = run(
                functools.partial(turning_kernel, sz),
                outs + (low, shape(8, sz.lanes)),
                info,
                (got, convs[depth], (depth, smalls), (depth, weights[depth & 1]))
                + (fields[depth], micro(cotangent)),
                f"layer_{depth}_both",
                18,
                scratch=[
                    pltpu.VMEM((tokens, hid), BF16),
                    pltpu.VMEM((tokens, hid), BF16),
                    pltpu.VMEM((tokens, chans), F32),
                    pltpu.VMEM((tokens, 1), F32),
                    pltpu.VMEM((tokens, 3 * sz.lanes), BF16),
                ]
                + packing,
                direct=2,
            )
            fields.append(results[5])
            stats.append(results[6])
        else:
            outs += (low, shape(CLOSE_ROWS, sz.lanes))
            active, slope, unit, spread, joined = saved[depth]
            results = run(
                functools.partial(backward_kernel, sz, False),
                outs,
                info,
                behind
                + ((depth, smalls), (depth, weights[depth & 1]), slope, unit, spread, active)
                + (joined, stats[depth], convs[depth]),
                f"layer_{depth}_backward",
                12,
                scratch=packing,
                direct=2,
            )
        kept, sent, normed_grad, hidden_grad, sums = results[:5]
        if behind is not None:
            grads[depth + 1], closes[depth + 1] = results[5:]
        halves[depth] = add_low(kept, swap(sent, "pipe", n_pipe, 1))
        if depth + 1 == layers:
            (sums,) = tie((sums,), (halves[depth],))
        if depth == 0:
            (sums,) = tie((sums,), (ends[1],))
        if depth < 2:
            mine = jnp.where(plane == 0, halves[depth], halves[depth + 2])
            other = jnp.where(plane == 0, halves[depth + 2], halves[depth])
            ends[depth] = (mine, swap(other, "pipe", n_pipe, 2))
            if depth == 1:
                ends[1] = add_low(*ends[1])
            else:
                (sums,) = tie((sums,), (other,))
        got = lax.all_to_all(sums, "dp", 0, 0)
        (got,) = tie((got,), (halves[depth],))
        behind = (
            got,
            stats[depth],
            (depth, smalls),
            normed_grad,
            convs[depth],
            hidden_grad,
            fields[depth],
        )
    ring = Ring(n_dp, n_pipe, dp, core)
    (odd,), even = tie((ends[1],), (sums,)), add_low(*tie(ends[0], (behind[0],)))
    moves = [functools.partial(ring.halve, step=step) for step in range(ring.steps)]
    moves += [functools.partial(ring.double, step=step) for step in reversed(range(ring.steps))]
    odd_moves, even_moves = iter(moves), iter(moves)
    odd = next(odd_moves)(odd)

    def beside_step(function, *held):
        return function(*tie(held, (even, odd)))

    def step_on(*held):
        nonlocal even, odd
        even = next(even_moves)(even)
        odd_move = next(odd_moves, None)
        odd = odd if odd_move is None else odd_move(odd)
        even, odd, *held = tie((even, odd) + held, ())
        return held

    def end_chain(got):
        return run(
            functools.partial(finish_kernel, sz),
            (low, shape(CLOSE_ROWS, sz.lanes)),
            info,
            (got,) + behind[1:],
            "finish",
            4,
        )

    def add_taps(closing):
        taps = jnp.sum(closing[:, 4:13], axis=0)
        return lax.all_to_all(
            jnp.broadcast_to(taps[None], (n_dp,) + taps.shape), "dp", 0, 0
        )

    grads[0], closes[0] = beside_step(end_chain, behind[0])
    grads[0], closes[0] = step_on(grads[0], closes[0])
    closing = beside_step(
        lambda *held: lax.all_to_all(jnp.stack(held), "pipe", 0, 0), *closes
    )
    (closing,) = step_on(closing)
    output_parts = beside_step(lambda *held: to_owners(held), *fields[1:])
    grad_parts = beside_step(lambda *held: to_owners(held), *grads)
    for _ in range(2, ring.steps):
        step_on()
    taps = beside_step(add_taps, closing)
    for _ in range(2, ring.steps):
        step_on()
    layer_outputs = beside_step(lambda *held: collect(held), *output_parts)
    layer_outputs, taps = step_on(layer_outputs, taps)
    input_grads = beside_step(lambda *held: collect(held), *grad_parts)
    (input_grads,) = step_on(input_grads)
    parts = [odd, even]
    mine = jnp.where(core == 0, parts[1], parts[0])
    other = jnp.where(core == 0, parts[0], parts[1])
    got = swap(other, "pipe", n_pipe, 1)
    row = shape(1, chans)
    outs = (
        shape(3, 3, 1, chans),
        row,
        row,
        shape(side, 1, side),
        shape(1, side),
        shape(side, 1, side),
        shape(1, side),
        shape(chans, 3 * chans),
        row,
        row,
        row,
        shape(chans, hid),
        shape(1, hid),
        shape(chans, hid),
        row,
        row,
        row,
    )
    finished = list(
        run_whole(
            functools.partial(closing_kernel, sz),
            outs,
            info,
            (mine, got, closing, taps, running_mean, running_var),
            "closing",
            4,
        )
    )
    finished[0] = jnp.transpose(finished[0], (2, 0, 1, 3))
    for k in (3, 5):
        finished[k] = jnp.transpose(finished[k], (1, 0, 2))
    for k in (7, 13):
        finished[k] = finished[k].T[None]
    finished[11] = finished[11][None]
    return (layer_outputs, input_grads) + tuple(finished)


def solution(mesh):
    four = P("pipe", None, None, None)
    three = P("pipe", None, None)
    two = P("pipe", None)
    images = P("dp", None, None, None)
    in_specs = (
        images, P("dp"), four, two, two, three, two, three, two, three, two, two, two,
        three, two, three, two, two, two, images,
    )
    stacked = P("pipe", "dp", None, None, None)
    out_specs = (
        stacked, stacked, four, two, two, three, two, three, two, three, two, two, two,
        three, two, three, two, two, two,
    )
    return jax.shard_map(
        shards, mesh=mesh, in_specs=in_specs, out_specs=out_specs, check_vma=False
    )
```

```python
import functools

import jax
import jax.numpy as jnp
from jax import lax
from jax.experimental import pallas as pl
from jax.experimental.pallas import tpu as pltpu
from jax.sharding import PartitionSpec as P

F32 = jnp.float32
BF16 = jnp.bfloat16
LANES = 128
HID_STEP = 1280
ROW_STEP = 64
LN_STEP = 32
VMEM_BYTES = 58 * 1024 * 1024
EXTRA = 128
ROW_BN_GAIN, ROW_BN_BIAS, ROW_UNITE_B, ROW_LN_GAIN, ROW_LN_BIAS, ROW_B_OUT = range(9, 15)
ROW_MIX_BIAS, ROW_B_IN, ROW_MIX = 15, 16, 24
SMALL_ROWS = 40
CLOSE_ROWS = 16
GRAD_ROWS = 64


def wide(value):
    return -(-value // LANES) * LANES


def tall(value):
    return -(-value // 16) * 16


def dot(left, right):
    return lax.dot_general(left, right, (((1,), (0,)), ((), ())), preferred_element_type=F32)


def dot_nt(left, right):
    return lax.dot_general(left, right, (((1,), (1,)), ((), ())), preferred_element_type=F32)


def dot_exact(left, right):
    return lax.dot_general(
        left,
        right,
        (((1,), (0,)), ((), ())),
        preferred_element_type=F32,
        precision=lax.Precision.HIGHEST,
    )


class Sizes:
    def __init__(self, batch, side, chans, hid, n_dp):
        self.batch, self.side, self.chans, self.hid, self.n_dp = batch, side, chans, hid, n_dp
        self.pad = tall(side)
        self.image = side * self.pad
        self.tokens = batch * self.image
        self.lanes = wide(chans)
        self.full = chans // LANES
        self.rest = chans - self.full * LANES
        self.hid_blocks = hid // LANES
        left_blocks = -(-3 * self.rest // LANES)
        self.unite_blocks = 3 * self.full + left_blocks
        self.blocks = 2 * self.hid_blocks + self.unite_blocks
        self.half_blocks = self.blocks // 2
        self.half_rows = self.half_blocks * chans + EXTRA
        self.weight_lanes = 2 * hid + 3 * self.lanes

    def place(self, block):
        half, place = divmod(block, self.half_blocks)
        return half, place * self.chans

    def unite(self, part):
        first = 2 * self.hid + part * self.lanes
        return slice(first, first + self.chans)


def token_mask(sz, valid):
    row = lax.broadcasted_iota(jnp.int32, (sz.tokens, 1), 0)
    return ((row < valid * sz.image) & (row % sz.pad < sz.side)).astype(F32)


def taps_of(sz, small):
    return [small[k : k + 1, : sz.chans] for k in range(9)]


def row_of(sz, small, index):
    return small[index : index + 1, : sz.chans]


def fill_lanes(sz, row):
    if sz.lanes == sz.chans:
        return row
    return jnp.concatenate([row, jnp.zeros((1, sz.lanes - sz.chans), F32)], axis=1)


def lane_rows(sz, row):
    row = fill_lanes(sz, row)
    return [row[:, k * LANES : (k + 1) * LANES] for k in range(sz.lanes // LANES)]


def put_sums(sz, ref, first, second, number):
    pieces = lane_rows(sz, first) + lane_rows(sz, second)
    pieces.append(jnp.zeros((1, LANES), F32) + number)
    pieces.append(jnp.zeros((8 - len(pieces), LANES), F32))
    block = jnp.concatenate(pieces, axis=0)
    for index in range(sz.n_dp):
        ref[index] = block


def take_sums(sz, ref):
    total = ref[0]
    for index in range(1, sz.n_dp):
        total = total + ref[index]
    count = sz.lanes // LANES
    first = jnp.concatenate([total[k : k + 1] for k in range(count)], axis=1)
    second = jnp.concatenate([total[count + k : count + k + 1] for k in range(count)], axis=1)
    return first[:, : sz.chans], second[:, : sz.chans], total[2 * count : 2 * count + 1, 0:1]


def sum_rows(value):
    return jnp.sum(value, axis=0, keepdims=True)


def mean_lanes(value):
    return jnp.mean(value, axis=1, keepdims=True)


def pick_rows(sz):
    row = lax.broadcasted_iota(jnp.int32, (sz.image, sz.pad), 0)
    col = lax.broadcasted_iota(jnp.int32, (sz.image, sz.pad), 1)
    return (row // sz.pad == col), (row % sz.pad == col)


def same_masks(sz):
    row = lax.broadcasted_iota(jnp.int32, (sz.image, sz.image), 0)
    col = lax.broadcasted_iota(jnp.int32, (sz.image, sz.image), 1)
    return (row % sz.pad == col % sz.pad), (row // sz.pad == col // sz.pad)


def mixers(sz, small, turned):
    pick_i, pick_j = pick_rows(sz)
    same_j, same_i = same_masks(sz)
    product = dot_nt if turned else dot
    found = []
    for pick, same, lane in ((pick_i, same_j, 0), (pick_j, same_i, LANES)):
        mix = small[ROW_MIX : ROW_MIX + sz.pad, lane : lane + sz.pad].astype(BF16)
        pick = pick.astype(BF16)
        spread = dot_nt(product(pick, mix).astype(BF16), pick)
        found.append(jnp.where(same, spread, 0.0).astype(BF16))
    return found


class Arrivals:
    def __init__(self, sources, buffers, sems, role_of, bit, layers):
        self.buffers, self.copies = buffers, []
        for k, (source, buffer) in enumerate(zip(sources, buffers)):
            if layers[k] is None:
                copies = [pltpu.make_async_copy(source, buffer, sems.at[k, 0])]
                copies[0].start()
            else:
                halved = isinstance(source[-1], tuple)
                rows = buffer.shape[0] // 2 if halved else buffer.shape[0]
                spots = [pl.ds(0, rows), pl.ds(rows, rows)] if halved else [pl.ds(0, rows)]
                copies = [
                    pltpu.make_async_copy(source[0].at[spot], buffer.at[spot], sems.at[k, h])
                    for h, spot in enumerate(spots)
                ]
                for place, held in enumerate(source):

                    @pl.when(role_of(layers[k]) == place)
                    def _(held=held, buffer=buffer, k=k, spots=spots, rows=rows):
                        for h, spot in enumerate(spots):
                            if isinstance(held, tuple):
                                piece = held[h]
                                at = h ^ bit
                                spot = pl.ds(pl.multiple_of(at * rows, 16), rows)
                            else:
                                piece = held.at[spot]
                            pltpu.make_async_copy(piece, buffer.at[spot], sems.at[k, h]).start()

            self.copies.append(copies)

    def __getitem__(self, k):
        if self.copies[k] is not None:
            for copy in self.copies[k]:
                copy.wait()
            self.copies[k] = None
        return self.buffers[k]

    def close(self):
        for k in range(len(self.copies)):
            self[k]


class Departures:
    def __init__(self, targets, buffers, sems, direct):
        self.buffers, self.targets = buffers, targets
        self.copies = [
            None if k < direct else pltpu.make_async_copy(buffer, target, sems.at[k])
            for k, (target, buffer) in enumerate(zip(targets, buffers))
        ]
        self.started, self.parts = [False] * len(self.copies), []

    def put(self, k, value):
        self.buffers[k][...] = value
        self.send(k)

    def send(self, k):
        self.copies[k].start()
        self.started[k] = True

    def send_part(self, k, lanes, sem):
        spot = (slice(None), lanes)
        copy = pltpu.make_async_copy(self.buffers[k].at[spot], self.targets[k].at[spot], sem)
        copy.start()
        self.parts.append(copy)

    def close(self):
        for copy, started in zip(self.copies, self.started):
            if started:
                copy.wait()
        for copy in self.parts:
            copy.wait()


def prepare_kernel(
    sz,
    info,
    taps_ref,
    bn_gain_ref,
    bn_bias_ref,
    mix_h_ref,
    mix_h_bias_ref,
    mix_w_ref,
    mix_w_bias_ref,
    unite_ref,
    unite_b_ref,
    ln_gain_ref,
    ln_bias_ref,
    in_ref,
    b_in_ref,
    w_out_ref,
    b_out_ref,
    weights_ref,
    half_ref,
    small_ref,
):
    chans, hid = sz.chans, sz.hid
    weights_ref[:, :hid] = in_ref[...]
    weights_ref[:, hid : 2 * hid] = w_out_ref[...]
    gap = jnp.zeros((chans, sz.lanes - chans), BF16)
    for part in range(3):
        first = 2 * hid + part * sz.lanes
        weights_ref[:, first : first + sz.lanes] = jnp.concatenate(
            [unite_ref[:, part * chans : (part + 1) * chans], gap], axis=1
        )
    rows = half_ref.shape[0]
    half_ref[...] = weights_ref[pl.ds(pl.multiple_of(info[2] * rows, 16), rows)]
    small_ref[...] = jnp.zeros(small_ref.shape, F32)
    for p in range(3):
        small_ref[3 * p : 3 * p + 3, :chans] = taps_ref[p].astype(F32)
    rows = (bn_gain_ref, bn_bias_ref, unite_b_ref, ln_gain_ref, ln_bias_ref, b_out_ref)
    for place, ref in zip(range(ROW_BN_GAIN, ROW_MIX_BIAS), rows):
        small_ref[place : place + 1, :chans] = ref[...]
    place = ROW_MIX_BIAS
    small_ref[place : place + 1, : sz.side] = mix_h_bias_ref[...]
    small_ref[place : place + 1, LANES : LANES + sz.side] = mix_w_bias_ref[...]
    for k, lane in enumerate(range(0, hid, sz.lanes)):
        wide_part = min(sz.lanes, hid - lane)
        small_ref[ROW_B_IN + k : ROW_B_IN + k + 1, :wide_part] = b_in_ref[
            :, lane : lane + wide_part
        ]
    rows = slice(ROW_MIX, ROW_MIX + sz.side)
    small_ref[rows, : sz.side] = mix_h_ref[...].astype(F32)
    small_ref[rows, LANES : LANES + sz.side] = mix_w_ref[...].astype(F32)


def steps(size, step):
    return [slice(first, min(first + step, size)) for first in range(0, size, step)]


def fold(value):
    total = value[:8]
    for first in range(8, value.shape[0], 8):
        total = total + value[first : first + 8]
    return total


def conv_rows(sz, rows, taps, back=False):
    order = (2, 1, 0) if back else (0, 1, 2)
    parts = []
    for row in rows:
        near = (pltpu.roll(row, 1, 0), row, pltpu.roll(row, sz.pad - 1, 0))
        near = [near[q] for q in order]
        parts.append(
            [taps[3 * p] * near[0] + taps[3 * p + 1] * near[1] + taps[3 * p + 2] * near[2] for p in order]
        )
    found = []
    for i in range(len(rows)):
        total = parts[i][1]
        if i > 0:
            total = total + parts[i - 1][0]
        if i + 1 < len(rows):
            total = total + parts[i + 1][2]
        found.append(total)
    return found


def next_conv(sz, rows, taps, masks, conv_ref, sums_ref, number):
    first = jnp.zeros((8, sz.chans), F32)
    second = jnp.zeros((8, sz.chans), F32)
    for n in range(sz.batch):
        part = range(n * sz.side, (n + 1) * sz.side)
        for i, conv in zip(part, conv_rows(sz, [rows[i] for i in part], taps)):
            conv_ref[i * sz.pad : (i + 1) * sz.pad] = conv
            masked = masks[i] * conv
            first = first + fold(masked)
            second = second + fold(masked * conv)
    put_sums(sz, sums_ref, sum_rows(first), sum_rows(second), number)


def row_masks(sz, valid):
    mask = token_mask(sz, valid)
    return [mask[i : i + sz.pad] for i in range(0, sz.tokens, sz.pad)]


def start_kernel(sz, info, ins, outs):
    field = ins[0]
    kernel = ins[1]
    taps = [kernel[p, q : q + 1].astype(F32) for p in range(3) for q in range(3)]
    rows = [field[i : i + sz.pad].astype(F32) for i in range(0, sz.tokens, sz.pad)]
    number = (info[0] * (sz.side * sz.side)).astype(F32)
    masks = row_masks(sz, info[0])
    next_conv(sz, rows, taps, masks, outs.buffers[0], outs.buffers[1], number)
    outs.send(0)
    outs.send(1)


def forward_kernel(sz, last, info, ins, outs, part_sems):
    GOT, CONV, SMALL, WEIGHTS, FIELD = range(5)
    OUT, ACTIVE, SLOPE, UNIT, SPREAD, JOINED, STAT, CONV_NEXT, SUMS = range(9)
    small = ins[SMALL]
    total, square, count = take_sums(sz, ins[GOT])
    center = total / count
    variance = square / count - center * center
    inverse = lax.rsqrt(variance + 1e-05)
    stat = [
        fill_lanes(sz, center),
        fill_lanes(sz, inverse),
        fill_lanes(sz, variance * count / (count - 1.0)),
        jnp.zeros((1, sz.lanes), F32) + count,
        jnp.zeros((4, sz.lanes), F32),
    ]
    outs.put(STAT, jnp.concatenate(stat, axis=0))
    gain = inverse * row_of(sz, small, ROW_BN_GAIN)
    shift = row_of(sz, small, ROW_BN_BIAS)
    conv, joined = ins[CONV], outs.buffers[JOINED]
    chans, lanes = sz.chans, sz.lanes
    for rows in steps(sz.tokens, ROW_STEP):
        normed = ((conv[rows] - center) * gain + shift).astype(BF16)
        gap = jnp.zeros((normed.shape[0], lanes - chans), BF16)
        joined[rows, :lanes] = jnp.concatenate([normed, gap], axis=1)
    mix_h, mix_w = mixers(sz, small, False)
    pick_i, pick_j = pick_rows(sz)
    bias = small[ROW_MIX_BIAS : ROW_MIX_BIAS + 1]
    bias_h = jnp.sum(jnp.where(pick_i, bias[:, : sz.pad], 0.0), axis=1, keepdims=True)
    bias_w = jnp.sum(
        jnp.where(pick_j, bias[:, LANES : LANES + sz.pad], 0.0), axis=1, keepdims=True
    )
    for n in range(sz.batch):
        normed = joined[n * sz.image : (n + 1) * sz.image, :lanes]
        for mix, add, place in ((mix_h, bias_h, 1), (mix_w, bias_w, 2)):
            mixed = dot(mix, normed)
            for rows in steps(sz.image, ROW_STEP):
                there = slice(n * sz.image + rows.start, n * sz.image + rows.stop)
                joined[there, place * lanes : (place + 1) * lanes] = (
                    mixed[rows] + add[rows]
                ).astype(BF16)
    outs.send(JOINED)
    weights_ref = ins[WEIGHTS]
    field = ins[FIELD]
    united = dot_nt(joined[...], weights_ref[:, 2 * sz.hid :])
    unite_b = row_of(sz, small, ROW_UNITE_B)
    ln_gain, ln_bias = row_of(sz, small, ROW_LN_GAIN), row_of(sz, small, ROW_LN_BIAS)
    hidden, lnormed = [], []
    for rows in steps(sz.tokens, LN_STEP):
        part = field[rows].astype(F32) + (united[rows] + unite_b)
        offset = part - mean_lanes(part)
        spread = lax.rsqrt(mean_lanes(offset * offset) + 1e-06)
        unit = offset * spread
        outs.buffers[UNIT][rows] = unit
        outs.buffers[SPREAD][rows] = spread
        hidden.append(part)
        lnormed.append((unit * ln_gain + ln_bias).astype(BF16))
    hidden = jnp.concatenate(hidden, axis=0)
    lnormed = jnp.concatenate(lnormed, axis=0)
    outs.send(UNIT)
    outs.send(SPREAD)
    lanes_in = [small[ROW_B_IN + k : ROW_B_IN + k + 1] for k in range(-(-sz.hid // lanes))]
    b_in = jnp.concatenate(lanes_in, axis=1)
    root = 0.7978845608028654
    cubic = 0.044715
    for part in steps(sz.hid, HID_STEP):
        product = dot(lnormed, weights_ref[:, part])
        for rows in steps(sz.tokens, ROW_STEP):
            before = product[rows] + b_in[:, part]
            squared = before * before
            bent = jnp.tanh(before * (root + (root * cubic) * squared))
            half = 0.5 + 0.5 * bent
            active = before * half
            slope = half + (active * (1.0 - bent)) * (root + (3.0 * root * cubic) * squared)
            outs.buffers[ACTIVE][rows, part] = active.astype(BF16)
            outs.buffers[SLOPE][rows, part] = slope.astype(BF16)
        index = part.start // HID_STEP
        if not last:
            outs.send_part(ACTIVE, part, part_sems.at[0, index])
            outs.send_part(SLOPE, part, part_sems.at[1, index])
    branch = dot_nt(outs.buffers[ACTIVE][...], weights_ref[:, sz.hid : 2 * sz.hid])
    masks = row_masks(sz, info[0])
    b_out = row_of(sz, small, ROW_B_OUT)
    results = []
    for i, mask in enumerate(masks):
        rows = slice(i * sz.pad, (i + 1) * sz.pad)
        result = (mask * (hidden[rows] + (branch[rows] + b_out))).astype(BF16)
        outs.buffers[OUT][rows] = result
        results.append(result.astype(F32))
    outs.send(OUT)
    if not last:
        number = (info[0] * (sz.side * sz.side)).astype(F32)
        taps = taps_of(sz, ins[5])
        next_conv(
            sz, results, taps, masks, outs.buffers[CONV_NEXT], outs.buffers[SUMS], number
        )
        outs.send(SUMS)
        outs.send(CONV_NEXT)


def finish_layer(sz, info, ins, outs, first_out):
    GOT, STAT, SMALL, NORMED_GRAD, CONV, HIDDEN_GRAD, FIELD = range(7)
    small, stat = ins[SMALL], ins[STAT]
    chans = sz.chans
    taps = taps_of(sz, small)
    sum_dz, sum_dzx, _ = take_sums(sz, ins[GOT])
    count = stat[3:4, 0:1]
    center, inverse = stat[0:1, :chans], stat[1:2, :chans]
    scale = inverse * row_of(sz, small, ROW_BN_GAIN)
    mean_dz, mean_dzx = sum_dz / count, inverse * (sum_dzx / count)
    normed_grad, conv, hidden_grad, field = (
        ins[k] for k in (NORMED_GRAD, CONV, HIDDEN_GRAD, FIELD)
    )
    masks = row_masks(sz, info[0])
    sums = [jnp.zeros((8, chans), F32) for _ in range(9)]
    grads = []
    for n in range(sz.batch):
        spots = [
            slice(i * sz.pad, (i + 1) * sz.pad) for i in range(n * sz.side, (n + 1) * sz.side)
        ]
        conv_grads = [
            (masks[n * sz.side + i] * scale)
            * (normed_grad[rows] - mean_dz - (conv[rows] - center) * mean_dzx)
            for i, rows in enumerate(spots)
        ]
        for rows, back in zip(spots, conv_rows(sz, conv_grads, taps, back=True)):
            grad = (hidden_grad[rows] + back).astype(BF16)
            outs.buffers[first_out][rows] = grad
            grads.append(grad)
        for i, rows in enumerate(spots):
            row = field[rows].astype(F32)
            near = (pltpu.roll(row, 1, 0), row, pltpu.roll(row, sz.pad - 1, 0))
            for p in range(3):
                there = i + 1 - p
                if 0 <= there < sz.side:
                    for q in range(3):
                        sums[3 * p + q] = sums[3 * p + q] + fold(conv_grads[there] * near[q])
    outs.send(first_out)
    pieces = [center, stat[2:3, :chans], sum_dz, sum_dzx] + [sum_rows(item) for item in sums]
    block = [fill_lanes(sz, piece) for piece in pieces]
    block.append(jnp.zeros((CLOSE_ROWS - len(pieces), sz.lanes), F32))
    outs.put(first_out + 1, jnp.concatenate(block, axis=0))
    return grads


def finish_kernel(sz, info, ins, outs):
    finish_layer(sz, info, ins, outs, 0)


def backward_kernel(sz, first, info, ins, outs, pack_ref, before_ref, pack_sems):
    base = 1 if first else 7
    SMALL, WEIGHTS, SLOPE, UNIT, SPREAD, ACTIVE, JOINED, STAT, CONV = range(base, base + 9)
    core = info[1] & 1
    chans, tokens, lanes = sz.chans, sz.tokens, sz.lanes
    shipped = []

    def put(block, value):
        half, row = sz.place(block)
        pack_ref[half ^ core, row : row + chans] = value

    def ship(half, first_row, rows):
        spot, sem = pl.ds(first_row, rows), pack_sems.at[len(shipped)]
        for place in range(2):

            @pl.when(half ^ core == place)
            def _(place=place):
                pltpu.make_async_copy(
                    pack_ref.at[place, spot], outs.targets[place].at[spot], sem
                ).start()

        shipped.append(
            pltpu.make_async_copy(pack_ref.at[0, spot], outs.targets[0].at[spot], sem)
        )

    if first:
        upstream = [ins[0][i : i + sz.pad] for i in range(0, tokens, sz.pad)]
    else:
        upstream = finish_layer(sz, info, ins, outs, 5)
    small = ins[SMALL]
    masks = row_masks(sz, info[0])
    out_grads = [mask * grad.astype(F32) for mask, grad in zip(masks, upstream)]
    branch_grad = jnp.concatenate([item.astype(BF16) for item in out_grads], axis=0)
    out_sum = fold(out_grads[0])
    for item in out_grads[1:]:
        out_sum = out_sum + fold(item)
    out_grads = jnp.concatenate(out_grads, axis=0)
    unit = ins[UNIT]
    ln_gain, ln_bias = row_of(sz, small, ROW_LN_GAIN), row_of(sz, small, ROW_LN_BIAS)
    lnormed = [
        (unit[rows] * ln_gain + ln_bias).astype(BF16) for rows in steps(tokens, ROW_STEP)
    ]
    lnormed = jnp.concatenate(lnormed, axis=0)
    turned_ln = jnp.concatenate([lnormed.T, jnp.ones((16, tokens), BF16)], axis=0)
    turned_branch = branch_grad.T
    weights_ref, slope_ref, active_ref = ins[WEIGHTS], ins[SLOPE], ins[ACTIVE]
    in_pieces = []
    for k in range(0, sz.hid, HID_STEP):
        part = slice(k, k + HID_STEP)
        active_grad = dot(branch_grad, weights_ref[:, sz.hid + k : sz.hid + k + HID_STEP])
        for rows in steps(tokens, ROW_STEP):
            before_ref[rows, part] = (
                active_grad[rows] * slope_ref[rows, part].astype(F32)
            ).astype(BF16)
        grad_in = dot(turned_ln, before_ref[:, part])
        grad_out = dot(turned_branch, active_ref[:, part])
        for lane in range(0, HID_STEP, LANES):
            block = (k + lane) // LANES
            put(block, grad_in[:chans, lane : lane + LANES].astype(BF16))
            put(sz.hid_blocks + block, grad_out[:, lane : lane + LANES].astype(BF16))
            in_pieces.append(grad_in[chans : chans + 1, lane : lane + LANES])
    norm_grad = dot_nt(before_ref[...], weights_ref[:, : sz.hid])
    ship(0, 0, sz.half_blocks * chans)
    spread = ins[SPREAD]
    token_grad = []
    token_sum, gain_sum, bias_sum = (jnp.zeros((8, chans), F32) for _ in range(3))
    for rows in steps(tokens, LN_STEP):
        grad, part = norm_grad[rows], unit[rows]
        product = grad * part
        gain_sum = gain_sum + fold(product)
        bias_sum = bias_sum + fold(grad)
        scaled = grad * ln_gain
        hidden_grad = out_grads[rows] + spread[rows] * (
            scaled - mean_lanes(scaled) - part * mean_lanes(product * ln_gain)
        )
        outs.buffers[3][rows] = hidden_grad
        token = hidden_grad.astype(BF16)
        token_grad.append(token)
        token_sum = token_sum + fold(token.astype(F32))
    token_grad = jnp.concatenate(token_grad, axis=0)
    outs.send(3)
    joined = ins[JOINED]
    joined_grad = dot(token_grad, weights_ref[:, 2 * sz.hid :])
    rows_grad = joined_grad[:, lanes : lanes + chans].astype(BF16)
    cols_grad = joined_grad[:, 2 * lanes : 2 * lanes + chans].astype(BF16)
    turned_h, turned_w = mixers(sz, small, True)
    stat, conv = ins[STAT], ins[CONV]
    center, inverse = stat[0:1, :chans], stat[1:2, :chans]
    sum_dz, sum_dzx = (jnp.zeros((8, chans), F32) for _ in range(2))
    for n in range(sz.batch):
        image = slice(n * sz.image, (n + 1) * sz.image)
        back_h = dot(turned_h, rows_grad[image])
        back_w = dot(turned_w, cols_grad[image])
        for rows in steps(sz.image, ROW_STEP):
            there = slice(image.start + rows.start, image.start + rows.stop)
            normed_grad = joined_grad[there, :chans] + (back_h[rows] + back_w[rows])
            outs.buffers[2][there] = normed_grad
            sum_dz = sum_dz + fold(normed_grad)
            sum_dzx = sum_dzx + fold(normed_grad * ((conv[there] - center) * inverse))
    put_sums(sz, outs.buffers[4], sum_rows(sum_dz), sum_rows(sum_dzx), 0.0)
    outs.send(4)
    outs.send(2)
    grad_unite = dot(token_grad.T, joined[...]).astype(BF16)
    block = 2 * sz.hid_blocks
    leftovers = []
    for part in range(3):
        for k in range(sz.full):
            lane = part * lanes + k * LANES
            put(block, grad_unite[:, lane : lane + LANES])
            block += 1
        if sz.rest:
            lane = part * lanes + sz.full * LANES
            leftovers.append(grad_unite[:, lane : lane + sz.rest])
    if sz.rest:
        left = jnp.concatenate(leftovers, axis=1)
        fill = wide(left.shape[1]) - left.shape[1]
        if fill:
            left = jnp.concatenate([left, jnp.zeros((chans, fill), BF16)], axis=1)
        for lane in range(0, left.shape[1], LANES):
            put(block, left[:, lane : lane + LANES])
            block += 1
    ship(1, 0, sz.half_blocks * chans)
    pick_i, pick_j = pick_rows(sz)
    same_j, same_i = same_masks(sz)
    mix_pieces, bias_pieces = [], []
    for grads, pick, same in ((rows_grad, pick_i, same_j), (cols_grad, pick_j, same_i)):
        pairs = jnp.zeros((sz.image, sz.image), F32)
        sums = jnp.zeros((sz.image, 1), F32)
        for n in range(sz.batch):
            image = slice(n * sz.image, (n + 1) * sz.image)
            pairs = pairs + dot_nt(grads[image], joined[image, :chans])
            sums = sums + jnp.sum(grads[image].astype(F32), axis=1, keepdims=True)
        pairs = jnp.where(same, pairs, 0.0)
        picked = pick.astype(F32)
        groups = [pairs[i : i + sz.pad] for i in range(0, sz.image, sz.pad)]
        if pick is pick_i:
            near = [sum_rows(group) for group in groups]
            near.append(jnp.zeros((sz.pad - sz.side, sz.image), F32))
            near = jnp.concatenate(near, axis=0)
        else:
            near = groups[0]
            for group in groups[1:]:
                near = near + group
        small_grad = dot_exact(near, picked)
        gap = LANES - sz.pad
        mix_pieces.append(
            jnp.concatenate([small_grad, jnp.zeros((sz.pad, gap), F32)], axis=1)
        )
        bias_pieces.append(
            jnp.concatenate([sum_rows(picked * sums), jnp.zeros((1, gap), F32)], axis=1)
        )
    pieces = (
        lane_rows(sz, sum_rows(token_sum))
        + lane_rows(sz, sum_rows(gain_sum))
        + lane_rows(sz, sum_rows(bias_sum))
        + lane_rows(sz, sum_rows(out_sum))
        + in_pieces
        + bias_pieces
        + mix_pieces
    )
    used = sum(piece.shape[0] for piece in pieces)
    pieces.append(jnp.zeros((EXTRA - used, LANES), F32))
    place = sz.half_blocks * chans
    pack_ref[core, place : place + EXTRA] = jnp.concatenate(pieces, axis=0).astype(BF16)
    pack_ref[1 - core, place : place + EXTRA] = jnp.zeros((EXTRA, LANES), BF16)
    ship(0, place, EXTRA)
    ship(1, place, EXTRA)
    for copy in shipped:
        copy.wait()


class Inner:
    def __init__(self, outs, places):
        leaves = [isinstance(place, int) for place in places]
        self.outs, self.places, self.leaves = outs, places, leaves
        self.buffers = [
            outs.buffers[place] if leave else place for place, leave in zip(places, leaves)
        ]

    def put(self, k, value):
        self.buffers[k][...] = value
        self.send(k)

    def send(self, k):
        if self.leaves[k]:
            self.outs.send(self.places[k])

    def send_part(self, k, part, sem):
        pass


class Inputs:
    def __init__(self, ins, places):
        self.ins, self.places = ins, places

    def __getitem__(self, k):
        place = self.places[k]
        return self.ins[place] if isinstance(place, int) else place


def turning_kernel(sz, info, ins, outs, active, slope, unit, spread, joined, *scratch):
    GOT, CONV, SMALL, WEIGHTS, FIELD, UPSTREAM = range(6)
    forward = Inner(outs, [5, active, slope, unit, spread, joined, 6])
    forward_kernel(sz, True, info, ins, forward, None)
    held = [UPSTREAM, SMALL, WEIGHTS, slope, unit, spread, active, joined]
    held += [outs.buffers[6], CONV]
    backward_kernel(sz, True, info, Inputs(ins, held), outs, *scratch)


def closing_kernel(sz, info, mine_ref, got_ref, close_ref, taps_got_ref, mean_ref, var_ref, *outs):
    (
        taps_ref,
        gain_ref,
        bias_ref,
        mix_h_ref,
        mix_h_bias_ref,
        mix_w_ref,
        mix_w_bias_ref,
        unite_ref,
        unite_b_ref,
        ln_gain_ref,
        ln_bias_ref,
        in_ref,
        b_in_ref,
        w_out_ref,
        b_out_ref,
        new_mean_ref,
        new_var_ref,
    ) = outs
    chans = sz.chans
    first_half = (info[1] & 1) == 0

    def take(half, row, rows):
        mine, got = mine_ref[row : row + rows], got_ref[row : row + rows]
        chosen = jnp.where(first_half, mine, got) if half == 0 else jnp.where(first_half, got, mine)
        return chosen.astype(F32)

    mean, var = mean_ref[...], var_ref[...]
    dz = jnp.zeros((1, sz.lanes), F32)
    dzx = jnp.zeros((1, sz.lanes), F32)
    for m in range(close_ref.shape[0]):
        block = close_ref[m]
        mean = 0.9 * mean + 0.1 * block[0:1, :chans]
        var = 0.9 * var + 0.1 * block[1:2, :chans]
        dz = dz + block[2:3]
        dzx = dzx + block[3:4]
    new_mean_ref[...] = mean
    new_var_ref[...] = var
    bias_ref[...] = dz[:, :chans]
    gain_ref[...] = dzx[:, :chans]
    for block in range(sz.hid_blocks):
        lanes = slice(block * LANES, (block + 1) * LANES)
        in_ref[:, lanes] = take(*sz.place(block), chans)
        w_out_ref[:, lanes] = take(*sz.place(sz.hid_blocks + block), chans)
    block = 2 * sz.hid_blocks
    parts = [[] for _ in range(3)]
    for part in range(3):
        for k in range(sz.full):
            parts[part].append(take(*sz.place(block), chans))
            block += 1
    if sz.rest:
        left = jnp.concatenate(
            [take(*sz.place(b), chans) for b in range(block, sz.blocks)], axis=1
        )
        for part in range(3):
            parts[part].append(left[:, part * sz.rest : (part + 1) * sz.rest])
    unite_ref[...] = jnp.concatenate([piece for part in parts for piece in part], axis=1)
    small = take(0, sz.half_blocks * chans, EXTRA)
    count = sz.lanes // LANES

    def joined(first, number, size):
        row = jnp.concatenate([small[first + k : first + k + 1] for k in range(number)], axis=1)
        return row[:, :size]

    unite_b_ref[...] = joined(0, count, chans)
    ln_gain_ref[...] = joined(count, count, chans)
    ln_bias_ref[...] = joined(2 * count, count, chans)
    b_out_ref[...] = joined(3 * count, count, chans)
    first = 4 * count
    b_in_ref[...] = joined(first, sz.hid_blocks, sz.hid)
    first += sz.hid_blocks
    mix_h_bias_ref[...] = small[first : first + 1, : sz.side]
    mix_w_bias_ref[...] = small[first + 1 : first + 2, : sz.side]
    first += 2
    for ref in (mix_h_ref, mix_w_ref):
        for i in range(sz.side):
            ref[i] = small[first + i : first + i + 1, : sz.side]
        first += sz.pad
    taps = taps_got_ref[0]
    for index in range(1, sz.n_dp):
        taps = taps + taps_got_ref[index]
    for p in range(3):
        for q in range(3):
            taps_ref[p, q] = taps[3 * p + q : 3 * p + q + 1, :chans]


def settings(cost):
    return {
        "compiler_params": pltpu.CompilerParams(vmem_limit_bytes=VMEM_BYTES),
        "cost_estimate": pl.CostEstimate(
            flops=0, bytes_accessed=int(cost * 3.0e6), transcendentals=0
        ),
    }


def run_whole(body, outs, info, flat, name, cost):
    def whole(item):
        return pl.BlockSpec(item.shape, lambda step, rank=len(item.shape): (0,) * rank)

    return pl.pallas_call(
        body,
        grid=(1,),
        out_shape=tuple(outs),
        in_specs=[pl.BlockSpec(memory_space=pltpu.SMEM)] + [whole(item) for item in flat],
        out_specs=tuple(whole(item) for item in outs),
        name=name,
        **settings(cost),
    )(info, *flat)


def run(body, outs, info, flat, name, cost, scratch=(), direct=0):
    layers = [item[0] if isinstance(item, tuple) else None for item in flat]
    args, spots, buffers = [], [], []

    def add(item):
        args.append(item)
        return len(args) - 1

    for item in flat:
        held = item[1] if isinstance(item, tuple) else (item,)
        spots.append(
            [tuple(add(one) for one in part) if isinstance(part, tuple) else add(part) for part in held]
        )
        buffers.append(pltpu.VMEM(held[0].shape, held[0].dtype))
    out_buffers = [pltpu.VMEM(item.shape, item.dtype) for item in outs[direct:]]

    def kernel(info_ref, *refs):
        sources, refs = refs[: len(args)], refs[len(args) :]
        targets, refs = refs[: len(outs)], refs[len(outs) :]
        ins_held, refs = refs[: len(buffers)], refs[len(buffers) :]
        outs_held, refs = refs[: len(out_buffers)], refs[len(out_buffers) :]
        in_sems, out_sems = refs[:2]
        picked = []
        for layer, spot in zip(layers, spots):
            found = [
                tuple(sources[one] for one in part) if isinstance(part, tuple) else sources[part]
                for part in spot
            ]
            picked.append(found[0] if layer is None else found)
        ins = Arrivals(
            picked, ins_held, in_sems, lambda layer: info_ref[1] ^ layer, info_ref[2], layers
        )
        held = (None,) * direct + tuple(outs_held)
        departures = Departures(targets, held, out_sems, direct)
        body(info_ref, ins, departures, *refs[2:])
        ins.close()
        departures.close()

    return pl.pallas_call(
        kernel,
        out_shape=tuple(outs),
        in_specs=[pl.BlockSpec(memory_space=pltpu.SMEM)]
        + [pl.BlockSpec(memory_space=pl.ANY) for _ in args],
        out_specs=tuple(pl.BlockSpec(memory_space=pl.ANY) for _ in outs),
        scratch_shapes=buffers
        + out_buffers
        + [pltpu.SemaphoreType.DMA((len(flat), 2)), pltpu.SemaphoreType.DMA((len(outs),))]
        + list(scratch),
        name=name,
        **settings(cost),
    )(info, *args)


def swap(block, axis, size, bit):
    return lax.ppermute(block, axis, [(i, i ^ bit) for i in range(size)])


def tie(first, second):
    first = tuple(first)
    return lax.optimization_barrier(first + tuple(second))[: len(first)]


def add_low(left, right):
    return (left.astype(F32) + right.astype(F32)).astype(BF16)


class Ring:
    def __init__(self, n_dp, n_pipe, dp, core):
        bits = [1 << k for k in range(n_dp.bit_length() - 1)]
        self.orders = (bits, bits[1:] + bits[:1])
        self.steps = len(bits)
        self.n_dp, self.n_pipe, self.dp, self.core = n_dp, n_pipe, dp, core

    def swap(self, block, step):
        route = []
        for d in range(self.n_dp):
            for p in range(self.n_pipe):
                there = d ^ self.orders[p & 1][step]
                route.append((d * self.n_pipe + p, there * self.n_pipe + p))
        return lax.ppermute(block, ("dp", "pipe"), route)

    def upper(self, step):
        bit = jnp.where(self.core == 0, self.orders[0][step], self.orders[1][step])
        return (self.dp & bit) != 0

    def halve(self, block, step):
        side = jnp.where(self.upper(step), 1, 0)
        parts = block.reshape((2, block.shape[0] // 2) + block.shape[1:])
        kept = lax.dynamic_index_in_dim(parts, side, 0, keepdims=False)
        sent = lax.dynamic_index_in_dim(parts, 1 - side, 0, keepdims=False)
        return add_low(kept, self.swap(sent, step))

    def double(self, block, step):
        got = self.swap(block, step)
        side = jnp.where(self.upper(step), 1, 0)
        rows = block.shape[0]
        whole = jnp.zeros((2 * rows,) + block.shape[1:], block.dtype)
        whole = lax.dynamic_update_slice_in_dim(whole, block, side * rows, 0)
        return lax.dynamic_update_slice_in_dim(whole, got, (1 - side) * rows, 0)


def shards(
    images,
    image_counts,
    conv_kernel,
    bn_gain,
    bn_bias,
    mix_h,
    mix_h_bias,
    mix_w,
    mix_w_bias,
    unite_w,
    unite_b,
    ln_gain,
    ln_bias,
    w_in,
    b_in,
    w_out,
    b_out,
    running_mean,
    running_var,
    cotangent,
):
    n_dp, n_pipe = lax.axis_size("dp"), lax.axis_size("pipe")
    dp, pipe = lax.axis_index("dp"), lax.axis_index("pipe")
    layers = n_pipe
    batch = images.shape[0] // n_pipe
    side, chans, hid = images.shape[1], images.shape[3], w_in.shape[2]
    sz = Sizes(batch, side, chans, hid, n_dp)
    core, plane = pipe & 1, pipe >> 1
    tokens = sz.tokens

    def shape(*dims, dtype=F32):
        return jax.ShapeDtypeStruct(dims, dtype)

    valid = jnp.clip(image_counts[0] - pipe * batch, 0, batch).astype(jnp.int32)
    info = jnp.stack([valid, pipe.astype(jnp.int32), (dp & 1).astype(jnp.int32)])

    def to_all(block):
        over = swap(block, "pipe", n_pipe, 2)
        return (block, swap(block, "pipe", n_pipe, 1), over, swap(over, "pipe", n_pipe, 1))

    first_taps = to_all(conv_kernel[0])
    own, own_half, small_own = run_whole(
        functools.partial(prepare_kernel, sz),
        (
            shape(chans, sz.weight_lanes, dtype=BF16),
            shape(chans // 2, sz.weight_lanes, dtype=BF16),
            shape(SMALL_ROWS, sz.lanes),
        ),
        info,
        (
            conv_kernel[0],
            bn_gain,
            bn_bias,
            mix_h[0],
            mix_h_bias,
            mix_w[0],
            mix_w_bias,
            unite_w[0].T,
            unite_b,
            ln_gain,
            ln_bias,
            w_in[0],
            b_in,
            w_out[0].T,
            b_out,
        ),
        "prepare",
        2,
    )
    beside = swap(own, "pipe", n_pipe, 1)

    def across_plane(block, cores):
        return lax.ppermute(block, "pipe", [(p, p ^ 2) for p in cores])

    def to_beside(block, cores):
        return lax.ppermute(block, "pipe", [(p, p ^ 1) for p in cores])

    def to_neighbour(block, cores):
        route = [
            (d * n_pipe + p, (d ^ 1) * n_pipe + p) for d in range(n_dp) for p in cores
        ]
        return lax.ppermute(block, ("dp", "pipe"), route)

    (half_sent,) = tie((own_half,), (first_taps[2],))
    first = across_plane(half_sent, (0, 2))

    def micro(array):
        block = lax.dynamic_slice_in_dim(array, pipe * batch, batch, 0)
        block = jnp.pad(block, ((0, 0), (0, 0), (0, sz.pad - side), (0, 0)))
        return block.reshape(tokens, chans)

    sums_shape = shape(n_dp, 8, LANES)
    plain = shape(tokens, chans)
    low = shape(tokens, chans, dtype=BF16)

    field = micro(images)
    conv, sums = run(
        functools.partial(start_kernel, sz),
        (plain, sums_shape),
        info,
        (field, (0, first_taps)),
        "start",
        2,
    )
    got = lax.all_to_all(sums, "dp", 0, 0)
    (small_own,) = tie((small_own,), (sums,))
    smalls = to_all(small_own)
    (first,) = tie((first,), (sums,))
    first_beside, second = to_beside(first, (0, 2)), to_neighbour(first, (0, 2))
    (second,) = tie((second,), (got,))
    (half_late,) = tie((own_half,), (first_beside, smalls[2]))
    first_odd = across_plane(half_late, (1, 3))
    second_beside = to_beside(second, (0, 2))
    even = (own, beside, (first, second), (first_beside, second_beside))

    fields, convs, saved, stats, weights = [field], [conv], [], [], [even]
    for depth in range(layers - 1):
        if depth:
            got = lax.all_to_all(sums, "dp", 0, 0)
        outs = (
            low,
            shape(tokens, hid, dtype=BF16),
            shape(tokens, hid, dtype=BF16),
            plain,
            shape(tokens, 1),
            shape(tokens, 3 * sz.lanes, dtype=BF16),
            shape(8, sz.lanes),
        )
        flat = (got, convs[depth], (depth, smalls), (depth, weights[depth & 1]), fields[depth])
        outs += (plain, sums_shape)
        flat += ((depth + 1, smalls),)
        results = run(
            functools.partial(forward_kernel, sz, False),
            outs,
            info,
            flat,
            f"layer_{depth}_forward",
            6,
            scratch=[pltpu.SemaphoreType.DMA((2, -(-hid // HID_STEP)))],
        )
        fields.append(results[0])
        if depth == 0:
            (first_odd,) = tie((first_odd,), (second_beside,))
            first_odd_beside = to_beside(first_odd, (1, 3))
            second_odd = to_neighbour(first_odd, (1, 3))
            (second_odd,) = tie((second_odd,), (results[0],))
            second_odd_beside = to_beside(second_odd, (1, 3))
            weights.append(
                (own, beside, (first_odd, second_odd), (first_odd_beside, second_odd_beside))
            )
        saved.append(results[1:6])
        stats.append(results[6])
        convs.append(results[7])
        sums = results[8]

    def to_owners(parts):
        sent = [lax.select_n(pipe ^ bit, *parts) for bit in range(n_pipe)]
        return sent[:1] + [swap(sent[bit], "pipe", n_pipe, bit) for bit in range(1, n_pipe)]

    def collect(parts):
        whole = jnp.zeros((n_pipe, batch, side, side, chans), BF16)
        for bit, part in enumerate(parts):
            part = part.reshape(1, batch, side, sz.pad, chans)[:, :, :, :side]
            whole = lax.dynamic_update_slice(whole, part, (pipe ^ bit, 0, 0, 0, 0))
        return whole.reshape(1, n_pipe * batch, side, side, chans)

    half_shape = shape(sz.half_rows, LANES, dtype=BF16)
    halves, ends = [None] * layers, [None] * 2
    grads, closes = [None] * layers, [None] * layers
    behind = None
    for depth in reversed(range(layers)):
        outs = (half_shape, half_shape, plain, plain, sums_shape)
        packing = [
            pltpu.VMEM((2,) + half_shape.shape, BF16),
            pltpu.VMEM((tokens, hid), BF16),
            pltpu.SemaphoreType.DMA((4,)),
        ]
        if behind is None:
            got = lax.all_to_all(sums, "dp", 0, 0)
            results = run(
                functools.partial(turning_kernel, sz),
                outs + (low, shape(8, sz.lanes)),
                info,
                (got, convs[depth], (depth, smalls), (depth, weights[depth & 1]))
                + (fields[depth], micro(cotangent)),
                f"layer_{depth}_both",
                18,
                scratch=[
                    pltpu.VMEM((tokens, hid), BF16),
                    pltpu.VMEM((tokens, hid), BF16),
                    pltpu.VMEM((tokens, chans), F32),
                    pltpu.VMEM((tokens, 1), F32),
                    pltpu.VMEM((tokens, 3 * sz.lanes), BF16),
                ]
                + packing,
                direct=2,
            )
            fields.append(results[5])
            stats.append(results[6])
        else:
            outs += (low, shape(CLOSE_ROWS, sz.lanes))
            active, slope, unit, spread, joined = saved[depth]
            results = run(
                functools.partial(backward_kernel, sz, False),
                outs,
                info,
                behind
                + ((depth, smalls), (depth, weights[depth & 1]), slope, unit, spread, active)
                + (joined, stats[depth], convs[depth]),
                f"layer_{depth}_backward",
                12,
                scratch=packing,
                direct=2,
            )
        kept, sent, normed_grad, hidden_grad, sums = results[:5]
        if behind is not None:
            grads[depth + 1], closes[depth + 1] = results[5:]
        halves[depth] = add_low(kept, swap(sent, "pipe", n_pipe, 1))
        if depth + 1 == layers:
            (sums,) = tie((sums,), (halves[depth],))
        if depth == 0:
            (sums,) = tie((sums,), (ends[1],))
        if depth < 2:
            mine = jnp.where(plane == 0, halves[depth], halves[depth + 2])
            other = jnp.where(plane == 0, halves[depth + 2], halves[depth])
            ends[depth] = (mine, swap(other, "pipe", n_pipe, 2))
            if depth == 1:
                ends[1] = add_low(*ends[1])
            else:
                (sums,) = tie((sums,), (other,))
        got = lax.all_to_all(sums, "dp", 0, 0)
        (got,) = tie((got,), (halves[depth],))
        behind = (
            got,
            stats[depth],
            (depth, smalls),
            normed_grad,
            convs[depth],
            hidden_grad,
            fields[depth],
        )
    ring = Ring(n_dp, n_pipe, dp, core)
    (odd,), even = tie((ends[1],), (sums,)), add_low(*tie(ends[0], (behind[0],)))
    moves = [functools.partial(ring.halve, step=step) for step in range(ring.steps)]
    moves += [functools.partial(ring.double, step=step) for step in reversed(range(ring.steps))]
    odd_moves, even_moves = iter(moves), iter(moves)
    odd = next(odd_moves)(odd)

    def beside_step(function, *held):
        return function(*tie(held, (even, odd)))

    def step_on(*held):
        nonlocal even, odd
        even = next(even_moves)(even)
        odd_move = next(odd_moves, None)
        odd = odd if odd_move is None else odd_move(odd)
        even, odd, *held = tie((even, odd) + held, ())
        return held

    def end_chain(got):
        return run(
            functools.partial(finish_kernel, sz),
            (low, shape(CLOSE_ROWS, sz.lanes)),
            info,
            (got,) + behind[1:],
            "finish",
            4,
        )

    def add_taps(closing):
        taps = jnp.sum(closing[:, 4:13], axis=0)
        return lax.all_to_all(
            jnp.broadcast_to(taps[None], (n_dp,) + taps.shape), "dp", 0, 0
        )

    grads[0], closes[0] = beside_step(end_chain, behind[0])
    grads[0], closes[0] = step_on(grads[0], closes[0])
    closing = beside_step(
        lambda *held: lax.all_to_all(jnp.stack(held), "pipe", 0, 0), *closes
    )
    (closing,) = step_on(closing)
    output_parts = beside_step(lambda *held: to_owners(held), *fields[1:])
    grad_parts = beside_step(lambda *held: to_owners(held), *grads)
    for _ in range(2, ring.steps):
        step_on()
    taps = beside_step(add_taps, closing)
    for _ in range(2, ring.steps):
        step_on()
    layer_outputs = beside_step(lambda *held: collect(held), *output_parts)
    layer_outputs, taps = step_on(layer_outputs, taps)
    input_grads = beside_step(lambda *held: collect(held), *grad_parts)
    (input_grads,) = step_on(input_grads)
    parts = [odd, even]
    mine = jnp.where(core == 0, parts[1], parts[0])
    other = jnp.where(core == 0, parts[0], parts[1])
    got = swap(other, "pipe", n_pipe, 1)
    row = shape(1, chans)
    outs = (
        shape(3, 3, 1, chans),
        row,
        row,
        shape(side, 1, side),
        shape(1, side),
        shape(side, 1, side),
        shape(1, side),
        shape(chans, 3 * chans),
        row,
        row,
        row,
        shape(chans, hid),
        shape(1, hid),
        shape(chans, hid),
        row,
        row,
        row,
    )
    finished = list(
        run_whole(
            functools.partial(closing_kernel, sz),
            outs,
            info,
            (mine, got, closing, taps, running_mean, running_var),
            "closing",
            4,
        )
    )
    finished[0] = jnp.transpose(finished[0], (2, 0, 1, 3))
    for k in (3, 5):
        finished[k] = jnp.transpose(finished[k], (1, 0, 2))
    for k in (7, 13):
        finished[k] = finished[k].T[None]
    finished[11] = finished[11][None]
    return (layer_outputs, input_grads) + tuple(finished)


def solution(mesh):
    four = P("pipe", None, None, None)
    three = P("pipe", None, None)
    two = P("pipe", None)
    images = P("dp", None, None, None)
    in_specs = (
        images, P("dp"), four, two, two, three, two, three, two, three, two, two, two,
        three, two, three, two, two, two, images,
    )
    stacked = P("pipe", "dp", None, None, None)
    out_specs = (
        stacked, stacked, four, two, two, three, two, three, two, three, two, two, two,
        three, two, three, two, two, two,
    )
    return jax.shard_map(
        shards, mesh=mesh, in_specs=in_specs, out_specs=out_specs, check_vma=False
    )
```

```python
import functools

import jax
import jax.numpy as jnp
from jax import lax
from jax.experimental import pallas as pl
from jax.experimental.pallas import tpu as pltpu
from jax.sharding import PartitionSpec as P

F32 = jnp.float32
BF16 = jnp.bfloat16
LANES = 128
HID_STEP = 640
ROW_STEP = 64
LN_STEP = 32
VMEM_BYTES = 58 * 1024 * 1024
EXTRA = 128
ROW_BN_GAIN, ROW_BN_BIAS, ROW_UNITE_B, ROW_LN_GAIN, ROW_LN_BIAS, ROW_B_OUT = range(9, 15)
ROW_MIX_BIAS, ROW_B_IN, ROW_MIX = 15, 16, 24
SMALL_ROWS = 40
CLOSE_ROWS = 16
GRAD_ROWS = 64


def wide(value):
    return -(-value // LANES) * LANES


def tall(value):
    return -(-value // 16) * 16


def dot(left, right):
    return lax.dot_general(left, right, (((1,), (0,)), ((), ())), preferred_element_type=F32)


def dot_nt(left, right):
    return lax.dot_general(left, right, (((1,), (1,)), ((), ())), preferred_element_type=F32)


def dot_exact(left, right):
    return lax.dot_general(
        left,
        right,
        (((1,), (0,)), ((), ())),
        preferred_element_type=F32,
        precision=lax.Precision.HIGHEST,
    )


class Sizes:
    def __init__(self, batch, side, chans, hid, n_dp):
        self.batch, self.side, self.chans, self.hid, self.n_dp = batch, side, chans, hid, n_dp
        self.pad = tall(side)
        self.image = side * self.pad
        self.tokens = batch * self.image
        self.lanes = wide(chans)
        self.full = chans // LANES
        self.rest = chans - self.full * LANES
        self.hid_blocks = hid // LANES
        left_blocks = -(-3 * self.rest // LANES)
        self.unite_blocks = 3 * self.full + left_blocks
        self.blocks = 2 * self.hid_blocks + self.unite_blocks
        self.half_blocks = self.blocks // 2
        self.half_rows = self.half_blocks * chans + EXTRA
        self.weight_lanes = 2 * hid + 3 * self.lanes

    def place(self, block):
        half, place = divmod(block, self.half_blocks)
        return half, place * self.chans

    def unite(self, part):
        first = 2 * self.hid + part * self.lanes
        return slice(first, first + self.chans)


def token_mask(sz, valid):
    row = lax.broadcasted_iota(jnp.int32, (sz.tokens, 1), 0)
    return ((row < valid * sz.image) & (row % sz.pad < sz.side)).astype(F32)


def taps_of(sz, small):
    return [small[k : k + 1, : sz.chans] for k in range(9)]


def row_of(sz, small, index):
    return small[index : index + 1, : sz.chans]


def fill_lanes(sz, row):
    if sz.lanes == sz.chans:
        return row
    return jnp.concatenate([row, jnp.zeros((1, sz.lanes - sz.chans), F32)], axis=1)


def lane_rows(sz, row):
    row = fill_lanes(sz, row)
    return [row[:, k * LANES : (k + 1) * LANES] for k in range(sz.lanes // LANES)]


def put_sums(sz, ref, first, second, number):
    pieces = lane_rows(sz, first) + lane_rows(sz, second)
    pieces.append(jnp.zeros((1, LANES), F32) + number)
    pieces.append(jnp.zeros((8 - len(pieces), LANES), F32))
    block = jnp.concatenate(pieces, axis=0)
    for index in range(sz.n_dp):
        ref[index] = block


def take_sums(sz, ref):
    total = ref[0]
    for index in range(1, sz.n_dp):
        total = total + ref[index]
    count = sz.lanes // LANES
    first = jnp.concatenate([total[k : k + 1] for k in range(count)], axis=1)
    second = jnp.concatenate([total[count + k : count + k + 1] for k in range(count)], axis=1)
    return first[:, : sz.chans], second[:, : sz.chans], total[2 * count : 2 * count + 1, 0:1]


def sum_rows(value):
    return jnp.sum(value, axis=0, keepdims=True)


def mean_lanes(value):
    return jnp.mean(value, axis=1, keepdims=True)


def pick_rows(sz):
    row = lax.broadcasted_iota(jnp.int32, (sz.image, sz.pad), 0)
    col = lax.broadcasted_iota(jnp.int32, (sz.image, sz.pad), 1)
    return (row // sz.pad == col), (row % sz.pad == col)


def same_masks(sz):
    row = lax.broadcasted_iota(jnp.int32, (sz.image, sz.image), 0)
    col = lax.broadcasted_iota(jnp.int32, (sz.image, sz.image), 1)
    return (row % sz.pad == col % sz.pad), (row // sz.pad == col // sz.pad)


def mixers(sz, small, turned):
    pick_i, pick_j = pick_rows(sz)
    same_j, same_i = same_masks(sz)
    product = dot_nt if turned else dot
    found = []
    for pick, same, lane in ((pick_i, same_j, 0), (pick_j, same_i, LANES)):
        mix = small[ROW_MIX : ROW_MIX + sz.pad, lane : lane + sz.pad].astype(BF16)
        pick = pick.astype(BF16)
        spread = dot_nt(product(pick, mix).astype(BF16), pick)
        found.append(jnp.where(same, spread, 0.0).astype(BF16))
    return found


class Arrivals:
    def __init__(self, sources, buffers, sems, role_of, bit, layers):
        self.buffers, self.copies = buffers, []
        for k, (source, buffer) in enumerate(zip(sources, buffers)):
            if layers[k] is None:
                copies = [pltpu.make_async_copy(source, buffer, sems.at[k, 0])]
                copies[0].start()
            else:
                halved = isinstance(source[-1], tuple)
                rows = buffer.shape[0] // 2 if halved else buffer.shape[0]
                spots = [pl.ds(0, rows), pl.ds(rows, rows)] if halved else [pl.ds(0, rows)]
                copies = [
                    pltpu.make_async_copy(source[0].at[spot], buffer.at[spot], sems.at[k, h])
                    for h, spot in enumerate(spots)
                ]
                for place, held in enumerate(source):

                    @pl.when(role_of(layers[k]) == place)
                    def _(held=held, buffer=buffer, k=k, spots=spots, rows=rows):
                        for h, spot in enumerate(spots):
                            if isinstance(held, tuple):
                                piece = held[h]
                                at = h ^ bit
                                spot = pl.ds(pl.multiple_of(at * rows, 16), rows)
                            else:
                                piece = held.at[spot]
                            pltpu.make_async_copy(piece, buffer.at[spot], sems.at[k, h]).start()

            self.copies.append(copies)

    def __getitem__(self, k):
        if self.copies[k] is not None:
            for copy in self.copies[k]:
                copy.wait()
            self.copies[k] = None
        return self.buffers[k]

    def close(self):
        for k in range(len(self.copies)):
            self[k]


class Departures:
    def __init__(self, targets, buffers, sems, direct):
        self.buffers, self.targets = buffers, targets
        self.copies = [
            None if k < direct else pltpu.make_async_copy(buffer, target, sems.at[k])
            for k, (target, buffer) in enumerate(zip(targets, buffers))
        ]
        self.started, self.parts = [False] * len(self.copies), []

    def put(self, k, value):
        self.buffers[k][...] = value
        self.send(k)

    def send(self, k):
        self.copies[k].start()
        self.started[k] = True

    def send_part(self, k, lanes, sem):
        spot = (slice(None), lanes)
        copy = pltpu.make_async_copy(self.buffers[k].at[spot], self.targets[k].at[spot], sem)
        copy.start()
        self.parts.append(copy)

    def close(self):
        for copy, started in zip(self.copies, self.started):
            if started:
                copy.wait()
        for copy in self.parts:
            copy.wait()


def prepare_kernel(
    sz,
    info,
    taps_ref,
    bn_gain_ref,
    bn_bias_ref,
    mix_h_ref,
    mix_h_bias_ref,
    mix_w_ref,
    mix_w_bias_ref,
    unite_ref,
    unite_b_ref,
    ln_gain_ref,
    ln_bias_ref,
    in_ref,
    b_in_ref,
    w_out_ref,
    b_out_ref,
    weights_ref,
    half_ref,
    small_ref,
):
    chans, hid = sz.chans, sz.hid
    weights_ref[:, :hid] = in_ref[...]
    weights_ref[:, hid : 2 * hid] = w_out_ref[...]
    gap = jnp.zeros((chans, sz.lanes - chans), BF16)
    for part in range(3):
        first = 2 * hid + part * sz.lanes
        weights_ref[:, first : first + sz.lanes] = jnp.concatenate(
            [unite_ref[:, part * chans : (part + 1) * chans], gap], axis=1
        )
    rows = half_ref.shape[0]
    half_ref[...] = weights_ref[pl.ds(pl.multiple_of(info[2] * rows, 16), rows)]
    small_ref[...] = jnp.zeros(small_ref.shape, F32)
    for p in range(3):
        small_ref[3 * p : 3 * p + 3, :chans] = taps_ref[p].astype(F32)
    rows = (bn_gain_ref, bn_bias_ref, unite_b_ref, ln_gain_ref, ln_bias_ref, b_out_ref)
    for place, ref in zip(range(ROW_BN_GAIN, ROW_MIX_BIAS), rows):
        small_ref[place : place + 1, :chans] = ref[...]
    place = ROW_MIX_BIAS
    small_ref[place : place + 1, : sz.side] = mix_h_bias_ref[...]
    small_ref[place : place + 1, LANES : LANES + sz.side] = mix_w_bias_ref[...]
    for k, lane in enumerate(range(0, hid, sz.lanes)):
        wide_part = min(sz.lanes, hid - lane)
        small_ref[ROW_B_IN + k : ROW_B_IN + k + 1, :wide_part] = b_in_ref[
            :, lane : lane + wide_part
        ]
    rows = slice(ROW_MIX, ROW_MIX + sz.side)
    small_ref[rows, : sz.side] = mix_h_ref[...].astype(F32)
    small_ref[rows, LANES : LANES + sz.side] = mix_w_ref[...].astype(F32)


def steps(size, step):
    return [slice(first, min(first + step, size)) for first in range(0, size, step)]


def fold(value):
    total = value[:8]
    for first in range(8, value.shape[0], 8):
        total = total + value[first : first + 8]
    return total


def conv_rows(sz, rows, taps, back=False):
    order = (2, 1, 0) if back else (0, 1, 2)
    parts = []
    for row in rows:
        near = (pltpu.roll(row, 1, 0), row, pltpu.roll(row, sz.pad - 1, 0))
        near = [near[q] for q in order]
        parts.append(
            [taps[3 * p] * near[0] + taps[3 * p + 1] * near[1] + taps[3 * p + 2] * near[2] for p in order]
        )
    found = []
    for i in range(len(rows)):
        total = parts[i][1]
        if i > 0:
            total = total + parts[i - 1][0]
        if i + 1 < len(rows):
            total = total + parts[i + 1][2]
        found.append(total)
    return found


def next_conv(sz, rows, taps, masks, conv_ref, sums_ref, number):
    first = jnp.zeros((8, sz.chans), F32)
    second = jnp.zeros((8, sz.chans), F32)
    for n in range(sz.batch):
        part = range(n * sz.side, (n + 1) * sz.side)
        for i, conv in zip(part, conv_rows(sz, [rows[i] for i in part], taps)):
            conv_ref[i * sz.pad : (i + 1) * sz.pad] = conv
            masked = masks[i] * conv
            first = first + fold(masked)
            second = second + fold(masked * conv)
    put_sums(sz, sums_ref, sum_rows(first), sum_rows(second), number)


def row_masks(sz, valid):
    mask = token_mask(sz, valid)
    return [mask[i : i + sz.pad] for i in range(0, sz.tokens, sz.pad)]


def start_kernel(sz, info, ins, outs):
    field = ins[0]
    kernel = ins[1]
    taps = [kernel[p, q : q + 1].astype(F32) for p in range(3) for q in range(3)]
    rows = [field[i : i + sz.pad].astype(F32) for i in range(0, sz.tokens, sz.pad)]
    number = (info[0] * (sz.side * sz.side)).astype(F32)
    masks = row_masks(sz, info[0])
    next_conv(sz, rows, taps, masks, outs.buffers[0], outs.buffers[1], number)
    outs.send(0)
    outs.send(1)


def forward_kernel(sz, last, info, ins, outs, part_sems):
    GOT, CONV, SMALL, WEIGHTS, FIELD = range(5)
    OUT, ACTIVE, SLOPE, UNIT, SPREAD, JOINED, STAT, CONV_NEXT, SUMS = range(9)
    small = ins[SMALL]
    total, square, count = take_sums(sz, ins[GOT])
    center = total / count
    variance = square / count - center * center
    inverse = lax.rsqrt(variance + 1e-05)
    stat = [
        fill_lanes(sz, center),
        fill_lanes(sz, inverse),
        fill_lanes(sz, variance * count / (count - 1.0)),
        jnp.zeros((1, sz.lanes), F32) + count,
        jnp.zeros((4, sz.lanes), F32),
    ]
    outs.put(STAT, jnp.concatenate(stat, axis=0))
    gain = inverse * row_of(sz, small, ROW_BN_GAIN)
    shift = row_of(sz, small, ROW_BN_BIAS)
    conv, joined = ins[CONV], outs.buffers[JOINED]
    chans, lanes = sz.chans, sz.lanes
    for rows in steps(sz.tokens, ROW_STEP):
        normed = ((conv[rows] - center) * gain + shift).astype(BF16)
        gap = jnp.zeros((normed.shape[0], lanes - chans), BF16)
        joined[rows, :lanes] = jnp.concatenate([normed, gap], axis=1)
    mix_h, mix_w = mixers(sz, small, False)
    pick_i, pick_j = pick_rows(sz)
    bias = small[ROW_MIX_BIAS : ROW_MIX_BIAS + 1]
    bias_h = jnp.sum(jnp.where(pick_i, bias[:, : sz.pad], 0.0), axis=1, keepdims=True)
    bias_w = jnp.sum(
        jnp.where(pick_j, bias[:, LANES : LANES + sz.pad], 0.0), axis=1, keepdims=True
    )
    for n in range(sz.batch):
        normed = joined[n * sz.image : (n + 1) * sz.image, :lanes]
        for mix, add, place in ((mix_h, bias_h, 1), (mix_w, bias_w, 2)):
            mixed = dot(mix, normed)
            for rows in steps(sz.image, ROW_STEP):
                there = slice(n * sz.image + rows.start, n * sz.image + rows.stop)
                joined[there, place * lanes : (place + 1) * lanes] = (
                    mixed[rows] + add[rows]
                ).astype(BF16)
    outs.send(JOINED)
    weights_ref = ins[WEIGHTS]
    field = ins[FIELD]
    united = dot_nt(joined[...], weights_ref[:, 2 * sz.hid :])
    unite_b = row_of(sz, small, ROW_UNITE_B)
    ln_gain, ln_bias = row_of(sz, small, ROW_LN_GAIN), row_of(sz, small, ROW_LN_BIAS)
    hidden, lnormed = [], []
    for rows in steps(sz.tokens, LN_STEP):
        part = field[rows].astype(F32) + (united[rows] + unite_b)
        offset = part - mean_lanes(part)
        spread = lax.rsqrt(mean_lanes(offset * offset) + 1e-06)
        unit = offset * spread
        outs.buffers[UNIT][rows] = unit
        outs.buffers[SPREAD][rows] = spread
        hidden.append(part)
        lnormed.append((unit * ln_gain + ln_bias).astype(BF16))
    hidden = jnp.concatenate(hidden, axis=0)
    lnormed = jnp.concatenate(lnormed, axis=0)
    outs.send(UNIT)
    outs.send(SPREAD)
    lanes_in = [small[ROW_B_IN + k : ROW_B_IN + k + 1] for k in range(-(-sz.hid // lanes))]
    b_in = jnp.concatenate(lanes_in, axis=1)
    root = 0.7978845608028654
    cubic = 0.044715
    for part in steps(sz.hid, HID_STEP):
        product = dot(lnormed, weights_ref[:, part])
        for rows in steps(sz.tokens, ROW_STEP):
            before = product[rows] + b_in[:, part]
            squared = before * before
            bent = jnp.tanh(before * (root + (root * cubic) * squared))
            half = 0.5 + 0.5 * bent
            active = before * half
            slope = half + (active * (1.0 - bent)) * (root + (3.0 * root * cubic) * squared)
            outs.buffers[ACTIVE][rows, part] = active.astype(BF16)
            outs.buffers[SLOPE][rows, part] = slope.astype(BF16)
        index = part.start // HID_STEP
        if not last:
            outs.send_part(ACTIVE, part, part_sems.at[0, index])
            outs.send_part(SLOPE, part, part_sems.at[1, index])
    branch = dot_nt(outs.buffers[ACTIVE][...], weights_ref[:, sz.hid : 2 * sz.hid])
    masks = row_masks(sz, info[0])
    b_out = row_of(sz, small, ROW_B_OUT)
    results = []
    for i, mask in enumerate(masks):
        rows = slice(i * sz.pad, (i + 1) * sz.pad)
        result = (mask * (hidden[rows] + (branch[rows] + b_out))).astype(BF16)
        outs.buffers[OUT][rows] = result
        results.append(result.astype(F32))
    outs.send(OUT)
    if not last:
        number = (info[0] * (sz.side * sz.side)).astype(F32)
        taps = taps_of(sz, ins[5])
        next_conv(
            sz, results, taps, masks, outs.buffers[CONV_NEXT], outs.buffers[SUMS], number
        )
        outs.send(SUMS)
        outs.send(CONV_NEXT)


def finish_layer(sz, info, ins, outs, first_out):
    GOT, STAT, SMALL, NORMED_GRAD, CONV, HIDDEN_GRAD, FIELD = range(7)
    small, stat = ins[SMALL], ins[STAT]
    chans = sz.chans
    taps = taps_of(sz, small)
    sum_dz, sum_dzx, _ = take_sums(sz, ins[GOT])
    count = stat[3:4, 0:1]
    center, inverse = stat[0:1, :chans], stat[1:2, :chans]
    scale = inverse * row_of(sz, small, ROW_BN_GAIN)
    mean_dz, mean_dzx = sum_dz / count, inverse * (sum_dzx / count)
    normed_grad, conv, hidden_grad, field = (
        ins[k] for k in (NORMED_GRAD, CONV, HIDDEN_GRAD, FIELD)
    )
    masks = row_masks(sz, info[0])
    sums = [jnp.zeros((8, chans), F32) for _ in range(9)]
    grads = []
    for n in range(sz.batch):
        spots = [
            slice(i * sz.pad, (i + 1) * sz.pad) for i in range(n * sz.side, (n + 1) * sz.side)
        ]
        conv_grads = [
            (masks[n * sz.side + i] * scale)
            * (normed_grad[rows] - mean_dz - (conv[rows] - center) * mean_dzx)
            for i, rows in enumerate(spots)
        ]
        for rows, back in zip(spots, conv_rows(sz, conv_grads, taps, back=True)):
            grad = (hidden_grad[rows] + back).astype(BF16)
            outs.buffers[first_out][rows] = grad
            grads.append(grad)
        for i, rows in enumerate(spots):
            row = field[rows].astype(F32)
            near = (pltpu.roll(row, 1, 0), row, pltpu.roll(row, sz.pad - 1, 0))
            for p in range(3):
                there = i + 1 - p
                if 0 <= there < sz.side:
                    for q in range(3):
                        sums[3 * p + q] = sums[3 * p + q] + fold(conv_grads[there] * near[q])
    outs.send(first_out)
    pieces = [center, stat[2:3, :chans], sum_dz, sum_dzx] + [sum_rows(item) for item in sums]
    block = [fill_lanes(sz, piece) for piece in pieces]
    block.append(jnp.zeros((CLOSE_ROWS - len(pieces), sz.lanes), F32))
    outs.put(first_out + 1, jnp.concatenate(block, axis=0))
    return grads


def finish_kernel(sz, info, ins, outs):
    finish_layer(sz, info, ins, outs, 0)


def backward_kernel(sz, first, info, ins, outs, pack_ref, before_ref, pack_sems):
    base = 1 if first else 7
    SMALL, WEIGHTS, SLOPE, UNIT, SPREAD, ACTIVE, JOINED, STAT, CONV = range(base, base + 9)
    core = info[1] & 1
    chans, tokens, lanes = sz.chans, sz.tokens, sz.lanes
    shipped = []

    def put(block, value):
        half, row = sz.place(block)
        pack_ref[half ^ core, row : row + chans] = value

    def ship(half, first_row, rows):
        spot, sem = pl.ds(first_row, rows), pack_sems.at[len(shipped)]
        for place in range(2):

            @pl.when(half ^ core == place)
            def _(place=place):
                pltpu.make_async_copy(
                    pack_ref.at[place, spot], outs.targets[place].at[spot], sem
                ).start()

        shipped.append(
            pltpu.make_async_copy(pack_ref.at[0, spot], outs.targets[0].at[spot], sem)
        )

    if first:
        upstream = [ins[0][i : i + sz.pad] for i in range(0, tokens, sz.pad)]
    else:
        upstream = finish_layer(sz, info, ins, outs, 5)
    small = ins[SMALL]
    masks = row_masks(sz, info[0])
    out_grads = [mask * grad.astype(F32) for mask, grad in zip(masks, upstream)]
    branch_grad = jnp.concatenate([item.astype(BF16) for item in out_grads], axis=0)
    out_sum = fold(out_grads[0])
    for item in out_grads[1:]:
        out_sum = out_sum + fold(item)
    out_grads = jnp.concatenate(out_grads, axis=0)
    unit = ins[UNIT]
    ln_gain, ln_bias = row_of(sz, small, ROW_LN_GAIN), row_of(sz, small, ROW_LN_BIAS)
    lnormed = [
        (unit[rows] * ln_gain + ln_bias).astype(BF16) for rows in steps(tokens, ROW_STEP)
    ]
    lnormed = jnp.concatenate(lnormed, axis=0)
    turned_ln = jnp.concatenate([lnormed.T, jnp.ones((16, tokens), BF16)], axis=0)
    turned_branch = branch_grad.T
    weights_ref, slope_ref, active_ref = ins[WEIGHTS], ins[SLOPE], ins[ACTIVE]
    in_pieces = []
    for k in range(0, sz.hid, HID_STEP):
        part = slice(k, k + HID_STEP)
        active_grad = dot(branch_grad, weights_ref[:, sz.hid + k : sz.hid + k + HID_STEP])
        for rows in steps(tokens, ROW_STEP):
            before_ref[rows, part] = (
                active_grad[rows] * slope_ref[rows, part].astype(F32)
            ).astype(BF16)
        grad_in = dot(turned_ln, before_ref[:, part])
        grad_out = dot(turned_branch, active_ref[:, part])
        for lane in range(0, HID_STEP, LANES):
            block = (k + lane) // LANES
            put(block, grad_in[:chans, lane : lane + LANES].astype(BF16))
            put(sz.hid_blocks + block, grad_out[:, lane : lane + LANES].astype(BF16))
            in_pieces.append(grad_in[chans : chans + 1, lane : lane + LANES])
    norm_grad = dot_nt(before_ref[...], weights_ref[:, : sz.hid])
    ship(0, 0, sz.half_blocks * chans)
    spread = ins[SPREAD]
    token_grad = []
    token_sum, gain_sum, bias_sum = (jnp.zeros((8, chans), F32) for _ in range(3))
    for rows in steps(tokens, LN_STEP):
        grad, part = norm_grad[rows], unit[rows]
        product = grad * part
        gain_sum = gain_sum + fold(product)
        bias_sum = bias_sum + fold(grad)
        scaled = grad * ln_gain
        hidden_grad = out_grads[rows] + spread[rows] * (
            scaled - mean_lanes(scaled) - part * mean_lanes(product * ln_gain)
        )
        outs.buffers[3][rows] = hidden_grad
        token = hidden_grad.astype(BF16)
        token_grad.append(token)
        token_sum = token_sum + fold(token.astype(F32))
    token_grad = jnp.concatenate(token_grad, axis=0)
    outs.send(3)
    joined = ins[JOINED]
    joined_grad = dot(token_grad, weights_ref[:, 2 * sz.hid :])
    rows_grad = joined_grad[:, lanes : lanes + chans].astype(BF16)
    cols_grad = joined_grad[:, 2 * lanes : 2 * lanes + chans].astype(BF16)
    turned_h, turned_w = mixers(sz, small, True)
    stat, conv = ins[STAT], ins[CONV]
    center, inverse = stat[0:1, :chans], stat[1:2, :chans]
    sum_dz, sum_dzx = (jnp.zeros((8, chans), F32) for _ in range(2))
    for n in range(sz.batch):
        image = slice(n * sz.image, (n + 1) * sz.image)
        back_h = dot(turned_h, rows_grad[image])
        back_w = dot(turned_w, cols_grad[image])
        for rows in steps(sz.image, ROW_STEP):
            there = slice(image.start + rows.start, image.start + rows.stop)
            normed_grad = joined_grad[there, :chans] + (back_h[rows] + back_w[rows])
            outs.buffers[2][there] = normed_grad
            sum_dz = sum_dz + fold(normed_grad)
            sum_dzx = sum_dzx + fold(normed_grad * ((conv[there] - center) * inverse))
    put_sums(sz, outs.buffers[4], sum_rows(sum_dz), sum_rows(sum_dzx), 0.0)
    outs.send(4)
    outs.send(2)
    grad_unite = dot(token_grad.T, joined[...]).astype(BF16)
    block = 2 * sz.hid_blocks
    leftovers = []
    for part in range(3):
        for k in range(sz.full):
            lane = part * lanes + k * LANES
            put(block, grad_unite[:, lane : lane + LANES])
            block += 1
        if sz.rest:
            lane = part * lanes + sz.full * LANES
            leftovers.append(grad_unite[:, lane : lane + sz.rest])
    if sz.rest:
        left = jnp.concatenate(leftovers, axis=1)
        fill = wide(left.shape[1]) - left.shape[1]
        if fill:
            left = jnp.concatenate([left, jnp.zeros((chans, fill), BF16)], axis=1)
        for lane in range(0, left.shape[1], LANES):
            put(block, left[:, lane : lane + LANES])
            block += 1
    ship(1, 0, sz.half_blocks * chans)
    pick_i, pick_j = pick_rows(sz)
    same_j, same_i = same_masks(sz)
    mix_pieces, bias_pieces = [], []
    for grads, pick, same in ((rows_grad, pick_i, same_j), (cols_grad, pick_j, same_i)):
        pairs = jnp.zeros((sz.image, sz.image), F32)
        sums = jnp.zeros((sz.image, 1), F32)
        for n in range(sz.batch):
            image = slice(n * sz.image, (n + 1) * sz.image)
            pairs = pairs + dot_nt(grads[image], joined[image, :chans])
            sums = sums + jnp.sum(grads[image].astype(F32), axis=1, keepdims=True)
        pairs = jnp.where(same, pairs, 0.0)
        picked = pick.astype(F32)
        groups = [pairs[i : i + sz.pad] for i in range(0, sz.image, sz.pad)]
        if pick is pick_i:
            near = [sum_rows(group) for group in groups]
            near.append(jnp.zeros((sz.pad - sz.side, sz.image), F32))
            near = jnp.concatenate(near, axis=0)
        else:
            near = groups[0]
            for group in groups[1:]:
                near = near + group
        small_grad = dot_exact(near, picked)
        gap = LANES - sz.pad
        mix_pieces.append(
            jnp.concatenate([small_grad, jnp.zeros((sz.pad, gap), F32)], axis=1)
        )
        bias_pieces.append(
            jnp.concatenate([sum_rows(picked * sums), jnp.zeros((1, gap), F32)], axis=1)
        )
    pieces = (
        lane_rows(sz, sum_rows(token_sum))
        + lane_rows(sz, sum_rows(gain_sum))
        + lane_rows(sz, sum_rows(bias_sum))
        + lane_rows(sz, sum_rows(out_sum))
        + in_pieces
        + bias_pieces
        + mix_pieces
    )
    used = sum(piece.shape[0] for piece in pieces)
    pieces.append(jnp.zeros((EXTRA - used, LANES), F32))
    place = sz.half_blocks * chans
    pack_ref[core, place : place + EXTRA] = jnp.concatenate(pieces, axis=0).astype(BF16)
    pack_ref[1 - core, place : place + EXTRA] = jnp.zeros((EXTRA, LANES), BF16)
    ship(0, place, EXTRA)
    ship(1, place, EXTRA)
    for copy in shipped:
        copy.wait()


class Inner:
    def __init__(self, outs, places):
        leaves = [isinstance(place, int) for place in places]
        self.outs, self.places, self.leaves = outs, places, leaves
        self.buffers = [
            outs.buffers[place] if leave else place for place, leave in zip(places, leaves)
        ]

    def put(self, k, value):
        self.buffers[k][...] = value
        self.send(k)

    def send(self, k):
        if self.leaves[k]:
            self.outs.send(self.places[k])

    def send_part(self, k, part, sem):
        pass


class Inputs:
    def __init__(self, ins, places):
        self.ins, self.places = ins, places

    def __getitem__(self, k):
        place = self.places[k]
        return self.ins[place] if isinstance(place, int) else place


def turning_kernel(sz, info, ins, outs, active, slope, unit, spread, joined, *scratch):
    GOT, CONV, SMALL, WEIGHTS, FIELD, UPSTREAM = range(6)
    forward = Inner(outs, [5, active, slope, unit, spread, joined, 6])
    forward_kernel(sz, True, info, ins, forward, None)
    held = [UPSTREAM, SMALL, WEIGHTS, slope, unit, spread, active, joined]
    held += [outs.buffers[6], CONV]
    backward_kernel(sz, True, info, Inputs(ins, held), outs, *scratch)


def closing_kernel(sz, info, mine_ref, got_ref, close_ref, taps_got_ref, mean_ref, var_ref, *outs):
    (
        taps_ref,
        gain_ref,
        bias_ref,
        mix_h_ref,
        mix_h_bias_ref,
        mix_w_ref,
        mix_w_bias_ref,
        unite_ref,
        unite_b_ref,
        ln_gain_ref,
        ln_bias_ref,
        in_ref,
        b_in_ref,
        w_out_ref,
        b_out_ref,
        new_mean_ref,
        new_var_ref,
    ) = outs
    chans = sz.chans
    first_half = (info[1] & 1) == 0

    def take(half, row, rows):
        mine, got = mine_ref[row : row + rows], got_ref[row : row + rows]
        chosen = jnp.where(first_half, mine, got) if half == 0 else jnp.where(first_half, got, mine)
        return chosen.astype(F32)

    mean, var = mean_ref[...], var_ref[...]
    dz = jnp.zeros((1, sz.lanes), F32)
    dzx = jnp.zeros((1, sz.lanes), F32)
    for m in range(close_ref.shape[0]):
        block = close_ref[m]
        mean = 0.9 * mean + 0.1 * block[0:1, :chans]
        var = 0.9 * var + 0.1 * block[1:2, :chans]
        dz = dz + block[2:3]
        dzx = dzx + block[3:4]
    new_mean_ref[...] = mean
    new_var_ref[...] = var
    bias_ref[...] = dz[:, :chans]
    gain_ref[...] = dzx[:, :chans]
    for block in range(sz.hid_blocks):
        lanes = slice(block * LANES, (block + 1) * LANES)
        in_ref[:, lanes] = take(*sz.place(block), chans)
        w_out_ref[:, lanes] = take(*sz.place(sz.hid_blocks + block), chans)
    block = 2 * sz.hid_blocks
    parts = [[] for _ in range(3)]
    for part in range(3):
        for k in range(sz.full):
            parts[part].append(take(*sz.place(block), chans))
            block += 1
    if sz.rest:
        left = jnp.concatenate(
            [take(*sz.place(b), chans) for b in range(block, sz.blocks)], axis=1
        )
        for part in range(3):
            parts[part].append(left[:, part * sz.rest : (part + 1) * sz.rest])
    unite_ref[...] = jnp.concatenate([piece for part in parts for piece in part], axis=1)
    small = take(0, sz.half_blocks * chans, EXTRA)
    count = sz.lanes // LANES

    def joined(first, number, size):
        row = jnp.concatenate([small[first + k : first + k + 1] for k in range(number)], axis=1)
        return row[:, :size]

    unite_b_ref[...] = joined(0, count, chans)
    ln_gain_ref[...] = joined(count, count, chans)
    ln_bias_ref[...] = joined(2 * count, count, chans)
    b_out_ref[...] = joined(3 * count, count, chans)
    first = 4 * count
    b_in_ref[...] = joined(first, sz.hid_blocks, sz.hid)
    first += sz.hid_blocks
    mix_h_bias_ref[...] = small[first : first + 1, : sz.side]
    mix_w_bias_ref[...] = small[first + 1 : first + 2, : sz.side]
    first += 2
    for ref in (mix_h_ref, mix_w_ref):
        for i in range(sz.side):
            ref[i] = small[first + i : first + i + 1, : sz.side]
        first += sz.pad
    taps = taps_got_ref[0]
    for index in range(1, sz.n_dp):
        taps = taps + taps_got_ref[index]
    for p in range(3):
        for q in range(3):
            taps_ref[p, q] = taps[3 * p + q : 3 * p + q + 1, :chans]


def settings(cost):
    return {
        "compiler_params": pltpu.CompilerParams(vmem_limit_bytes=VMEM_BYTES),
        "cost_estimate": pl.CostEstimate(
            flops=0, bytes_accessed=int(cost * 3.0e6), transcendentals=0
        ),
    }


def run_whole(body, outs, info, flat, name, cost):
    def whole(item):
        return pl.BlockSpec(item.shape, lambda step, rank=len(item.shape): (0,) * rank)

    return pl.pallas_call(
        body,
        grid=(1,),
        out_shape=tuple(outs),
        in_specs=[pl.BlockSpec(memory_space=pltpu.SMEM)] + [whole(item) for item in flat],
        out_specs=tuple(whole(item) for item in outs),
        name=name,
        **settings(cost),
    )(info, *flat)


def run(body, outs, info, flat, name, cost, scratch=(), direct=0):
    layers = [item[0] if isinstance(item, tuple) else None for item in flat]
    args, spots, buffers = [], [], []

    def add(item):
        args.append(item)
        return len(args) - 1

    for item in flat:
        held = item[1] if isinstance(item, tuple) else (item,)
        spots.append(
            [tuple(add(one) for one in part) if isinstance(part, tuple) else add(part) for part in held]
        )
        buffers.append(pltpu.VMEM(held[0].shape, held[0].dtype))
    out_buffers = [pltpu.VMEM(item.shape, item.dtype) for item in outs[direct:]]

    def kernel(info_ref, *refs):
        sources, refs = refs[: len(args)], refs[len(args) :]
        targets, refs = refs[: len(outs)], refs[len(outs) :]
        ins_held, refs = refs[: len(buffers)], refs[len(buffers) :]
        outs_held, refs = refs[: len(out_buffers)], refs[len(out_buffers) :]
        in_sems, out_sems = refs[:2]
        picked = []
        for layer, spot in zip(layers, spots):
            found = [
                tuple(sources[one] for one in part) if isinstance(part, tuple) else sources[part]
                for part in spot
            ]
            picked.append(found[0] if layer is None else found)
        ins = Arrivals(
            picked, ins_held, in_sems, lambda layer: info_ref[1] ^ layer, info_ref[2], layers
        )
        held = (None,) * direct + tuple(outs_held)
        departures = Departures(targets, held, out_sems, direct)
        body(info_ref, ins, departures, *refs[2:])
        ins.close()
        departures.close()

    return pl.pallas_call(
        kernel,
        out_shape=tuple(outs),
        in_specs=[pl.BlockSpec(memory_space=pltpu.SMEM)]
        + [pl.BlockSpec(memory_space=pl.ANY) for _ in args],
        out_specs=tuple(pl.BlockSpec(memory_space=pl.ANY) for _ in outs),
        scratch_shapes=buffers
        + out_buffers
        + [pltpu.SemaphoreType.DMA((len(flat), 2)), pltpu.SemaphoreType.DMA((len(outs),))]
        + list(scratch),
        name=name,
        **settings(cost),
    )(info, *args)


def swap(block, axis, size, bit):
    return lax.ppermute(block, axis, [(i, i ^ bit) for i in range(size)])


def tie(first, second):
    first = tuple(first)
    return lax.optimization_barrier(first + tuple(second))[: len(first)]


def add_low(left, right):
    return (left.astype(F32) + right.astype(F32)).astype(BF16)


class Ring:
    def __init__(self, n_dp, n_pipe, dp, core):
        bits = [1 << k for k in range(n_dp.bit_length() - 1)]
        self.orders = (bits, bits[1:] + bits[:1])
        self.steps = len(bits)
        self.n_dp, self.n_pipe, self.dp, self.core = n_dp, n_pipe, dp, core

    def swap(self, block, step):
        route = []
        for d in range(self.n_dp):
            for p in range(self.n_pipe):
                there = d ^ self.orders[p & 1][step]
                route.append((d * self.n_pipe + p, there * self.n_pipe + p))
        return lax.ppermute(block, ("dp", "pipe"), route)

    def upper(self, step):
        bit = jnp.where(self.core == 0, self.orders[0][step], self.orders[1][step])
        return (self.dp & bit) != 0

    def halve(self, block, step):
        side = jnp.where(self.upper(step), 1, 0)
        parts = block.reshape((2, block.shape[0] // 2) + block.shape[1:])
        kept = lax.dynamic_index_in_dim(parts, side, 0, keepdims=False)
        sent = lax.dynamic_index_in_dim(parts, 1 - side, 0, keepdims=False)
        return add_low(kept, self.swap(sent, step))

    def double(self, block, step):
        got = self.swap(block, step)
        side = jnp.where(self.upper(step), 1, 0)
        rows = block.shape[0]
        whole = jnp.zeros((2 * rows,) + block.shape[1:], block.dtype)
        whole = lax.dynamic_update_slice_in_dim(whole, block, side * rows, 0)
        return lax.dynamic_update_slice_in_dim(whole, got, (1 - side) * rows, 0)


def shards(
    images,
    image_counts,
    conv_kernel,
    bn_gain,
    bn_bias,
    mix_h,
    mix_h_bias,
    mix_w,
    mix_w_bias,
    unite_w,
    unite_b,
    ln_gain,
    ln_bias,
    w_in,
    b_in,
    w_out,
    b_out,
    running_mean,
    running_var,
    cotangent,
):
    n_dp, n_pipe = lax.axis_size("dp"), lax.axis_size("pipe")
    dp, pipe = lax.axis_index("dp"), lax.axis_index("pipe")
    layers = n_pipe
    batch = images.shape[0] // n_pipe
    side, chans, hid = images.shape[1], images.shape[3], w_in.shape[2]
    sz = Sizes(batch, side, chans, hid, n_dp)
    core, plane = pipe & 1, pipe >> 1
    tokens = sz.tokens

    def shape(*dims, dtype=F32):
        return jax.ShapeDtypeStruct(dims, dtype)

    valid = jnp.clip(image_counts[0] - pipe * batch, 0, batch).astype(jnp.int32)
    info = jnp.stack([valid, pipe.astype(jnp.int32), (dp & 1).astype(jnp.int32)])

    def to_all(block):
        over = swap(block, "pipe", n_pipe, 2)
        return (block, swap(block, "pipe", n_pipe, 1), over, swap(over, "pipe", n_pipe, 1))

    first_taps = to_all(conv_kernel[0])
    own, own_half, small_own = run_whole(
        functools.partial(prepare_kernel, sz),
        (
            shape(chans, sz.weight_lanes, dtype=BF16),
            shape(chans // 2, sz.weight_lanes, dtype=BF16),
            shape(SMALL_ROWS, sz.lanes),
        ),
        info,
        (
            conv_kernel[0],
            bn_gain,
            bn_bias,
            mix_h[0],
            mix_h_bias,
            mix_w[0],
            mix_w_bias,
            unite_w[0].T,
            unite_b,
            ln_gain,
            ln_bias,
            w_in[0],
            b_in,
            w_out[0].T,
            b_out,
        ),
        "prepare",
        2,
    )
    beside = swap(own, "pipe", n_pipe, 1)

    def across_plane(block, cores):
        return lax.ppermute(block, "pipe", [(p, p ^ 2) for p in cores])

    def to_beside(block, cores):
        return lax.ppermute(block, "pipe", [(p, p ^ 1) for p in cores])

    def to_neighbour(block, cores):
        route = [
            (d * n_pipe + p, (d ^ 1) * n_pipe + p) for d in range(n_dp) for p in cores
        ]
        return lax.ppermute(block, ("dp", "pipe"), route)

    (half_sent,) = tie((own_half,), (first_taps[2],))
    first = across_plane(half_sent, (0, 2))

    def micro(array):
        block = lax.dynamic_slice_in_dim(array, pipe * batch, batch, 0)
        block = jnp.pad(block, ((0, 0), (0, 0), (0, sz.pad - side), (0, 0)))
        return block.reshape(tokens, chans)

    sums_shape = shape(n_dp, 8, LANES)
    plain = shape(tokens, chans)
    low = shape(tokens, chans, dtype=BF16)

    field = micro(images)
    conv, sums = run(
        functools.partial(start_kernel, sz),
        (plain, sums_shape),
        info,
        (field, (0, first_taps)),
        "start",
        2,
    )
    got = lax.all_to_all(sums, "dp", 0, 0)
    (small_own,) = tie((small_own,), (sums,))
    smalls = to_all(small_own)
    (first,) = tie((first,), (sums,))
    first_beside, second = to_beside(first, (0, 2)), to_neighbour(first, (0, 2))
    (second,) = tie((second,), (got,))
    (half_late,) = tie((own_half,), (first_beside, smalls[2]))
    first_odd = across_plane(half_late, (1, 3))
    second_beside = to_beside(second, (0, 2))
    even = (own, beside, (first, second), (first_beside, second_beside))

    fields, convs, saved, stats, weights = [field], [conv], [], [], [even]
    for depth in range(layers - 1):
        if depth:
            got = lax.all_to_all(sums, "dp", 0, 0)
        outs = (
            low,
            shape(tokens, hid, dtype=BF16),
            shape(tokens, hid, dtype=BF16),
            plain,
            shape(tokens, 1),
            shape(tokens, 3 * sz.lanes, dtype=BF16),
            shape(8, sz.lanes),
        )
        flat = (got, convs[depth], (depth, smalls), (depth, weights[depth & 1]), fields[depth])
        outs += (plain, sums_shape)
        flat += ((depth + 1, smalls),)
        results = run(
            functools.partial(forward_kernel, sz, False),
            outs,
            info,
            flat,
            f"layer_{depth}_forward",
            6,
            scratch=[pltpu.SemaphoreType.DMA((2, -(-hid // HID_STEP)))],
        )
        fields.append(results[0])
        if depth == 0:
            (first_odd,) = tie((first_odd,), (second_beside,))
            first_odd_beside = to_beside(first_odd, (1, 3))
            second_odd = to_neighbour(first_odd, (1, 3))
            (second_odd,) = tie((second_odd,), (results[0],))
            second_odd_beside = to_beside(second_odd, (1, 3))
            weights.append(
                (own, beside, (first_odd, second_odd), (first_odd_beside, second_odd_beside))
            )
        saved.append(results[1:6])
        stats.append(results[6])
        convs.append(results[7])
        sums = results[8]

    def to_owners(parts):
        sent = [lax.select_n(pipe ^ bit, *parts) for bit in range(n_pipe)]
        return sent[:1] + [swap(sent[bit], "pipe", n_pipe, bit) for bit in range(1, n_pipe)]

    def collect(parts):
        whole = jnp.zeros((n_pipe, batch, side, side, chans), BF16)
        for bit, part in enumerate(parts):
            part = part.reshape(1, batch, side, sz.pad, chans)[:, :, :, :side]
            whole = lax.dynamic_update_slice(whole, part, (pipe ^ bit, 0, 0, 0, 0))
        return whole.reshape(1, n_pipe * batch, side, side, chans)

    half_shape = shape(sz.half_rows, LANES, dtype=BF16)
    halves, ends = [None] * layers, [None] * 2
    grads, closes = [None] * layers, [None] * layers
    behind = None
    for depth in reversed(range(layers)):
        outs = (half_shape, half_shape, plain, plain, sums_shape)
        packing = [
            pltpu.VMEM((2,) + half_shape.shape, BF16),
            pltpu.VMEM((tokens, hid), BF16),
            pltpu.SemaphoreType.DMA((4,)),
        ]
        if behind is None:
            got = lax.all_to_all(sums, "dp", 0, 0)
            results = run(
                functools.partial(turning_kernel, sz),
                outs + (low, shape(8, sz.lanes)),
                info,
                (got, convs[depth], (depth, smalls), (depth, weights[depth & 1]))
                + (fields[depth], micro(cotangent)),
                f"layer_{depth}_both",
                18,
                scratch=[
                    pltpu.VMEM((tokens, hid), BF16),
                    pltpu.VMEM((tokens, hid), BF16),
                    pltpu.VMEM((tokens, chans), F32),
                    pltpu.VMEM((tokens, 1), F32),
                    pltpu.VMEM((tokens, 3 * sz.lanes), BF16),
                ]
                + packing,
                direct=2,
            )
            fields.append(results[5])
            stats.append(results[6])
        else:
            outs += (low, shape(CLOSE_ROWS, sz.lanes))
            active, slope, unit, spread, joined = saved[depth]
            results = run(
                functools.partial(backward_kernel, sz, False),
                outs,
                info,
                behind
                + ((depth, smalls), (depth, weights[depth & 1]), slope, unit, spread, active)
                + (joined, stats[depth], convs[depth]),
                f"layer_{depth}_backward",
                12,
                scratch=packing,
                direct=2,
            )
        kept, sent, normed_grad, hidden_grad, sums = results[:5]
        if behind is not None:
            grads[depth + 1], closes[depth + 1] = results[5:]
        halves[depth] = add_low(kept, swap(sent, "pipe", n_pipe, 1))
        if depth + 1 == layers:
            (sums,) = tie((sums,), (halves[depth],))
        if depth == 0:
            (sums,) = tie((sums,), (ends[1],))
        if depth < 2:
            mine = jnp.where(plane == 0, halves[depth], halves[depth + 2])
            other = jnp.where(plane == 0, halves[depth + 2], halves[depth])
            ends[depth] = (mine, swap(other, "pipe", n_pipe, 2))
            if depth == 1:
                ends[1] = add_low(*ends[1])
            else:
                (sums,) = tie((sums,), (other,))
        got = lax.all_to_all(sums, "dp", 0, 0)
        (got,) = tie((got,), (halves[depth],))
        behind = (
            got,
            stats[depth],
            (depth, smalls),
            normed_grad,
            convs[depth],
            hidden_grad,
            fields[depth],
        )
    ring = Ring(n_dp, n_pipe, dp, core)
    (odd,), even = tie((ends[1],), (sums,)), add_low(*tie(ends[0], (behind[0],)))
    moves = [functools.partial(ring.halve, step=step) for step in range(ring.steps)]
    moves += [functools.partial(ring.double, step=step) for step in reversed(range(ring.steps))]
    odd_moves, even_moves = iter(moves), iter(moves)
    odd = next(odd_moves)(odd)

    def beside_step(function, *held):
        return function(*tie(held, (even, odd)))

    def step_on(*held):
        nonlocal even, odd
        even = next(even_moves)(even)
        odd_move = next(odd_moves, None)
        odd = odd if odd_move is None else odd_move(odd)
        even, odd, *held = tie((even, odd) + held, ())
        return held

    def end_chain(got):
        return run(
            functools.partial(finish_kernel, sz),
            (low, shape(CLOSE_ROWS, sz.lanes)),
            info,
            (got,) + behind[1:],
            "finish",
            4,
        )

    def add_taps(closing):
        taps = jnp.sum(closing[:, 4:13], axis=0)
        return lax.all_to_all(
            jnp.broadcast_to(taps[None], (n_dp,) + taps.shape), "dp", 0, 0
        )

    grads[0], closes[0] = beside_step(end_chain, behind[0])
    grads[0], closes[0] = step_on(grads[0], closes[0])
    closing = beside_step(
        lambda *held: lax.all_to_all(jnp.stack(held), "pipe", 0, 0), *closes
    )
    (closing,) = step_on(closing)
    output_parts = beside_step(lambda *held: to_owners(held), *fields[1:])
    grad_parts = beside_step(lambda *held: to_owners(held), *grads)
    for _ in range(2, ring.steps):
        step_on()
    taps = beside_step(add_taps, closing)
    for _ in range(2, ring.steps):
        step_on()
    layer_outputs = beside_step(lambda *held: collect(held), *output_parts)
    layer_outputs, taps = step_on(layer_outputs, taps)
    input_grads = beside_step(lambda *held: collect(held), *grad_parts)
    (input_grads,) = step_on(input_grads)
    parts = [odd, even]
    mine = jnp.where(core == 0, parts[1], parts[0])
    other = jnp.where(core == 0, parts[0], parts[1])
    got = swap(other, "pipe", n_pipe, 1)
    row = shape(1, chans)
    outs = (
        shape(3, 3, 1, chans),
        row,
        row,
        shape(side, 1, side),
        shape(1, side),
        shape(side, 1, side),
        shape(1, side),
        shape(chans, 3 * chans),
        row,
        row,
        row,
        shape(chans, hid),
        shape(1, hid),
        shape(chans, hid),
        row,
        row,
        row,
    )
    finished = list(
        run_whole(
            functools.partial(closing_kernel, sz),
            outs,
            info,
            (mine, got, closing, taps, running_mean, running_var),
            "closing",
            4,
        )
    )
    finished[0] = jnp.transpose(finished[0], (2, 0, 1, 3))
    for k in (3, 5):
        finished[k] = jnp.transpose(finished[k], (1, 0, 2))
    for k in (7, 13):
        finished[k] = finished[k].T[None]
    finished[11] = finished[11][None]
    return (layer_outputs, input_grads) + tuple(finished)


def solution(mesh):
    four = P("pipe", None, None, None)
    three = P("pipe", None, None)
    two = P("pipe", None)
    images = P("dp", None, None, None)
    in_specs = (
        images, P("dp"), four, two, two, three, two, three, two, three, two, two, two,
        three, two, three, two, two, two, images,
    )
    stacked = P("pipe", "dp", None, None, None)
    out_specs = (
        stacked, stacked, four, two, two, three, two, three, two, three, two, two, two,
        three, two, three, two, two, two,
    )
    return jax.shard_map(
        shards, mesh=mesh, in_specs=in_specs, out_specs=out_specs, check_vma=False
    )
```
